32 devices in a mesh: dp: 16 (over z, y, x), mp: 2 (over core).
Axes of the slice: x: 2, y: 2, z: 4, core: 2. Of those that a mesh axis runs over, the one named last changes fastest.
Arguments:
- tokens: bfloat16 [25216, 384], P('dp'), may hold values from -6 to 6
- cotangent: bfloat16 [25216, 384], P('dp'), may hold values from -6 to 6
- queue: bfloat16 [2048, 384], P('dp'), may hold values from -6 to 6
- nbr_index: int32 [128, 8], P('dp'), may hold values from 0 to 2047
- nbr_valid: int32 [128, 8], P('dp'), may hold values 0 or 1
- norm_params: float32 [4, 384], replicated, may hold values from -1 to 2.41, as said below
- norm_first: float32 [4, 384], replicated, may hold values from -160 to 160
- norm_second: float32 [4, 384], replicated, may hold values from 2773.76 to 11347.2
- attn_weight: float32 [4, 384, 384], P(None, None, 'mp'), may hold values from -0.8164966 to 0.8164966
- mlp_weight: float32 [2, 384, 1536], P(None, None, 'mp'), may hold values from -0.21875 to 0.21875
- attn_first: float32 [4, 384, 384], P(None, None, 'mp'), may hold values from -104.80501 to 104.80501
- attn_second: float32 [4, 384, 384], P(None, None, 'mp'), may hold values from 118.5152 to 11952.384
- mlp_first: float32 [2, 384, 1536], P(None, None, 'mp'), may hold values from -48 to 48
- mlp_second: float32 [2, 384, 1536], P(None, None, 'mp'), may hold values from 264.768 to 1059.072
- attn_left: float32 [4, 768, 384], P(None, 'mp'), may hold values from -0.03827328 to 1.0382733, as said below
- attn_right: float32 [4, 384, 192], P(None, 'mp'), may hold values from -0.054126588 to 1.0541266, as said below
- mlp_left: float32 [2, 768, 384], P(None, 'mp'), may hold values from -0.03827328 to 1.0382733, as said below
- mlp_right: float32 [2, 1536, 768], P(None, 'mp'), may hold values from -0.027063294 to 1.0270633, as said below
Outputs:
- block_out: bfloat16 [25216, 384], P('dp')
- input_grad: float32 [25216, 384], P('dp')
- norm_grad: float32 [4, 384], replicated
- attn_grad: float32 [4, 384, 384], P(None, None, 'mp')
- mlp_grad: float32 [2, 384, 1536], P(None, None, 'mp')
- norm_first_new: float32 [4, 384], replicated
- norm_second_new: float32 [4, 384], replicated
- norm_new: float32 [4, 384], replicated
- attn_first_new: float32 [4, 384, 384], P(None, None, 'mp')
- attn_second_new: float32 [4, 384, 384], P(None, None, 'mp')
- mlp_first_new: float32 [2, 384, 1536], P(None, None, 'mp')
- mlp_second_new: float32 [2, 384, 1536], P(None, None, 'mp')
- attn_left_new: float32 [4, 768, 384], P(None, 'mp')
- attn_right_new: float32 [4, 384, 192], P(None, 'mp')
- mlp_left_new: float32 [2, 768, 384], P(None, 'mp')
- mlp_right_new: float32 [2, 1536, 768], P(None, 'mp')
- attn_new: float32 [4, 384, 384], P(None, None, 'mp')
- attn_copy: bfloat16 [4, 384, 384], P(None, None, 'mp')
- mlp_new: float32 [2, 384, 1536], P(None, None, 'mp')
- mlp_copy: bfloat16 [2, 384, 1536], P(None, None, 'mp')
The draws below stay inside these ranges and needn't reach their ends.
Inputs may be any that keep to these rules, and one draw needn't show every extreme that they name: `norm_params`: rows 0 and 2 are positive gains, rows 1 and 3 shifts. `attn_left`: each block of rows is a full-rank basis. `attn_right`: each block of rows is a full-rank basis. `mlp_left`: each block of rows is a full-rank basis. `mlp_right`: each block of rows is a full-rank basis.
All inputs are finite; a program needn't handle non-finite values. No bound on the sum of `nbr_valid` on one device may be relied on, other than what follows from the above.
Results may differ from the reference program's by a relative error of at most 0.0095.
The reference program's roundings to bfloat16 on the way count: a program that leaves them out, or rounds other values in their place, can miss the bound.
Values may be sent and summed in bfloat16 or wider, within the bound.
A program may use at most 256 MiB of HBM per device.

```python
import math
import jax
import jax.numpy as jnp
from jax import lax

D = 384
HEADS = 6
FF = 1536
P_SIZE = 197
NBR = 8
STEP = 10
IMG_DEV = 8
HEAD = 64
IMAGES = 128
TOKENS = 25216
QUEUE = 2048
N_MP = 2


def attn_grad_scale():
    return jnp.array([1.5, 1.5, 1.2, 0.3], jnp.float32)[:, None, None] * TOKENS ** 0.5


def near_identity(noise, total, size):
    eye_block = jnp.tile(jnp.eye(size, dtype=jnp.float32), (total // size, 1))
    return eye_block[None, :, :] + noise * (0.15 / size ** 0.5)


def draw_norm_params(key, part):
    key = jax.random.fold_in(key, 1)
    noise = jnp.clip(jax.random.normal(key, (4, D), jnp.float32), -2.5, 2.5) * 0.5
    shifts = 0.4 * noise * 2.0
    pick = (jnp.arange(4) % 2 == 0)[:, None]
    return jnp.where(pick, jnp.exp(0.7 * noise), jnp.clip(shifts, -1.0, 1.0))


def draw_attn_weight(key, part):
    key = jax.random.fold_in(key, 2)
    factor = jnp.array([1.5, 1.5, 1.0, 4.0], jnp.float32)[:, None, None] * D ** (-0.5)
    base = jnp.clip(jax.random.normal(key, (4, D, D), jnp.float32), -4.0, 4.0)
    return base * factor


def draw_attn_first(key, part):
    key = jax.random.fold_in(key, 3)
    base = jnp.clip(jax.random.normal(key, (4, D, D), jnp.float32), -4.0, 4.0)
    return base * 0.11 * attn_grad_scale()


def draw_attn_second(key, part):
    key = jax.random.fold_in(key, 4)
    factor = jnp.exp(jax.random.uniform(key, (4, D, D), jnp.float32, 0.0, 1.386))
    scale = attn_grad_scale()
    return factor * 0.0526 * scale * scale


def basis_noise(key, shape):
    return jnp.clip(jax.random.normal(key, shape, jnp.float32), -4.0, 4.0)


def draw_attn_left(key, part):
    key = jax.random.fold_in(key, 5)
    shape = (4, N_MP * D, D)
    noise = basis_noise(key, shape)
    return near_identity(noise, N_MP * D, D)


def draw_attn_right(key, part):
    key = jax.random.fold_in(key, 6)
    shape = (4, D, D // N_MP)
    noise = basis_noise(key, shape)
    return near_identity(noise, D, D // N_MP)


def draw_mlp_left(key, part):
    key = jax.random.fold_in(key, 7)
    shape = (2, N_MP * D, D)
    noise = basis_noise(key, shape)
    return near_identity(noise, N_MP * D, D)


def draw_mlp_right(key, part):
    key = jax.random.fold_in(key, 8)
    shape = (2, FF, FF // N_MP)
    noise = basis_noise(key, shape)
    return near_identity(noise, FF, FF // N_MP)


def touch_ends(values, rng, smallest, largest):
    longest = values.shape.index(max(values.shape))
    spots = []
    for shift in (0, 1):
        where = [jax.random.randint(jax.random.fold_in(rng, axis), (), 0, length) for axis, length in enumerate(values.shape)]
        where[longest] = (where[longest] + shift) % values.shape[longest]
        spots.append(tuple(where))
    return values.at[spots[0]].set(smallest).at[spots[1]].set(largest)


def shard_levels(own_key, shape, cuts, least, top_value):
    level = 1.0
    for position, blocks in cuts:
        heights = jax.random.uniform(jax.random.fold_in(jax.random.fold_in(own_key, 6), position), (blocks,), jnp.float32, least / len(cuts), top_value / len(cuts))
        level = level * jnp.repeat(jnp.exp(heights), shape[position] // blocks).reshape((-1,) + (1,) * (len(shape) - 1 - position))
    return level


def gaussian(own_key, extent, spread, bound, split=(), kind=jnp.bfloat16):
    entries = spread * jax.random.normal(own_key, extent, jnp.float32)
    if split:
        entries = entries * shard_levels(own_key, extent, split, -0.22, 0.18)
    return jnp.clip(entries, -bound, bound).astype(kind)


def setup_inputs(seed: int = 0) -> dict:
    splits = jax.random.split(jax.random.key(seed), 19)
    tokens = gaussian(splits[0], (TOKENS, D), 1.0, 6.0, ((0, 16),))
    cotangent = gaussian(splits[1], (TOKENS, D), 1.0, 6.0, ((0, 16),))
    queue = gaussian(splits[2], (QUEUE, D), 1.0, 6.0, ((0, 16),))
    nbr_index = touch_ends(jax.random.randint(splits[3], (IMAGES, NBR), 0, QUEUE), jax.random.fold_in(splits[3], 1), 0, QUEUE - 1).astype(jnp.int32)
    nbr_valid = touch_ends((jax.random.randint(splits[4], (IMAGES, NBR), 0, 4) < 3).astype(jnp.int32), jax.random.fold_in(splits[4], 1), 0, 1)
    norm_params = draw_norm_params(jax.random.fold_in(splits[18], 71), 0)
    norm_first = gaussian(splits[6], (4, D), (0.17 * TOKENS ** 0.5), 160.0, (), jnp.float32)
    norm_second = jnp.clip(jnp.exp(jax.random.uniform(splits[7], (4, D), jnp.float32, math.log(2773.76), math.log(11347.2))), 2773.76, 11347.2)
    attn_weight = draw_attn_weight(jax.random.fold_in(splits[18], 71), 0)
    mlp_weight = gaussian(splits[9], (2, D, FF), ((D * FF) ** 0.5) ** -0.5, 0.21875, ((2, 2),), jnp.float32)
    attn_first = draw_attn_first(jax.random.fold_in(splits[18], 71), 0)
    attn_second = draw_attn_second(jax.random.fold_in(splits[18], 71), 0)
    mlp_first = gaussian(splits[12], (2, D, FF), (0.05 * TOKENS ** 0.5), 48.0, ((2, 2),), jnp.float32)
    mlp_second = jnp.clip(jnp.exp(math.log(1059.072) - 1.3862944 * jax.random.uniform(splits[13], (2, D, FF), jnp.float32) ** shard_levels(splits[13], (2, D, FF), ((2, 2),), -0.2, 0.2)), 264.768, 1059.072)
    attn_left = draw_attn_left(jax.random.fold_in(splits[18], 71), 0)
    attn_right = draw_attn_right(jax.random.fold_in(splits[18], 71), 0)
    mlp_left = draw_mlp_left(jax.random.fold_in(splits[18], 71), 0)
    mlp_right = draw_mlp_right(jax.random.fold_in(splits[18], 71), 0)
    return dict(tokens=tokens, cotangent=cotangent, queue=queue, nbr_index=nbr_index, nbr_valid=nbr_valid, norm_params=norm_params, norm_first=norm_first, norm_second=norm_second, attn_weight=attn_weight, mlp_weight=mlp_weight, attn_first=attn_first, attn_second=attn_second, mlp_first=mlp_first, mlp_second=mlp_second, attn_left=attn_left, attn_right=attn_right, mlp_left=mlp_left, mlp_right=mlp_right)


@jax.custom_vjp
def low(v):
    return lax.optimization_barrier(v.astype(jnp.bfloat16)).astype(jnp.float32)

@jax.custom_vjp
def low_back(v):
    return v

def low_keep(v):
    return (low(v), None)

def low_pass(kept, grad):
    return (grad,)

def back_keep(v):
    return (v, None)

def back_low(kept, grad):
    return (low(grad),)
low.defvjp(low_keep, low_pass)
low_back.defvjp(back_keep, back_low)
BETA_FIRST = 0.9
BETA_SECOND = 0.95
EPSILON = 1e-08
RATE_MATRIX = 0.15
RATE_NORM = 0.6
DECAY_RATE = 0.05
TURN_RATE = 4.0

def product(left, right):
    return jnp.dot(left, right, precision=lax.Precision.HIGHEST)

def layer_norm(values, gain, shift):
    centre = values - lax.optimization_barrier(jnp.mean(values, axis=-1, keepdims=True))
    return centre * lax.rsqrt(lax.optimization_barrier(jnp.mean(centre * centre, axis=-1, keepdims=True)) + 1e-06) * gain + shift

def round_both(values):
    return low_back(low(values))

def block_group(item, norms, attn_low, mlp_low):
    tokens, neighbours, valid = item
    images = valid.shape[0]
    own_shape = (images, P_SIZE, HEADS, HEAD)
    far_shape = (images, NBR, HEADS, HEAD)
    normed = low(layer_norm(tokens, norms[0], norms[1]))
    query = round_both(product(normed, attn_low[0])).reshape(own_shape)
    keys = jnp.concatenate([round_both(product(normed, attn_low[1])).reshape(own_shape), round_both(product(neighbours, attn_low[1])).reshape(far_shape)], axis=1)
    values = jnp.concatenate([round_both(product(normed, attn_low[2])).reshape(own_shape), round_both(product(neighbours, attn_low[2])).reshape(far_shape)], axis=1)
    scores = jnp.einsum('gqhd,gkhd->ghqk', query, keys, precision=lax.Precision.HIGHEST) * 0.125
    allowed = jnp.concatenate([jnp.ones((images, P_SIZE), jnp.int32), valid], axis=1) > 0
    scores = low_back(jnp.where(allowed[:, None, None, :], scores, -1e+30))
    top = lax.optimization_barrier(jnp.max(scores, axis=-1, keepdims=True))
    powers = jnp.exp(scores - top)
    probs = low(powers / lax.optimization_barrier(jnp.sum(powers, axis=-1, keepdims=True)))
    mixed = jnp.einsum('ghqk,gkhd->gqhd', probs, values, precision=lax.Precision.HIGHEST)
    mixed = round_both(mixed.reshape(images * P_SIZE, HEADS * HEAD))
    middle = tokens + low_back(product(mixed, attn_low[3].T))
    normed_two = low(layer_norm(middle, norms[2], norms[3]))
    hidden = low(jax.nn.gelu(low_back(product(normed_two, mlp_low[0])), approximate=False))
    return middle + low_back(product(hidden, mlp_low[1].T))

def forward_all(tokens, norms, attn_weight, mlp_weight, neighbours, valid):
    attn_low = low(attn_weight)
    mlp_low = low(mlp_weight)
    groups = IMAGES // IMG_DEV

    def one_group(item):
        return block_group(item, norms, attn_low, mlp_low)
    result = lax.map(jax.checkpoint(one_group), (tokens.reshape(groups, IMG_DEV * P_SIZE, D), neighbours.reshape(groups, IMG_DEV * NBR, D), valid.reshape(groups, IMG_DEV, NBR)))
    return result.reshape(TOKENS, D)

def renew_basis(basis):
    factor = jnp.linalg.cholesky(product(basis.T, basis))
    return jax.scipy.linalg.solve_triangular(factor, basis.T, lower=True).T

def gram_energy(grad):
    if grad.shape[0] <= grad.shape[1]:
        gram = product(grad, grad.T)
    else:
        gram = product(grad.T, grad)
    return jnp.sqrt(jnp.sum(gram * gram)) + 1e-06

def rotate_update(grad, weight, first, second, left, right):
    turned = product(product(left.T, grad), right)
    first_new = BETA_FIRST * first + (1.0 - BETA_FIRST) * turned
    second_new = BETA_SECOND * second + (1.0 - BETA_SECOND) * turned * turned
    direction = first_new / (1.0 - BETA_FIRST ** STEP) / (jnp.sqrt(second_new / (1.0 - BETA_SECOND ** STEP)) + EPSILON)
    weight_new = weight * (1.0 - RATE_MATRIX * DECAY_RATE) - RATE_MATRIX * product(product(left, direction), right.T)
    energy = gram_energy(grad)
    left_new = renew_basis(left + TURN_RATE * product(grad, product(grad.T, left)) / energy)
    right_new = renew_basis(right + TURN_RATE * product(grad.T, product(grad, right)) / energy)
    return (weight_new, first_new, second_new, left_new, right_new)

def update_matrix(grad, weight, first, second, left, right, width):
    blocks = []
    for part in range(N_MP):
        cols = slice(part * width, (part + 1) * width)
        rows_left = slice(part * D, (part + 1) * D)
        blocks.append(rotate_update(grad[:, cols], weight[:, cols], first[:, cols], second[:, cols], left[rows_left], right[cols]))
    weight_new = jnp.concatenate([block[0] for block in blocks], axis=1)
    first_new = jnp.concatenate([block[1] for block in blocks], axis=1)
    second_new = jnp.concatenate([block[2] for block in blocks], axis=1)
    left_new = jnp.concatenate([block[3] for block in blocks], axis=0)
    right_new = jnp.concatenate([block[4] for block in blocks], axis=0)
    return (weight_new, first_new, second_new, left_new, right_new)

def update_stack(grads, weights, firsts, seconds, lefts, rights, width):
    made = [update_matrix(grads[slot], weights[slot], firsts[slot], seconds[slot], lefts[slot], rights[slot], width) for slot in range(grads.shape[0])]
    return tuple((jnp.stack([entry[place] for entry in made]) for place in range(5)))

def reference(tokens, cotangent, queue, nbr_index, nbr_valid, norm_params, norm_first, norm_second, attn_weight, mlp_weight, attn_first, attn_second, mlp_first, mlp_second, attn_left, attn_right, mlp_left, mlp_right):
    neighbours = queue.astype(jnp.float32)[nbr_index.reshape(-1)]

    def whole(inputs, norms, attn_w, mlp_w):
        return forward_all(inputs, norms, attn_w, mlp_w, neighbours, nbr_valid)
    result, pull = jax.vjp(whole, tokens.astype(jnp.float32), norm_params, attn_weight, mlp_weight)
    input_grad, norm_grad, attn_grad, mlp_grad = pull(cotangent.astype(jnp.float32))
    norm_first_new = BETA_FIRST * norm_first + (1.0 - BETA_FIRST) * norm_grad
    norm_second_new = BETA_SECOND * norm_second + (1.0 - BETA_SECOND) * norm_grad * norm_grad
    norm_new = norm_params - RATE_NORM * (norm_first_new / (1.0 - BETA_FIRST ** STEP)) / (jnp.sqrt(norm_second_new / (1.0 - BETA_SECOND ** STEP)) + EPSILON)
    attn_new, attn_first_new, attn_second_new, attn_left_new, attn_right_new = update_stack(attn_grad, attn_weight, attn_first, attn_second, attn_left, attn_right, D // N_MP)
    mlp_new, mlp_first_new, mlp_second_new, mlp_left_new, mlp_right_new = update_stack(mlp_grad, mlp_weight, mlp_first, mlp_second, mlp_left, mlp_right, FF // N_MP)
    return (result.astype(jnp.bfloat16), input_grad, norm_grad, attn_grad, mlp_grad, norm_first_new, norm_second_new, norm_new, attn_first_new, attn_second_new, mlp_first_new, mlp_second_new, attn_left_new, attn_right_new, mlp_left_new, mlp_right_new, attn_new, attn_new.astype(jnp.bfloat16), mlp_new, mlp_new.astype(jnp.bfloat16))
```

```python
import jax
import jax.numpy as jnp
from jax import lax
from jax.experimental import pallas as pl
from jax.experimental.pallas import tpu as pltpu
from jax.sharding import PartitionSpec as P

P_SIZE = 197
NBR = 8
STEP = 10
HEAD = 64


BETA_FIRST = 0.9
BETA_SECOND = 0.95
EPSILON = 1e-08
RATE_MATRIX = 0.15
RATE_NORM = 0.6
DECAY_RATE = 0.05
TURN_RATE = 4.0


def mult(left, right):
    return jnp.dot(left, right, preferred_element_type=jnp.float32)


def mult_right_t(left, right):
    return lax.dot_general(
        left, right, (((1,), (1,)), ((), ())), preferred_element_type=jnp.float32
    )


def mult_left_t(left, right):
    return lax.dot_general(
        left, right, (((0,), (0,)), ((), ())), preferred_element_type=jnp.float32
    )


def product(left, right):
    return jnp.dot(left, right, precision=lax.Precision.HIGHEST)


def layer_norm(values, gain, shift):
    centre = values - jnp.mean(values, axis=-1, keepdims=True)
    scale = lax.rsqrt(jnp.mean(centre * centre, axis=-1, keepdims=True) + 1e-06)
    normal = centre * scale
    return (normal * gain + shift, normal, scale)


def norm_back(grad, normal, scale, gain):
    shaped = grad * gain
    return scale * (
        shaped
        - jnp.mean(shaped, axis=-1, keepdims=True)
        - normal * jnp.mean(shaped * normal, axis=-1, keepdims=True)
    )


def fetch_rows(queue, nbr_index):
    wanted = nbr_index.reshape(-1)
    piece = lax.all_gather(queue, "dp", axis=0, tiled=True)
    places = lax.iota(jnp.int32, piece.shape[0])
    chooser = (wanted[:, None] == places[None, :]).astype(jnp.bfloat16)
    return mult(chooser, piece).astype(jnp.bfloat16)


def forward(tokens, norms, attn_low, mlp_low, neighbours, nbr_valid):
    images = nbr_valid.shape[0]
    width = attn_low.shape[2]
    heads = width // HEAD
    own_shape = (images, P_SIZE, heads, HEAD)
    far_shape = (images, NBR, heads, HEAD)
    normed_f, normal_one, scale_one = layer_norm(tokens, norms[0], norms[1])
    normed = normed_f.astype(jnp.bfloat16)
    quest = mult(normed, attn_low[0]).astype(jnp.bfloat16).reshape(own_shape)
    keys = jnp.concatenate(
        [
            mult(normed, attn_low[1]).astype(jnp.bfloat16).reshape(own_shape),
            mult(neighbours, attn_low[1]).astype(jnp.bfloat16).reshape(far_shape),
        ],
        axis=1,
    )
    values = jnp.concatenate(
        [
            mult(normed, attn_low[2]).astype(jnp.bfloat16).reshape(own_shape),
            mult(neighbours, attn_low[2]).astype(jnp.bfloat16).reshape(far_shape),
        ],
        axis=1,
    )
    scores = jnp.einsum("gqhd,gkhd->ghqk", quest, keys, preferred_element_type=jnp.float32) * 0.125
    allowed = jnp.concatenate([jnp.ones((images, P_SIZE), jnp.int32), nbr_valid], axis=1) > 0
    scores = jnp.where(allowed[:, None, None, :], scores, -1e30)
    top = jnp.max(scores, axis=-1, keepdims=True)
    powers = jnp.exp(scores - top)
    probs = powers / jnp.sum(powers, axis=-1, keepdims=True)
    probs_low = probs.astype(jnp.bfloat16)
    mixed = jnp.einsum("ghqk,gkhd->gqhd", probs_low, values, preferred_element_type=jnp.float32)
    mixed = mixed.reshape(images * P_SIZE, width).astype(jnp.bfloat16)
    attended = lax.psum(mult_right_t(mixed, attn_low[3]), "mp")
    middle = tokens + attended
    normed_two_f, normal_two, scale_two = layer_norm(middle, norms[2], norms[3])
    normed_two = normed_two_f.astype(jnp.bfloat16)
    inner = mult(normed_two, mlp_low[0])
    hidden = jax.nn.gelu(inner, approximate=False).astype(jnp.bfloat16)
    output = middle + lax.psum(mult_right_t(hidden, mlp_low[1]).astype(jnp.bfloat16), "mp").astype(
        jnp.float32
    )
    kept = (
        normed,
        normal_one,
        scale_one,
        quest,
        keys,
        values,
        probs,
        probs_low,
        mixed,
        normed_two,
        normal_two,
        scale_two,
        inner,
        hidden,
    )
    return (output, kept)


HIGH = lax.Precision.HIGH
HIGHEST = lax.Precision.HIGHEST
BLOCK = 256
NEAR = 0.01

BF = jnp.bfloat16


def dot_nn(a, b, precision=None):
    return lax.dot_general(a, b, (((1,), (0,)), ((), ())), precision=precision, preferred_element_type=jnp.float32)


def dot_nt(a, b, precision=None):
    return lax.dot_general(a, b, (((1,), (1,)), ((), ())), precision=precision, preferred_element_type=jnp.float32)


def dot_tn(a, b, precision=None):
    return lax.dot_general(a, b, (((0,), (0,)), ((), ())), precision=precision, preferred_element_type=jnp.float32)


def split(a):
    high = a.astype(BF)
    return high, (a - high.astype(jnp.float32)).astype(BF)


def below(size):
    row = lax.broadcasted_iota(jnp.int32, (size, size), 0)
    col = lax.broadcasted_iota(jnp.int32, (size, size), 1)
    return row > col, row == col


def whiten(gram, rounds):
    size = gram.shape[0]
    lower, same = below(size)
    eye = jnp.where(same, 1.0, 0.0)
    on_diag = jnp.where(same, gram, 0.0)
    s_col = lax.rsqrt(jnp.maximum(jnp.sum(on_diag, axis=1, keepdims=True), 1e-30))
    s_row = lax.rsqrt(jnp.maximum(jnp.sum(on_diag, axis=0, keepdims=True), 1e-30))
    state = gram * s_col * s_row
    made = jnp.where(same, s_col, 0.0)
    for turn in range(rounds):
        under = jnp.where(lower, state, 0.0)
        under_low = under.astype(BF)
        moved = dot_nn(under_low, state.astype(BF))
        mass = jnp.sum(under * under, axis=1, keepdims=True)
        curve = jnp.sum(moved * under, axis=1, keepdims=True)
        pace = jnp.where(curve > mass, mass / jnp.maximum(curve, 1e-30), 1.0)
        left = 1.0 - 2.0 * pace * mass + pace * pace * curve
        scale = lax.rsqrt(jnp.maximum(left, 1e-6))
        step = (scale * (eye - pace * under)).astype(BF)
        if turn + 1 < rounds:
            state = dot_nt((scale * (state - pace * moved)).astype(BF), step)
        made = dot_nn(step, made.astype(BF))
    return made.astype(BF)


def miss(gram):
    lower, same = below(gram.shape[0])
    return jnp.where(lower, gram, 0.0) + jnp.where(same, 0.5 * (gram - 1.0), 0.0)


def turn_by(base, made):
    high, low = split(base)
    return dot_nt(high, made) + dot_nt(low, made)


def cuts(width):
    return [(at, min(BLOCK, width - at)) for at in range(0, width, BLOCK)]


def renew_fast(base_ref, out_ref, rest_ref):
    width = base_ref.shape[1]
    worst = 0.0
    src = base_ref
    for at, size in cuts(width):
        block = src[:, at:at + size]
        low = block.astype(BF)
        made = whiten(dot_tn(low, low), 3)
        block = turn_by(block, made)
        off = miss(dot_tn(block, block, HIGH))
        worst = jnp.maximum(worst, jnp.sum(off * off) / size)
        block = block - dot_nt(block.astype(BF), off.astype(BF))
        out_ref[:, at:at + size] = block
        if at + size < width:
            rest = src[:, at + size:]
            rest_ref[:, at + size:] = rest - dot_nn(block, dot_tn(block, rest, HIGH), HIGH)
            src = rest_ref
    return worst


def renew_safe(base_ref, out_ref):
    width = base_ref.shape[1]
    out_ref[...] = base_ref[...]
    for at, size in cuts(width):
        cols = slice(at, at + size)

        def again(carry, cols=cols, size=size):
            count, unused = carry
            block = out_ref[:, cols]
            gram = dot_tn(block, block, HIGHEST)
            off = miss(gram)
            far = jnp.logical_not(jnp.sum(off * off) / size < NEAR)

            @pl.when(far)
            def _():
                out_ref[:, cols] = turn_by(block, whiten(gram, 3))

            @pl.when(jnp.logical_not(far))
            def _():
                out_ref[:, cols] = block - dot_nt(block, off, HIGH)

            return count + 1, far

        lax.while_loop(lambda carry: jnp.logical_and(carry[0] < 60, carry[1]), again, (0, True))
        if at + size < width:
            block = out_ref[:, cols]
            for unused in range(2):
                rest = out_ref[:, at + size:]
                out_ref[:, at + size:] = rest - dot_nn(block, dot_tn(block, rest, HIGHEST), HIGHEST)


def update_kernel(
    grad_ref, weight_ref, first_ref, second_ref, left_ref, right_ref,
    new_ref, copy_ref, first_new_ref, second_new_ref, left_new_ref, right_new_ref,
    left_base, right_base, left_rest, right_rest,
):
    grad = grad_ref[0].astype(BF)
    left_high, left_low = split(left_ref[0])
    right = right_ref[0]
    right_high = right.astype(BF)
    half = dot_tn(left_high, grad) + dot_tn(left_low, grad)
    turned = dot_nn(half, right, HIGH)
    first_new = BETA_FIRST * first_ref[0] + (1.0 - BETA_FIRST) * turned
    second_new = BETA_SECOND * second_ref[0] + (1.0 - BETA_SECOND) * turned * turned
    first_new_ref[0] = first_new
    second_new_ref[0] = second_new
    move = (
        first_new
        / (1.0 - BETA_FIRST**STEP)
        / (jnp.sqrt(second_new / (1.0 - BETA_SECOND**STEP)) + EPSILON)
    )
    back = dot_nn(left_high, move.astype(BF)).astype(BF)
    new = weight_ref[0] * (1.0 - RATE_MATRIX * DECAY_RATE) - RATE_MATRIX * dot_nt(back, right_high)
    new_ref[0] = new
    copy_ref[0] = new.astype(BF)

    if grad.shape[0] <= grad.shape[1]:
        gram = dot_nt(grad, grad)
        energy = jnp.sqrt(jnp.sum(gram * gram)) + 1e-06
        pace = TURN_RATE / energy
        left_base[...] = left_ref[0] + dot_nn(gram.astype(BF), left_high) * pace
        right_base[...] = right + dot_tn(grad, dot_nn(grad, right_high).astype(BF)) * pace
    else:
        gram = dot_tn(grad, grad)
        energy = jnp.sqrt(jnp.sum(gram * gram)) + 1e-06
        pace = TURN_RATE / energy
        left_base[...] = left_ref[0] + dot_nn(grad, dot_tn(grad, left_high).astype(BF)) * pace
        right_base[...] = right + dot_nn(gram.astype(BF), right_high) * pace

    worst_left = renew_fast(left_base, left_new_ref.at[0], left_rest)
    worst_right = renew_fast(right_base, right_new_ref.at[0], right_rest)

    @pl.when(jnp.logical_not(worst_left < NEAR))
    def _():
        renew_safe(left_base, left_new_ref.at[0])

    @pl.when(jnp.logical_not(worst_right < NEAR))
    def _():
        renew_safe(right_base, right_new_ref.at[0])


def update_stack(grad, weight, first, second, left, right):
    slots, rows, width = grad.shape

    def spec(shape):
        return pl.BlockSpec((1,) + shape, lambda slot: (slot, 0, 0))

    flat = spec((rows, width))
    f32 = jnp.float32
    return pl.pallas_call(
        update_kernel,
        grid=(slots,),
        in_specs=[flat] * 4 + [spec((rows, rows)), spec((width, width))],
        out_specs=[flat] * 4 + [spec((rows, rows)), spec((width, width))],
        out_shape=[
            jax.ShapeDtypeStruct(weight.shape, f32),
            jax.ShapeDtypeStruct(weight.shape, BF),
            jax.ShapeDtypeStruct(weight.shape, f32),
            jax.ShapeDtypeStruct(weight.shape, f32),
            jax.ShapeDtypeStruct(left.shape, f32),
            jax.ShapeDtypeStruct(right.shape, f32),
        ],
        scratch_shapes=[
            pltpu.VMEM((rows, rows), f32),
            pltpu.VMEM((width, width), f32),
            pltpu.VMEM((rows, rows), f32),
            pltpu.VMEM((width, width), f32),
        ],
        compiler_params=pltpu.CompilerParams(vmem_limit_bytes=60 * 1024 * 1024),
        name="rotated_update_%d" % width,
    )(grad, weight, first, second, left, right)


def body(
    tokens,
    cotangent,
    queue,
    nbr_index,
    nbr_valid,
    norm_params,
    norm_first,
    norm_second,
    attn_weight,
    mlp_weight,
    attn_first,
    attn_second,
    mlp_first,
    mlp_second,
    attn_left,
    attn_right,
    mlp_left,
    mlp_right,
):
    attn_low = attn_weight.astype(jnp.bfloat16)
    mlp_low = mlp_weight.astype(jnp.bfloat16)
    tokens_f = tokens.astype(jnp.float32)
    neighbours = fetch_rows(queue, nbr_index)
    output, kept = forward(tokens_f, norm_params, attn_low, mlp_low, neighbours, nbr_valid)
    again = lax.optimization_barrier((tokens_f, attn_low, mlp_low, queue, nbr_index))
    neighbours = fetch_rows(again[3], again[4])
    unused, kept = forward(again[0], norm_params, again[1], again[2], neighbours, nbr_valid)
    (
        normed,
        normal_one,
        scale_one,
        quest,
        keys,
        values,
        probs,
        probs_low,
        mixed,
        normed_two,
        normal_two,
        scale_two,
        inner,
        hidden,
    ) = kept
    images = nbr_valid.shape[0]
    width = attn_low.shape[2]
    grad_hidden = mult(cotangent, mlp_low[1])
    grad_w_two = mult_left_t(cotangent, hidden)
    unused_value, gelu_pull = jax.vjp(lambda value: jax.nn.gelu(value, approximate=False), inner)
    grad_inner = gelu_pull(grad_hidden)[0].astype(jnp.bfloat16)
    grad_w_one = mult_left_t(normed_two, grad_inner)
    grad_normed_two = lax.psum(mult_right_t(grad_inner, mlp_low[0]), "mp")
    grad_middle = cotangent.astype(jnp.float32) + norm_back(
        grad_normed_two, normal_two, scale_two, norm_params[2]
    )
    norm_two = jnp.stack(
        [jnp.sum(grad_normed_two * normal_two, axis=0), jnp.sum(grad_normed_two, axis=0)]
    )
    mlp_grad = jnp.stack([grad_w_one, grad_w_two])
    grad_middle_low = grad_middle.astype(jnp.bfloat16)
    grad_w_out = mult_left_t(grad_middle_low, mixed)
    grad_mixed = mult(grad_middle_low, attn_low[3]).astype(jnp.bfloat16)
    grad_mixed = grad_mixed.reshape(images, P_SIZE, width // HEAD, HEAD)
    grad_probs = jnp.einsum(
        "gqhd,gkhd->ghqk", grad_mixed, values, preferred_element_type=jnp.float32
    )
    grad_values = jnp.einsum(
        "ghqk,gqhd->gkhd", probs_low, grad_mixed, preferred_element_type=jnp.float32
    ).astype(jnp.bfloat16)
    grad_scores = (
        probs * (grad_probs - jnp.sum(grad_probs * probs, axis=-1, keepdims=True))
    ).astype(jnp.bfloat16)
    grad_query = (
        (
            jnp.einsum("ghqk,gkhd->gqhd", grad_scores, keys, preferred_element_type=jnp.float32)
            * 0.125
        )
        .astype(jnp.bfloat16)
        .reshape(images * P_SIZE, width)
    )
    grad_keys = (
        jnp.einsum("ghqk,gqhd->gkhd", grad_scores, quest, preferred_element_type=jnp.float32)
        * 0.125
    ).astype(jnp.bfloat16)
    key_own = grad_keys[:, :P_SIZE].reshape(images * P_SIZE, width)
    key_far = grad_keys[:, P_SIZE:].reshape(images * NBR, width)
    value_own = grad_values[:, :P_SIZE].reshape(images * P_SIZE, width)
    value_far = grad_values[:, P_SIZE:].reshape(images * NBR, width)
    grad_w_query = mult_left_t(normed, grad_query)
    grad_w_key = mult_left_t(normed, key_own) + mult_left_t(neighbours, key_far)
    grad_w_value = mult_left_t(normed, value_own) + mult_left_t(neighbours, value_far)
    attn_grad = jnp.stack([grad_w_query, grad_w_key, grad_w_value, grad_w_out])
    grad_normed = lax.psum(
        mult_right_t(grad_query, attn_low[0])
        + mult_right_t(key_own, attn_low[1])
        + mult_right_t(value_own, attn_low[2]),
        "mp",
    )
    input_grad = grad_middle + norm_back(grad_normed, normal_one, scale_one, norm_params[0])
    norm_one = jnp.stack([jnp.sum(grad_normed * normal_one, axis=0), jnp.sum(grad_normed, axis=0)])
    attn_grad, mlp_grad, norm_one, norm_two = lax.psum(
        (attn_grad, mlp_grad, norm_one, norm_two), "dp"
    )
    norm_grad = jnp.concatenate([norm_one, norm_two], axis=0)
    norm_first_new = BETA_FIRST * norm_first + (1.0 - BETA_FIRST) * norm_grad
    norm_second_new = BETA_SECOND * norm_second + (1.0 - BETA_SECOND) * norm_grad * norm_grad
    norm_new = norm_params - RATE_NORM * (norm_first_new / (1.0 - BETA_FIRST**STEP)) / (
        jnp.sqrt(norm_second_new / (1.0 - BETA_SECOND**STEP)) + EPSILON
    )
    def flip(value):
        return value.transpose(0, 2, 1)

    attn_new, attn_copy, attn_first_new, attn_second_new, attn_right_new, attn_left_new = update_stack(
        flip(attn_grad),
        flip(attn_weight),
        flip(attn_first),
        flip(attn_second),
        attn_right,
        attn_left,
    )
    attn_new, attn_copy, attn_first_new, attn_second_new = map(
        flip, (attn_new, attn_copy, attn_first_new, attn_second_new)
    )
    mlp_new, mlp_copy, mlp_first_new, mlp_second_new, mlp_left_new, mlp_right_new = update_stack(
        mlp_grad, mlp_weight, mlp_first, mlp_second, mlp_left, mlp_right
    )
    return (
        output.astype(jnp.bfloat16),
        input_grad,
        norm_grad,
        attn_grad,
        mlp_grad,
        norm_first_new,
        norm_second_new,
        norm_new,
        attn_first_new,
        attn_second_new,
        mlp_first_new,
        mlp_second_new,
        attn_left_new,
        attn_right_new,
        mlp_left_new,
        mlp_right_new,
        attn_new,
        attn_copy,
        mlp_new,
        mlp_copy,
    )


def solution(mesh):
    return jax.shard_map(
        body,
        mesh=mesh,
        in_specs=(
            P("dp", None),
            P("dp", None),
            P("dp", None),
            P("dp", None),
            P("dp", None),
            P(),
            P(),
            P(),
            P(None, None, "mp"),
            P(None, None, "mp"),
            P(None, None, "mp"),
            P(None, None, "mp"),
            P(None, None, "mp"),
            P(None, None, "mp"),
            P(None, "mp", None),
            P(None, "mp", None),
            P(None, "mp", None),
            P(None, "mp", None),
        ),
        out_specs=(
            P("dp", None),
            P("dp", None),
            P(),
            P(None, None, "mp"),
            P(None, None, "mp"),
            P(),
            P(),
            P(),
            P(None, None, "mp"),
            P(None, None, "mp"),
            P(None, None, "mp"),
            P(None, None, "mp"),
            P(None, "mp", None),
            P(None, "mp", None),
            P(None, "mp", None),
            P(None, "mp", None),
            P(None, None, "mp"),
            P(None, None, "mp"),
            P(None, None, "mp"),
            P(None, None, "mp"),
        ),
        check_vma=False,
    )
```

```python
import functools
import math

import jax
import jax.numpy as jnp
from jax import lax
from jax.experimental import pallas as pl
from jax.experimental.pallas import tpu as pltpu
from jax.sharding import PartitionSpec as P

BETA_FIRST = 0.9
BETA_SECOND = 0.95
EPSILON = 1e-08
RATE_MATRIX = 0.15
DECAY_RATE = 0.05
TURN_RATE = 4.0
STEP = 10
HIGH = lax.Precision.HIGH
HIGHEST = lax.Precision.HIGHEST
BLOCK = 256
NEAR = 0.01

BF = jnp.bfloat16


def dot_nn(a, b, precision=None):
    return lax.dot_general(a, b, (((1,), (0,)), ((), ())), precision=precision, preferred_element_type=jnp.float32)


def dot_nt(a, b, precision=None):
    return lax.dot_general(a, b, (((1,), (1,)), ((), ())), precision=precision, preferred_element_type=jnp.float32)


def dot_tn(a, b, precision=None):
    return lax.dot_general(a, b, (((0,), (0,)), ((), ())), precision=precision, preferred_element_type=jnp.float32)


def split(a):
    high = a.astype(BF)
    return high, (a - high.astype(jnp.float32)).astype(BF)


def below(size):
    row = lax.broadcasted_iota(jnp.int32, (size, size), 0)
    col = lax.broadcasted_iota(jnp.int32, (size, size), 1)
    return row > col, row == col


def whiten(gram, rounds):
    size = gram.shape[0]
    lower, same = below(size)
    eye = jnp.where(same, 1.0, 0.0)
    on_diag = jnp.where(same, gram, 0.0)
    s_col = lax.rsqrt(jnp.maximum(jnp.sum(on_diag, axis=1, keepdims=True), 1e-30))
    s_row = lax.rsqrt(jnp.maximum(jnp.sum(on_diag, axis=0, keepdims=True), 1e-30))
    state = gram * s_col * s_row
    made = jnp.where(same, s_col, 0.0)
    for turn in range(rounds):
        under = jnp.where(lower, state, 0.0)
        under_low = under.astype(BF)
        moved = dot_nn(under_low, state.astype(BF))
        mass = jnp.sum(under * under, axis=1, keepdims=True)
        curve = jnp.sum(moved * under, axis=1, keepdims=True)
        pace = jnp.where(curve > mass, mass / jnp.maximum(curve, 1e-30), 1.0)
        left = 1.0 - 2.0 * pace * mass + pace * pace * curve
        scale = lax.rsqrt(jnp.maximum(left, 1e-6))
        step = (scale * (eye - pace * under)).astype(BF)
        if turn + 1 < rounds:
            state = dot_nt((scale * (state - pace * moved)).astype(BF), step)
        made = dot_nn(step, made.astype(BF))
    return made.astype(BF)


def miss(gram):
    lower, same = below(gram.shape[0])
    return jnp.where(lower, gram, 0.0) + jnp.where(same, 0.5 * (gram - 1.0), 0.0)


def turn_by(base, made):
    high, low = split(base)
    return dot_nt(high, made) + dot_nt(low, made)


def cuts(width):
    return [(at, min(BLOCK, width - at)) for at in range(0, width, BLOCK)]


def renew_fast(base_ref, out_ref, rest_ref):
    width = base_ref.shape[1]
    worst = 0.0
    src = base_ref
    for at, size in cuts(width):
        block = src[:, at:at + size]
        low = block.astype(BF)
        made = whiten(dot_tn(low, low), 3)
        block = turn_by(block, made)
        off = miss(dot_tn(block, block, HIGH))
        worst = jnp.maximum(worst, jnp.sum(off * off) / size)
        block = block - dot_nt(block.astype(BF), off.astype(BF))
        out_ref[:, at:at + size] = block
        if at + size < width:
            rest = src[:, at + size:]
            rest_ref[:, at + size:] = rest - dot_nn(block, dot_tn(block, rest, HIGH), HIGH)
            src = rest_ref
    return worst


def renew_safe(base_ref, out_ref):
    width = base_ref.shape[1]
    out_ref[...] = base_ref[...]
    for at, size in cuts(width):
        cols = slice(at, at + size)

        def again(carry, cols=cols, size=size):
            count, unused = carry
            block = out_ref[:, cols]
            gram = dot_tn(block, block, HIGHEST)
            off = miss(gram)
            far = jnp.logical_not(jnp.sum(off * off) / size < NEAR)

            @pl.when(far)
            def _():
                out_ref[:, cols] = turn_by(block, whiten(gram, 3))

            @pl.when(jnp.logical_not(far))
            def _():
                out_ref[:, cols] = block - dot_nt(block, off, HIGH)

            return count + 1, far

        lax.while_loop(lambda carry: jnp.logical_and(carry[0] < 60, carry[1]), again, (0, True))
        if at + size < width:
            block = out_ref[:, cols]
            for unused in range(2):
                rest = out_ref[:, at + size:]
                out_ref[:, at + size:] = rest - dot_nn(block, dot_tn(block, rest, HIGHEST), HIGHEST)


def update_kernel(
    grad_ref, weight_ref, first_ref, second_ref, left_ref, right_ref,
    new_ref, copy_ref, first_new_ref, second_new_ref, left_new_ref, right_new_ref,
    left_base, right_base, left_rest, right_rest,
):
    grad = grad_ref[0].astype(BF)
    left_high, left_low = split(left_ref[0])
    right = right_ref[0]
    right_high = right.astype(BF)
    half = dot_tn(left_high, grad) + dot_tn(left_low, grad)
    turned = dot_nn(half, right, HIGH)
    first_new = BETA_FIRST * first_ref[0] + (1.0 - BETA_FIRST) * turned
    second_new = BETA_SECOND * second_ref[0] + (1.0 - BETA_SECOND) * turned * turned
    first_new_ref[0] = first_new
    second_new_ref[0] = second_new
    move = (
        first_new
        / (1.0 - BETA_FIRST**STEP)
        / (jnp.sqrt(second_new / (1.0 - BETA_SECOND**STEP)) + EPSILON)
    )
    back = dot_nn(left_high, move.astype(BF)).astype(BF)
    new = weight_ref[0] * (1.0 - RATE_MATRIX * DECAY_RATE) - RATE_MATRIX * dot_nt(back, right_high)
    new_ref[0] = new
    copy_ref[0] = new.astype(BF)

    if grad.shape[0] <= grad.shape[1]:
        gram = dot_nt(grad, grad)
        energy = jnp.sqrt(jnp.sum(gram * gram)) + 1e-06
        pace = TURN_RATE / energy
        left_base[...] = left_ref[0] + dot_nn(gram.astype(BF), left_high) * pace
        right_base[...] = right + dot_tn(grad, dot_nn(grad, right_high).astype(BF)) * pace
    else:
        gram = dot_tn(grad, grad)
        energy = jnp.sqrt(jnp.sum(gram * gram)) + 1e-06
        pace = TURN_RATE / energy
        left_base[...] = left_ref[0] + dot_nn(grad, dot_tn(grad, left_high).astype(BF)) * pace
        right_base[...] = right + dot_nn(gram.astype(BF), right_high) * pace

    worst_left = renew_fast(left_base, left_new_ref.at[0], left_rest)
    worst_right = renew_fast(right_base, right_new_ref.at[0], right_rest)

    @pl.when(jnp.logical_not(worst_left < NEAR))
    def _():
        renew_safe(left_base, left_new_ref.at[0])

    @pl.when(jnp.logical_not(worst_right < NEAR))
    def _():
        renew_safe(right_base, right_new_ref.at[0])


def update_stack(grad, weight, first, second, left, right):
    slots, rows, width = grad.shape

    def spec(shape):
        return pl.BlockSpec((1,) + shape, lambda slot: (slot, 0, 0))

    flat = spec((rows, width))
    f32 = jnp.float32
    return pl.pallas_call(
        update_kernel,
        grid=(slots,),
        in_specs=[flat] * 4 + [spec((rows, rows)), spec((width, width))],
        out_specs=[flat] * 4 + [spec((rows, rows)), spec((width, width))],
        out_shape=[
            jax.ShapeDtypeStruct(weight.shape, f32),
            jax.ShapeDtypeStruct(weight.shape, BF),
            jax.ShapeDtypeStruct(weight.shape, f32),
            jax.ShapeDtypeStruct(weight.shape, f32),
            jax.ShapeDtypeStruct(left.shape, f32),
            jax.ShapeDtypeStruct(right.shape, f32),
        ],
        scratch_shapes=[
            pltpu.VMEM((rows, rows), f32),
            pltpu.VMEM((width, width), f32),
            pltpu.VMEM((rows, rows), f32),
            pltpu.VMEM((width, width), f32),
        ],
        compiler_params=pltpu.CompilerParams(vmem_limit_bytes=60 * 1024 * 1024),
        name="rotated_update_%d" % width,
    )(grad, weight, first, second, left, right)


P_SIZE = 197
NBR = 8
HEAD = 64
ROWS = 208
FAR = 200
CHUNK = 256


def layer_norm(values, gain, shift):
    centre = values - jnp.mean(values, axis=-1, keepdims=True)
    scale = lax.rsqrt(jnp.mean(centre * centre, axis=-1, keepdims=True) + 1e-06)
    normal = centre * scale
    return (normal * gain + shift, normal, scale)


def norm_back(grad, normal, scale, gain):
    shaped = grad * gain
    return scale * (
        shaped
        - jnp.mean(shaped, axis=-1, keepdims=True)
        - normal * jnp.mean(shaped * normal, axis=-1, keepdims=True)
    )


def gelu_pair(value):
    size = jnp.abs(value) * (1.0 / math.sqrt(2.0))
    bell = jnp.exp(-0.5 * value * value)
    part = 1.0 / (1.0 + 0.3275911 * size)
    series = part * (
        0.254829592
        + part * (-0.284496736 + part * (1.421413741 + part * (-1.453152027 + part * 1.061405429)))
    )
    tail = 0.5 * series * bell
    share = jnp.where(value < 0.0, tail, 1.0 - tail)
    return value * share, share + value * bell * (1.0 / math.sqrt(2.0 * math.pi))


def block_kernel(
    images,
    core_ref, valid_ref,
    tokens_ref, cotangent_ref, near_ref, norms_ref, attn_ref, mlp_ref,
    out_ref, input_grad_ref, attn_grad_ref, mlp_grad_ref, norm_grad_ref,
    wide, far_f, tokens_f, normed, normal_one, scale_one, query, key, value, probs, mixed,
    middle, normal_two, scale_two, normed_two, cot_low, made, grad_two,
    grad_mid_low, grad_query, grad_key, grad_value,
):
    core = core_ref[0]
    total = tokens_ref.shape[0]
    width = tokens_ref.shape[1]

    def at_own_rows(act):
        for which in range(total // (images * P_SIZE)):

            @pl.when(core == which)
            def _(which=which):
                for image in range(images):
                    act((which * images + image) * P_SIZE, image * ROWS)

    def spread(source, target):
        def act(start, place):
            target[place:place + ROWS, :] = source[start:start + ROWS, :]

        at_own_rows(act)

    pairs = width // (2 * HEAD)
    wide[:total, :] = tokens_ref[...].astype(jnp.float32)
    wide[total:, :] = jnp.zeros((wide.shape[0] - total, width), jnp.float32)
    spread(wide, tokens_f)
    wide[:total, :] = cotangent_ref[...].astype(jnp.float32)
    spread(wide, made)
    far_f[...] = near_ref[...].astype(jnp.float32)
    own_row = lax.broadcasted_iota(jnp.int32, (ROWS, 1), 0) < P_SIZE
    lane = lax.broadcasted_iota(jnp.int32, (1, 2 * HEAD), 1)
    first_head = lane < HEAD
    key_lane = lax.broadcasted_iota(jnp.int32, (1, ROWS), 1)

    def halves(pair):
        zero = jnp.zeros_like(pair)
        return jnp.where(first_head, pair, zero), jnp.where(first_head, zero, pair)

    def step_forward(image, carry):
        here = pl.ds(pl.multiple_of(image * ROWS, ROWS), ROWS)
        x = tokens_f[here, :]
        cot_low[here, :] = jnp.where(own_row, made[here, :], 0.0).astype(BF)
        normed_f, normal, scale = layer_norm(x, norms_ref[0:1, :], norms_ref[1:2, :])
        normal_one[here, :] = normal
        scale_one[here, :] = scale
        allowed = key_lane < P_SIZE
        for slot in range(NBR):
            okay = valid_ref[core * images + image, slot] > 0
            allowed = jnp.logical_or(allowed, jnp.logical_and(key_lane == FAR + slot, okay))
        far = far_f[pl.ds(pl.multiple_of(image * NBR, NBR), NBR), :]
        normed_f = jnp.where(own_row, normed_f, 0.0)
        full = jnp.concatenate([normed_f[:FAR, :], far], axis=0).astype(BF)
        normed[here, :] = full
        q = dot_nt(full, attn_ref[0]).astype(BF)
        k = dot_nt(full, attn_ref[1]).astype(BF)
        v = dot_nt(full, attn_ref[2]).astype(BF)
        query[here, :] = q
        key[here, :] = k
        value[here, :] = v
        bias = jnp.where(allowed, 0.0, -1e30)
        parts = []
        for pair in range(pairs):
            cols = slice(pair * 2 * HEAD, (pair + 1) * 2 * HEAD)
            k_pair = k[:, cols]
            sums = 0.0
            for head, (q_one, v_one) in enumerate(zip(halves(q[:, cols]), halves(v[:, cols]))):
                scores = dot_nt(q_one, k_pair) * 0.125 + bias
                top = jnp.max(scores, axis=-1, keepdims=True)
                powers = jnp.exp(scores - top)
                prob = powers / jnp.sum(powers, axis=-1, keepdims=True)
                probs[image * 2 * pairs + 2 * pair + head] = prob
                sums = sums + dot_nn(prob.astype(BF), v_one)
            parts.append(sums.astype(BF))
        mix = jnp.concatenate(parts, axis=1)
        mixed[here, :] = mix
        mid = x + dot_nn(mix, attn_ref[3])
        middle[here, :] = mid
        two_f, normal, scale = layer_norm(mid, norms_ref[2:3, :], norms_ref[3:4, :])
        normal_two[here, :] = normal
        scale_two[here, :] = scale
        normed_two[here, :] = two_f.astype(BF)
        return carry

    lax.fori_loop(0, images, step_forward, 0)

    made[...] = jnp.zeros_like(made)
    grad_two[...] = jnp.zeros_like(grad_two)
    chunks = mlp_ref.shape[3] // CHUNK

    def step_mlp(turn, carry):
        half = turn // chunks
        cols = pl.ds(pl.multiple_of((turn % chunks) * CHUNK, CHUNK), CHUNK)
        w_one = mlp_ref[0, half, :, cols]
        w_two = mlp_ref[1, half, :, cols]
        two = normed_two[...]
        cot = cot_low[...]
        hidden, slope = gelu_pair(dot_nn(two, w_one))
        hidden = hidden.astype(BF)
        grad_inner = (dot_nn(cot, w_two) * slope).astype(BF)
        made[...] += dot_nt(hidden, w_two)
        grad_two[...] += dot_nt(grad_inner, w_one)
        mlp_grad_ref[0, half, :, cols] = dot_tn(two, grad_inner)
        mlp_grad_ref[1, half, :, cols] = dot_tn(cot, hidden)
        return carry

    lax.fori_loop(0, 2 * chunks, step_mlp, 0)

    norm_grad_ref[...] = jnp.zeros_like(norm_grad_ref)
    input_grad_ref[...] = jnp.zeros_like(input_grad_ref)
    wide[...] = jnp.zeros_like(wide)

    def step_backward(image, carry):
        here = pl.ds(pl.multiple_of(image * ROWS, ROWS), ROWS)
        made[here, :] += middle[here, :]
        grad_n = grad_two[here, :]
        normal = normal_two[here, :]
        norm_grad_ref[2:3, :] += jnp.sum(grad_n * normal, axis=0, keepdims=True)
        norm_grad_ref[3:4, :] += jnp.sum(grad_n, axis=0, keepdims=True)
        grad_mid = cot_low[here, :].astype(jnp.float32) + norm_back(
            grad_n, normal, scale_two[here, :], norms_ref[2:3, :]
        )
        low = grad_mid.astype(BF)
        grad_mid_low[here, :] = low
        grad_mix = dot_nt(low, attn_ref[3]).astype(BF)
        q = query[here, :]
        k = key[here, :]
        v = value[here, :]
        parts_q, parts_k, parts_v = [], [], []
        for pair in range(pairs):
            cols = slice(pair * 2 * HEAD, (pair + 1) * 2 * HEAD)
            gm_pair = grad_mix[:, cols]
            sum_q = sum_k = sum_v = 0.0
            for head, (q_one, k_one, v_one, gm_one) in enumerate(
                zip(halves(q[:, cols]), halves(k[:, cols]), halves(v[:, cols]), halves(gm_pair))
            ):
                prob = probs[image * 2 * pairs + 2 * pair + head]
                grad_prob = dot_nt(gm_pair, v_one)
                sum_v = sum_v + dot_tn(prob.astype(BF), gm_one)
                weighed = prob * grad_prob
                grad_score = (
                    weighed - prob * jnp.sum(weighed, axis=-1, keepdims=True)
                ).astype(BF)
                sum_q = sum_q + dot_nn(grad_score, k_one)
                sum_k = sum_k + dot_tn(grad_score, q_one)
            parts_q.append((sum_q * 0.125).astype(BF))
            parts_k.append((sum_k * 0.125).astype(BF))
            parts_v.append(sum_v.astype(BF))
        gq = jnp.concatenate(parts_q, axis=1)
        gk = jnp.concatenate(parts_k, axis=1)
        gv = jnp.concatenate(parts_v, axis=1)
        grad_query[here, :] = gq
        grad_key[here, :] = gk
        grad_value[here, :] = gv
        grad_n = dot_nn(gq, attn_ref[0]) + dot_nn(gk, attn_ref[1]) + dot_nn(gv, attn_ref[2])
        grad_n = jnp.where(own_row, grad_n, 0.0)
        normal = normal_one[here, :]
        norm_grad_ref[0:1, :] += jnp.sum(grad_n * normal, axis=0, keepdims=True)
        norm_grad_ref[1:2, :] += jnp.sum(grad_n, axis=0, keepdims=True)
        back = grad_mid + norm_back(grad_n, normal, scale_one[here, :], norms_ref[0:1, :])
        middle[here, :] = back
        return carry

    lax.fori_loop(0, images, step_backward, 0)

    def pack(start, place):
        wide[start:start + P_SIZE, :] = made[place:place + P_SIZE, :]
        input_grad_ref[start:start + P_SIZE, :] = middle[place:place + P_SIZE, :]

    at_own_rows(pack)
    out_ref[...] = wide[:total, :].astype(BF)
    attn_grad_ref[0] = dot_tn(grad_query[...], normed[...])
    attn_grad_ref[1] = dot_tn(grad_key[...], normed[...])
    attn_grad_ref[2] = dot_tn(grad_value[...], normed[...])
    attn_grad_ref[3] = dot_tn(mixed[...], grad_mid_low[...])


def block(core, nbr_valid, tokens, cotangent, near, norms, attn, mlp):
    total, width = tokens.shape
    images = nbr_valid.shape[0] // mlp.shape[1]
    rows = images * ROWS
    padded = total + 16 - total % 8
    f32 = jnp.float32
    vmem = pl.BlockSpec(memory_space=pltpu.VMEM)
    smem = pl.BlockSpec(memory_space=pltpu.SMEM)
    heads = width // HEAD
    flat_f = pltpu.VMEM((rows, width), f32)
    flat_low = pltpu.VMEM((rows, width), BF)
    column = pltpu.VMEM((rows, 1), f32)
    return pl.pallas_call(
        functools.partial(block_kernel, images),
        in_specs=[smem] * 2 + [vmem] * 6,
        out_specs=[vmem] * 5,
        out_shape=[
            jax.ShapeDtypeStruct((total, width), BF),
            jax.ShapeDtypeStruct((total, width), f32),
            jax.ShapeDtypeStruct(attn.shape, f32),
            jax.ShapeDtypeStruct(mlp.shape, f32),
            jax.ShapeDtypeStruct((4, width), f32),
        ],
        scratch_shapes=[
            pltpu.VMEM((padded, width), f32),
            pltpu.VMEM(near.shape, f32),
            flat_f,
            flat_low, flat_f, column, flat_low, flat_low, flat_low,
            pltpu.VMEM((images * heads, ROWS, ROWS), f32),
            flat_low,
            flat_f, flat_f, column, flat_low, flat_low, flat_f, flat_f,
            flat_low, flat_low, flat_low, flat_low,
        ],
        compiler_params=pltpu.CompilerParams(vmem_limit_bytes=60 * 1024 * 1024),
        name="block_both_ways",
    )(core, nbr_valid, tokens, cotangent, near, norms, attn, mlp)


MESH = pl.DeviceIdType.MESH


def fetch_kernel(
    chips, picks,
    wanted_ref, queue_ref, attn_ref, mlp_ref,
    near_ref, attn_out, mlp_out,
    asked, given, parts, ask_send, ask_recv, give_send, give_recv, swap_send, swap_recv,
):
    me = lax.axis_index("dp")
    core = lax.axis_index("mp")
    other = 1 - core
    depth = queue_ref.shape[0]
    barrier = pltpu.get_barrier_semaphore()
    pl.semaphore_signal(barrier, inc=1, device_id=(me, other), device_id_type=MESH)

    def greet(hop, carry):
        pl.semaphore_signal(
            barrier, inc=1, device_id=(lax.rem(me + hop, chips), core), device_id_type=MESH
        )
        return carry

    lax.fori_loop(1, chips, greet, 0)
    attn_out[:, core] = attn_ref[...].astype(BF)
    mlp_out[:, core] = mlp_ref[...].astype(BF)
    pl.semaphore_wait(barrier, chips)

    def ask(hop):
        return pltpu.make_async_remote_copy(
            src_ref=wanted_ref.at[core],
            dst_ref=asked.at[hop],
            send_sem=ask_send.at[hop],
            recv_sem=ask_recv.at[hop],
            device_id=(lax.rem(me + hop, chips), core),
            device_id_type=MESH,
        )

    def give(hop):
        return pltpu.make_async_remote_copy(
            src_ref=parts.at[hop],
            dst_ref=given.at[hop],
            send_sem=give_send.at[hop],
            recv_sem=give_recv.at[hop],
            device_id=(lax.rem(me + chips - hop, chips), core),
            device_id_type=MESH,
        )

    def start_ask(hop, carry):
        ask(hop).start()
        return carry

    lax.fori_loop(1, chips, start_ask, 0)
    swaps = [
        pltpu.make_async_remote_copy(
            src_ref=out.at[:, core],
            dst_ref=out.at[:, core],
            send_sem=swap_send.at[place],
            recv_sem=swap_recv.at[place],
            device_id=(me, other),
            device_id_type=MESH,
        )
        for place, out in enumerate((attn_out, mlp_out))
    ]
    for swap in swaps:
        swap.start()
    places = lax.broadcasted_iota(jnp.int32, (picks, depth), 1) + me * depth

    def choose(wanted):
        chooser = jnp.where(wanted == places, 1.0, 0.0).astype(BF)
        return dot_nn(chooser, queue_ref[...]).astype(BF)

    given[0] = choose(wanted_ref[core])

    def answer(hop, carry):
        ask(hop).wait_recv()
        parts[hop] = choose(asked[hop])
        give(hop).start()
        return carry

    lax.fori_loop(1, chips, answer, 0)

    def collect(hop, total):
        give(hop).wait_recv()
        return total + given[hop].astype(jnp.float32)

    total = lax.fori_loop(1, chips, collect, given[0].astype(jnp.float32))
    near_ref[...] = total.astype(BF)

    def finish(hop, carry):
        ask(hop).wait_send()
        give(hop).wait_send()
        return carry

    lax.fori_loop(1, chips, finish, 0)
    for swap in swaps:
        swap.wait()


def fetch(chips, wanted, queue, attn, mlp):
    cores, picks, lanes = wanted.shape
    vmem = pl.BlockSpec(memory_space=pltpu.VMEM)
    width = queue.shape[1]
    return pl.pallas_call(
        functools.partial(fetch_kernel, chips, picks),
        in_specs=[vmem] * 4,
        out_specs=[vmem] * 3,
        out_shape=[
            jax.ShapeDtypeStruct((picks, width), BF),
            jax.ShapeDtypeStruct((attn.shape[0], cores) + attn.shape[1:], BF),
            jax.ShapeDtypeStruct((mlp.shape[0], cores) + mlp.shape[1:], BF),
        ],
        scratch_shapes=[
            pltpu.VMEM((chips, picks, lanes), jnp.int32),
            pltpu.VMEM((chips, picks, width), BF),
            pltpu.VMEM((chips, picks, width), BF),
            pltpu.SemaphoreType.DMA((chips,)),
            pltpu.SemaphoreType.DMA((chips,)),
            pltpu.SemaphoreType.DMA((chips,)),
            pltpu.SemaphoreType.DMA((chips,)),
            pltpu.SemaphoreType.DMA((2,)),
            pltpu.SemaphoreType.DMA((2,)),
        ],
        compiler_params=pltpu.CompilerParams(
            collective_id=0, has_side_effects=True, vmem_limit_bytes=48 * 1024 * 1024
        ),
        name="fetch",
    )(wanted, queue, attn, mlp)


HALVINGS = 4


def orders(bits):
    base = list(range(bits))
    if bits < 3:
        return [base, base[::-1], base]
    low = base[:2]
    return [base, low[::-1] + base[2:], base[2:4] + low + base[4:]]


def sum_kernel(
    bits,
    attn_ref, mlp_ref, norm_ref,
    attn_out, mlp_out, norm_out,
    total, first_send, first_recv, sent, recv, done, norm_recv, norm_work,
    swap_send, swap_recv, step_send, step_recv, spread_send, spread_recv, norm_send, norm_sem,
):
    me = lax.axis_index("dp")
    core = lax.axis_index("mp")
    other = 1 - core
    slots, rows, width = attn_out.shape
    height = slots * rows
    halvings = min(HALVINGS, bits)
    plan = orders(bits)
    parts = 3

    def mate(bit):
        return me + (1 - 2 * ((me // 2**bit) % 2)) * 2**bit

    barrier = pltpu.get_barrier_semaphore()
    pl.semaphore_signal(barrier, inc=1, device_id=(me, other), device_id_type=MESH)
    for bit in range(bits):
        pl.semaphore_signal(barrier, inc=1, device_id=(mate(bit), core), device_id_type=MESH)

    def fill(target, part, whose, cast):
        if part < 2:
            for block in range(mlp_ref.shape[3] // width):
                target[part, block * mlp_ref.shape[2]:(block + 1) * mlp_ref.shape[2], :] = mlp_ref[
                    part, whose, :, block * width:(block + 1) * width
                ].astype(cast)
        else:
            for slot in range(slots):
                target[part, slot * rows:(slot + 1) * rows, :] = attn_ref[slot, whose].astype(cast)

    for part in range(parts):
        fill(first_send, part, other, BF)
    pl.semaphore_wait(barrier, bits + 1)

    def copy(src, dst, send, recv, device):
        return pltpu.make_async_remote_copy(
            src_ref=src, dst_ref=dst, send_sem=send, recv_sem=recv, device_id=device, device_id_type=MESH
        )

    pending = []
    swaps = []
    for part in range(parts):
        swap = copy(first_send.at[part], first_recv.at[part], swap_send.at[part], swap_recv.at[part], (me, other))
        swap.start()
        swaps.append(swap)
    norm_work[0] = norm_ref[...]
    norm_copy = copy(norm_work.at[0], norm_recv.at[0], norm_send.at[0], norm_sem.at[0], (me, other))
    norm_copy.start()
    for part in range(parts):
        fill(total, part, core, jnp.float32)

    offsets = [0] * parts
    size = height
    copies = [None] * parts
    for step in range(halvings + 1):
        half = size // 2
        for part in range(parts):
            held = pl.ds(pl.multiple_of(offsets[part], 16), size)
            if step == 0:
                swaps[part].wait_recv()
                arrived = first_recv.at[part]
            else:
                copies[part].wait_recv()
                arrived = recv.at[part, pl.ds(height - 2 * size, size)]
            total[part, held, :] += arrived[...].astype(jnp.float32)
            if step < halvings:
                bit = plan[part][step]
                mine = (me // 2**bit) % 2
                away = pl.multiple_of(offsets[part] + (1 - mine) * half, 16)
                slot = pl.ds(height - 2 * half, half)
                sent[part, slot, :] = total[part, pl.ds(away, half), :].astype(BF)
                copies[part] = copy(
                    sent.at[part, slot],
                    recv.at[part, slot],
                    step_send.at[part, step],
                    step_recv.at[part, step],
                    (mate(bit), core),
                )
                copies[part].start()
                pending.append(copies[part])
                offsets[part] = offsets[part] + mine * half
        if step < halvings:
            size = half
    for step in range(bits + 1):
        norm_copy.wait()
        if step < bits:
            norm_work[step + 1] = norm_work[step] + norm_recv[step]
            norm_copy = copy(
                norm_work.at[step + 1],
                norm_recv.at[step + 1],
                norm_send.at[step + 1],
                norm_sem.at[step + 1],
                (mate(step), core),
            )
            norm_copy.start()
        else:
            norm_out[...] = norm_work[step] + norm_recv[step]
    for step in range(halvings, bits):
        for part in range(parts):
            bit = plan[part][step]
            held = pl.ds(pl.multiple_of(offsets[part], 16), size)
            place = height + (step - halvings) * size
            slot = pl.ds(place, size)
            sent[part, slot, :] = total[part, held, :].astype(BF)
            copies[part] = copy(
                sent.at[part, slot],
                recv.at[part, slot],
                step_send.at[part, step],
                step_recv.at[part, step],
                (mate(bit), core),
            )
            copies[part].start()
            pending.append(copies[part])
        for part in range(parts):
            held = pl.ds(pl.multiple_of(offsets[part], 16), size)
            slot = pl.ds(height + (step - halvings) * size, size)
            copies[part].wait_recv()
            total[part, held, :] = sent[part, slot, :].astype(jnp.float32) + recv[part, slot, :].astype(jnp.float32)
    for part in range(parts):
        held = pl.ds(pl.multiple_of(offsets[part], 16), size)
        done[part, held, :] = total[part, held, :].astype(BF)
    for back in range(halvings):
        step = halvings - 1 - back
        for part in range(parts):
            bit = plan[part][step]
            held = pl.ds(pl.multiple_of(offsets[part], 16), size)
            copies[part] = copy(
                done.at[part, held],
                done.at[part, held],
                spread_send.at[part, step],
                spread_recv.at[part, step],
                (mate(bit), core),
            )
            if back > 0:
                previous[part].wait_recv()
            copies[part].start()
            pending.append(copies[part])
            mine = (me // 2**bit) % 2
            offsets[part] = offsets[part] - mine * size
        previous = list(copies)
        size = size * 2
    for part in range(parts):
        previous[part].wait_recv()
        if part < 2:
            for block in range(mlp_out.shape[2] // width):
                mlp_out[part, :, block * width:(block + 1) * width] = done[
                    part, block * mlp_out.shape[1]:(block + 1) * mlp_out.shape[1], :
                ].astype(jnp.float32)
        else:
            for slot in range(slots):
                attn_out[slot] = done[part, slot * rows:(slot + 1) * rows, :].astype(jnp.float32)
    for one in swaps + pending:
        one.wait_send()


def sum_grads(chips, attn, mlp, norm):
    bits = chips.bit_length() - 1
    slots, cores, rows, width = attn.shape
    height = slots * rows
    halvings = min(HALVINGS, bits)
    tall = height + (bits - halvings) * (height >> halvings)
    vmem = pl.BlockSpec(memory_space=pltpu.VMEM)
    f32 = jnp.float32
    dma = pltpu.SemaphoreType.DMA
    return pl.pallas_call(
        functools.partial(sum_kernel, bits),
        in_specs=[vmem] * 3,
        out_specs=[vmem] * 3,
        out_shape=[
            jax.ShapeDtypeStruct((slots, rows, width), f32),
            jax.ShapeDtypeStruct((mlp.shape[0],) + mlp.shape[2:], f32),
            jax.ShapeDtypeStruct(norm.shape, f32),
        ],
        scratch_shapes=[
            pltpu.VMEM((3, height, width), f32),
            pltpu.VMEM((3, height, width), BF),
            pltpu.VMEM((3, height, width), BF),
            pltpu.VMEM((3, tall, width), BF),
            pltpu.VMEM((3, tall, width), BF),
            pltpu.VMEM((3, height, width), BF),
            pltpu.VMEM((bits + 1,) + norm.shape, f32),
            pltpu.VMEM((bits + 1,) + norm.shape, f32),
            dma((3,)), dma((3,)),
            dma((3, bits)), dma((3, bits)),
            dma((3, halvings)), dma((3, halvings)),
            dma((bits + 1,)), dma((bits + 1,)),
        ],
        compiler_params=pltpu.CompilerParams(
            collective_id=1, has_side_effects=True, vmem_limit_bytes=60 * 1024 * 1024
        ),
        name="sum_grads",
    )(attn, mlp, norm)


RATE_NORM = 0.6


def body(
    chips,
    tokens,
    cotangent,
    queue,
    nbr_index,
    nbr_valid,
    norm_params,
    norm_first,
    norm_second,
    attn_weight,
    mlp_weight,
    attn_first,
    attn_second,
    mlp_first,
    mlp_second,
    attn_left,
    attn_right,
    mlp_left,
    mlp_right,
):
    def flip(value):
        return value.transpose(0, 2, 1)

    core = lax.axis_index("mp").reshape(1)
    cores = attn_weight.shape[1] // attn_weight.shape[2]
    picks = nbr_index.size // cores
    wanted = jnp.broadcast_to(nbr_index.reshape(cores, picks, 1), (cores, picks, queue.shape[0]))
    attn_own = flip(attn_weight)
    near, attn_low, mlp_low = fetch(chips, wanted, queue, attn_own, mlp_weight)
    width = queue.shape[1]
    block_out, input_grad, attn_part, mlp_part, norm_part = block(
        core,
        nbr_valid,
        tokens,
        cotangent,
        near,
        norm_params,
        attn_low.reshape(attn_low.shape[0], width, width),
        mlp_low,
    )
    attn_grad, mlp_grad, norm_grad = sum_grads(
        chips, attn_part.reshape(attn_low.shape), mlp_part, norm_part
    )
    block_out = lax.psum(block_out, "mp")
    input_grad = lax.psum(input_grad, "mp")
    norm_first_new = BETA_FIRST * norm_first + (1.0 - BETA_FIRST) * norm_grad
    norm_second_new = BETA_SECOND * norm_second + (1.0 - BETA_SECOND) * norm_grad * norm_grad
    norm_new = norm_params - RATE_NORM * (norm_first_new / (1.0 - BETA_FIRST**STEP)) / (
        jnp.sqrt(norm_second_new / (1.0 - BETA_SECOND**STEP)) + EPSILON
    )
    mlp_new, mlp_copy, mlp_first_new, mlp_second_new, mlp_left_new, mlp_right_new = update_stack(
        mlp_grad, mlp_weight, mlp_first, mlp_second, mlp_left, mlp_right
    )
    attn_new, attn_copy, attn_first_new, attn_second_new, attn_right_new, attn_left_new = update_stack(
        attn_grad, attn_own, flip(attn_first), flip(attn_second), attn_right, attn_left
    )
    return (
        block_out,
        input_grad,
        norm_grad,
        flip(attn_grad),
        mlp_grad,
        norm_first_new,
        norm_second_new,
        norm_new,
        flip(attn_first_new),
        flip(attn_second_new),
        mlp_first_new,
        mlp_second_new,
        attn_left_new,
        attn_right_new,
        mlp_left_new,
        mlp_right_new,
        flip(attn_new),
        flip(attn_copy),
        mlp_new,
        mlp_copy,
    )


def solution(mesh):
    return jax.shard_map(
        functools.partial(body, mesh.shape["dp"]),
        mesh=mesh,
        in_specs=(
            P("dp", None),
            P("dp", None),
            P("dp", None),
            P("dp", None),
            P("dp", None),
            P(),
            P(),
            P(),
            P(None, None, "mp"),
            P(None, None, "mp"),
            P(None, None, "mp"),
            P(None, None, "mp"),
            P(None, None, "mp"),
            P(None, None, "mp"),
            P(None, "mp", None),
            P(None, "mp", None),
            P(None, "mp", None),
            P(None, "mp", None),
        ),
        out_specs=(
            P("dp", None),
            P("dp", None),
            P(),
            P(None, None, "mp"),
            P(None, None, "mp"),
            P(),
            P(),
            P(),
            P(None, None, "mp"),
            P(None, None, "mp"),
            P(None, None, "mp"),
            P(None, None, "mp"),
            P(None, "mp", None),
            P(None, "mp", None),
            P(None, "mp", None),
            P(None, "mp", None),
            P(None, None, "mp"),
            P(None, None, "mp"),
            P(None, None, "mp"),
            P(None, None, "mp"),
        ),
        check_vma=False,
    )
```

```python
import functools
import math

import jax
import jax.numpy as jnp
from jax import lax
from jax.experimental import pallas as pl
from jax.experimental.pallas import tpu as pltpu
from jax.sharding import PartitionSpec as P

BETA_FIRST = 0.9
BETA_SECOND = 0.95
EPSILON = 1e-08
RATE_MATRIX = 0.15
DECAY_RATE = 0.05
TURN_RATE = 4.0
STEP = 10
BLOCK = 256
ROUNDS = 3
NEAR = 0.01
PIECE = 128

BF = jnp.bfloat16
F32 = jnp.float32


def dot_nn(a, b):
    return lax.dot_general(a, b, (((1,), (0,)), ((), ())), preferred_element_type=F32)


def dot_nt(a, b):
    return lax.dot_general(a, b, (((1,), (1,)), ((), ())), preferred_element_type=F32)


def dot_tn(a, b):
    return lax.dot_general(a, b, (((0,), (0,)), ((), ())), preferred_element_type=F32)


def split(a):
    high = a.astype(BF)
    return high, (a - high.astype(F32)).astype(BF)


def three(dot, a, b):
    return dot(a[0], b[0]) + (dot(a[0], b[1]) + dot(a[1], b[0]))


def below(size):
    row = lax.broadcasted_iota(jnp.int32, (size, size), 0)
    col = lax.broadcasted_iota(jnp.int32, (size, size), 1)
    return row > col, row == col


def in_step(chains):
    chains = list(chains)
    while chains:
        kept = []
        for chain in chains:
            try:
                next(chain)
                kept.append(chain)
            except StopIteration:
                pass
        chains = kept


def renew_chain(base_ref, out_ref, rest_ref, misses):
    width = base_ref.shape[1]
    source = base_ref
    for at in range(0, width, BLOCK):
        size = min(BLOCK, width - at)
        lower, same = below(size)
        eye = jnp.where(same, 1.0, 0.0)
        low = source[:, at:at + size].astype(BF)
        gram = dot_tn(low, low)
        yield
        on_diag = jnp.where(same, gram, 0.0)
        s_col = lax.rsqrt(jnp.maximum(jnp.sum(on_diag, axis=1, keepdims=True), 1e-30))
        s_row = lax.rsqrt(jnp.maximum(jnp.sum(on_diag, axis=0, keepdims=True), 1e-30))
        state = gram * s_col * s_row
        made = jnp.where(same, s_col, 0.0).astype(BF)
        for turn in range(ROUNDS):
            under = jnp.where(lower, state, 0.0)
            moved = dot_nn(under.astype(BF), state.astype(BF))
            mass = jnp.sum(under * under, axis=1, keepdims=True)
            yield
            curve = jnp.sum(moved * under, axis=1, keepdims=True)
            pace = jnp.where(curve > mass, mass / jnp.maximum(curve, 1e-30), 1.0)
            left = 1.0 - 2.0 * pace * mass + pace * pace * curve
            scale = lax.rsqrt(jnp.maximum(left, 1e-6))
            step = (scale * (eye - pace * under)).astype(BF)
            if turn + 1 < ROUNDS:
                state = dot_nt((scale * (state - pace * moved)).astype(BF), step)
            made = dot_nn(step, made).astype(BF)
            yield
        high, low = split(source[:, at:at + size])
        block = dot_nt(high, made) + dot_nt(low, made)
        yield
        pair = split(block)
        gram = three(dot_tn, pair, pair)
        yield
        off = jnp.where(lower, gram, 0.0) + jnp.where(same, 0.5 * (gram - 1.0), 0.0)
        misses.append(jnp.sum(off * off) * (1.0 / size))
        block = block - dot_nt(pair[0], off.astype(BF))
        out_ref[:, at:at + size] = block
        yield
        if at + size < width:
            pair = split(block)
            rest = source[:, at + size:]
            shared = split(three(dot_tn, pair, split(rest)))
            yield
            rest_ref[:, at + size:] = rest - three(dot_nn, pair, shared)
            source = rest_ref
            yield


def renew_rows(base_ref, out_ref, work_ref):
    size = base_ref.shape[0]
    group = 64
    work_ref[...] = base_ref[...].T

    def take(turn, carry):
        row = work_ref[pl.ds(turn, 1), :]
        row = row * lax.rsqrt(jnp.sum(row * row, axis=1, keepdims=True))
        work_ref[pl.ds(turn, 1), :] = row

        def clear(which, inner):
            here = pl.ds(pl.multiple_of(which * group, group), group)
            rows = work_ref[here, :]
            later = lax.broadcasted_iota(jnp.int32, (group, 1), 0) + which * group > turn
            share = jnp.where(later, jnp.sum(rows * row, axis=1, keepdims=True), 0.0)
            work_ref[here, :] = rows - share * row
            return inner

        return lax.fori_loop(turn // group, size // group, clear, carry)

    lax.fori_loop(0, size, take, 0)
    out_ref[...] = work_ref[...].T


def move_chain(grad, left_pair, right_pair, weight_ref, first_ref, second_ref, new_ref, copy_ref, first_new_ref, second_new_ref, move_ref):
    rows = grad.shape[0]
    for at in range(0, rows, PIECE):
        size = min(PIECE, rows - at)
        part = slice(at, at + size)
        half = dot_tn(left_pair[0][:, part], grad) + dot_tn(left_pair[1][:, part], grad)
        yield
        turned = three(dot_nn, split(half), right_pair)
        yield
        first_new = BETA_FIRST * first_ref[part, :] + (1.0 - BETA_FIRST) * turned
        second_new = BETA_SECOND * second_ref[part, :] + (1.0 - BETA_SECOND) * turned * turned
        first_new_ref[part, :] = first_new
        second_new_ref[part, :] = second_new
        move_ref[part, :] = (
            first_new
            / (1.0 - BETA_FIRST**STEP)
            / (jnp.sqrt(second_new / (1.0 - BETA_SECOND**STEP)) + EPSILON)
        ).astype(BF)
        yield
    for at in range(0, rows, PIECE):
        part = slice(at, min(at + PIECE, rows))
        back = dot_nn(left_pair[0][part, :], move_ref[...]).astype(BF)
        yield
        new = weight_ref[part, :] * (1.0 - RATE_MATRIX * DECAY_RATE) - RATE_MATRIX * dot_nt(back, right_pair[0])
        new_ref[part, :] = new
        copy_ref[part, :] = new.astype(BF)
        yield


def update_kernel(
    together,
    grad_ref, weight_ref, first_ref, second_ref, left_ref, right_ref,
    grad_out_ref, new_ref, copy_ref, first_new_ref, second_new_ref, left_new_ref, right_new_ref,
    left_base, right_base, left_rest, right_rest, move_ref,
):
    chains = []
    misses = []
    for which in range(together):
        grad = grad_ref[which]
        width = weight_ref.shape[2]
        if grad.shape[1] != width:
            height = weight_ref.shape[1]
            grad = jnp.concatenate([grad[at:at + height] for at in range(0, grad.shape[0], height)], axis=1)
        grad_out_ref[which] = grad.astype(F32)
        left = left_ref[which]
        right = right_ref[which]
        left_pair = split(left)
        right_pair = split(right)
        gram = dot_nt(grad, grad)
        pace = TURN_RATE / (jnp.sqrt(jnp.sum(gram * gram)) + 1e-06)
        left_base[which] = left + dot_nn(gram.astype(BF), left_pair[0]) * pace
        right_base[which] = right + dot_tn(grad, dot_nn(grad, right_pair[0]).astype(BF)) * pace
        misses.append(([], []))
        chains.append(renew_chain(right_base.at[which], right_new_ref.at[which], right_rest.at[which], misses[which][1]))
        chains.append(renew_chain(left_base.at[which], left_new_ref.at[which], left_rest.at[which], misses[which][0]))
        chains.append(
            move_chain(
                grad, left_pair, right_pair, weight_ref.at[which], first_ref.at[which], second_ref.at[which],
                new_ref.at[which], copy_ref.at[which], first_new_ref.at[which], second_new_ref.at[which],
                move_ref.at[which],
            )
        )
    in_step(chains)
    for which in range(together):
        for missed, base, out, rest in zip(
            misses[which], (left_base, right_base), (left_new_ref, right_new_ref), (left_rest, right_rest)
        ):
            worst = functools.reduce(jnp.maximum, missed)

            @pl.when(jnp.logical_not(worst < NEAR))
            def _(base=base, out=out, rest=rest):
                renew_rows(base.at[which], out.at[which], rest.at[which])


def update_stack(grad, skip, together, weight, first, second, left, right):
    slots, rows, width = weight.shape

    def spec(shape):
        return pl.BlockSpec((together,) + shape, lambda slot: (slot, 0, 0))

    flat = spec((rows, width))
    return pl.pallas_call(
        functools.partial(update_kernel, together),
        grid=(slots // together,),
        in_specs=[pl.BlockSpec((together,) + grad.shape[1:], lambda slot: (skip // together + slot, 0, 0))]
        + [flat] * 3 + [spec((rows, rows)), spec((width, width))],
        out_specs=[flat] * 5 + [spec((rows, rows)), spec((width, width))],
        out_shape=[
            jax.ShapeDtypeStruct(weight.shape, F32),
            jax.ShapeDtypeStruct(weight.shape, F32),
            jax.ShapeDtypeStruct(weight.shape, BF),
            jax.ShapeDtypeStruct(weight.shape, F32),
            jax.ShapeDtypeStruct(weight.shape, F32),
            jax.ShapeDtypeStruct(left.shape, F32),
            jax.ShapeDtypeStruct(right.shape, F32),
        ],
        scratch_shapes=[
            pltpu.VMEM((together, rows, rows), F32),
            pltpu.VMEM((together, width, width), F32),
            pltpu.VMEM((together, rows, rows), F32),
            pltpu.VMEM((together, width, width), F32),
            pltpu.VMEM((together, rows, width), BF),
        ],
        compiler_params=pltpu.CompilerParams(vmem_limit_bytes=60 * 1024 * 1024),
        name="rotated_update_%d" % width,
    )(grad, weight, first, second, left, right)


P_SIZE = 197
NBR = 8
HEAD = 64
ROWS = 208
FAR = 200
CHUNK = 256


def layer_norm(values, gain, shift):
    centre = values - jnp.mean(values, axis=-1, keepdims=True)
    scale = lax.rsqrt(jnp.mean(centre * centre, axis=-1, keepdims=True) + 1e-06)
    normal = centre * scale
    return (normal * gain + shift, normal, scale)


def norm_back(grad, normal, scale, gain):
    shaped = grad * gain
    return scale * (
        shaped
        - jnp.mean(shaped, axis=-1, keepdims=True)
        - normal * jnp.mean(shaped * normal, axis=-1, keepdims=True)
    )


def gelu_pair(value):
    size = jnp.abs(value) * (1.0 / math.sqrt(2.0))
    bell = jnp.exp(-0.5 * value * value)
    part = 1.0 / (1.0 + 0.3275911 * size)
    series = part * (
        0.254829592
        + part * (-0.284496736 + part * (1.421413741 + part * (-1.453152027 + part * 1.061405429)))
    )
    tail = 0.5 * series * bell
    share = jnp.where(value < 0.0, tail, 1.0 - tail)
    return value * share, share + value * bell * (1.0 / math.sqrt(2.0 * math.pi))


def block_kernel(
    images,
    core_ref, valid_ref,
    tokens_ref, cotangent_ref, near_ref, norms_ref, attn_ref, mlp_ref,
    out_ref, input_grad_ref, attn_grad_ref, mlp_grad_ref, norm_grad_ref,
    wide, far_f, tokens_f, normed, normal_one, scale_one, query, key, value, probs, mixed,
    middle, normal_two, scale_two, normed_two, cot_low, made, grad_two,
    grad_mid_low, grad_query, grad_key, grad_value,
):
    core = core_ref[0]
    total = tokens_ref.shape[0]
    width = tokens_ref.shape[1]

    def at_own_rows(act):
        for which in range(total // (images * P_SIZE)):

            @pl.when(core == which)
            def _(which=which):
                for image in range(images):
                    act((which * images + image) * P_SIZE, image * ROWS)

    def spread(source, target):
        def act(start, place):
            target[place:place + ROWS, :] = source[start:start + ROWS, :]

        at_own_rows(act)

    pairs = width // (2 * HEAD)
    wide[:total, :] = tokens_ref[...].astype(jnp.float32)
    wide[total:, :] = jnp.zeros((wide.shape[0] - total, width), jnp.float32)
    spread(wide, tokens_f)
    wide[:total, :] = cotangent_ref[...].astype(jnp.float32)
    spread(wide, made)
    far_f[...] = near_ref[...].astype(jnp.float32)
    own_row = lax.broadcasted_iota(jnp.int32, (ROWS, 1), 0) < P_SIZE
    lane = lax.broadcasted_iota(jnp.int32, (1, 2 * HEAD), 1)
    first_head = lane < HEAD
    key_lane = lax.broadcasted_iota(jnp.int32, (1, ROWS), 1)

    def halves(pair):
        zero = jnp.zeros_like(pair)
        return jnp.where(first_head, pair, zero), jnp.where(first_head, zero, pair)

    def step_forward(image, carry):
        here = pl.ds(pl.multiple_of(image * ROWS, ROWS), ROWS)
        x = tokens_f[here, :]
        cot_low[here, :] = jnp.where(own_row, made[here, :], 0.0).astype(BF)
        normed_f, normal, scale = layer_norm(x, norms_ref[0:1, :], norms_ref[1:2, :])
        normal_one[here, :] = normal
        scale_one[here, :] = scale
        allowed = key_lane < P_SIZE
        for slot in range(NBR):
            okay = valid_ref[core * images + image, slot] > 0
            allowed = jnp.logical_or(allowed, jnp.logical_and(key_lane == FAR + slot, okay))
        far = far_f[pl.ds(pl.multiple_of(image * NBR, NBR), NBR), :]
        normed_f = jnp.where(own_row, normed_f, 0.0)
        full = jnp.concatenate([normed_f[:FAR, :], far], axis=0).astype(BF)
        normed[here, :] = full
        q = dot_nt(full, attn_ref[0]).astype(BF)
        k = dot_nt(full, attn_ref[1]).astype(BF)
        v = dot_nt(full, attn_ref[2]).astype(BF)
        query[here, :] = q
        key[here, :] = k
        value[here, :] = v
        bias = jnp.where(allowed, 0.0, -1e30)
        parts = []
        for pair in range(pairs):
            cols = slice(pair * 2 * HEAD, (pair + 1) * 2 * HEAD)
            k_pair = k[:, cols]
            sums = 0.0
            for head, (q_one, v_one) in enumerate(zip(halves(q[:, cols]), halves(v[:, cols]))):
                scores = dot_nt(q_one, k_pair) * 0.125 + bias
                top = jnp.max(scores, axis=-1, keepdims=True)
                powers = jnp.exp(scores - top)
                prob = powers / jnp.sum(powers, axis=-1, keepdims=True)
                probs[image * 2 * pairs + 2 * pair + head] = prob
                sums = sums + dot_nn(prob.astype(BF), v_one)
            parts.append(sums.astype(BF))
        mix = jnp.concatenate(parts, axis=1)
        mixed[here, :] = mix
        mid = x + dot_nn(mix, attn_ref[3])
        middle[here, :] = mid
        two_f, normal, scale = layer_norm(mid, norms_ref[2:3, :], norms_ref[3:4, :])
        normal_two[here, :] = normal
        scale_two[here, :] = scale
        normed_two[here, :] = two_f.astype(BF)
        return carry

    lax.fori_loop(0, images, step_forward, 0)

    made[...] = jnp.zeros_like(made)
    grad_two[...] = jnp.zeros_like(grad_two)
    chunks = mlp_ref.shape[3] // CHUNK

    def step_mlp(turn, carry):
        half = turn // chunks
        cols = pl.ds(pl.multiple_of((turn % chunks) * CHUNK, CHUNK), CHUNK)
        w_one = mlp_ref[0, half, :, cols]
        w_two = mlp_ref[1, half, :, cols]
        two = normed_two[...]
        cot = cot_low[...]
        hidden, slope = gelu_pair(dot_nn(two, w_one))
        hidden = hidden.astype(BF)
        grad_inner = (dot_nn(cot, w_two) * slope).astype(BF)
        made[...] += dot_nt(hidden, w_two)
        grad_two[...] += dot_nt(grad_inner, w_one)
        mlp_grad_ref[0, half, :, cols] = dot_tn(two, grad_inner)
        mlp_grad_ref[1, half, :, cols] = dot_tn(cot, hidden)
        return carry

    lax.fori_loop(0, 2 * chunks, step_mlp, 0)

    norm_grad_ref[...] = jnp.zeros_like(norm_grad_ref)
    input_grad_ref[...] = jnp.zeros_like(input_grad_ref)
    wide[...] = jnp.zeros_like(wide)

    def step_backward(image, carry):
        here = pl.ds(pl.multiple_of(image * ROWS, ROWS), ROWS)
        made[here, :] += middle[here, :]
        grad_n = grad_two[here, :]
        normal = normal_two[here, :]
        norm_grad_ref[2:3, :] += jnp.sum(grad_n * normal, axis=0, keepdims=True)
        norm_grad_ref[3:4, :] += jnp.sum(grad_n, axis=0, keepdims=True)
        grad_mid = cot_low[here, :].astype(jnp.float32) + norm_back(
            grad_n, normal, scale_two[here, :], norms_ref[2:3, :]
        )
        low = grad_mid.astype(BF)
        grad_mid_low[here, :] = low
        grad_mix = dot_nt(low, attn_ref[3]).astype(BF)
        q = query[here, :]
        k = key[here, :]
        v = value[here, :]
        parts_q, parts_k, parts_v = [], [], []
        for pair in range(pairs):
            cols = slice(pair * 2 * HEAD, (pair + 1) * 2 * HEAD)
            gm_pair = grad_mix[:, cols]
            sum_q = sum_k = sum_v = 0.0
            for head, (q_one, k_one, v_one, gm_one) in enumerate(
                zip(halves(q[:, cols]), halves(k[:, cols]), halves(v[:, cols]), halves(gm_pair))
            ):
                prob = probs[image * 2 * pairs + 2 * pair + head]
                grad_prob = dot_nt(gm_pair, v_one)
                sum_v = sum_v + dot_tn(prob.astype(BF), gm_one)
                weighed = prob * grad_prob
                grad_score = (
                    weighed - prob * jnp.sum(weighed, axis=-1, keepdims=True)
                ).astype(BF)
                sum_q = sum_q + dot_nn(grad_score, k_one)
                sum_k = sum_k + dot_tn(grad_score, q_one)
            parts_q.append((sum_q * 0.125).astype(BF))
            parts_k.append((sum_k * 0.125).astype(BF))
            parts_v.append(sum_v.astype(BF))
        gq = jnp.concatenate(parts_q, axis=1)
        gk = jnp.concatenate(parts_k, axis=1)
        gv = jnp.concatenate(parts_v, axis=1)
        grad_query[here, :] = gq
        grad_key[here, :] = gk
        grad_value[here, :] = gv
        grad_n = dot_nn(gq, attn_ref[0]) + dot_nn(gk, attn_ref[1]) + dot_nn(gv, attn_ref[2])
        grad_n = jnp.where(own_row, grad_n, 0.0)
        normal = normal_one[here, :]
        norm_grad_ref[0:1, :] += jnp.sum(grad_n * normal, axis=0, keepdims=True)
        norm_grad_ref[1:2, :] += jnp.sum(grad_n, axis=0, keepdims=True)
        back = grad_mid + norm_back(grad_n, normal, scale_one[here, :], norms_ref[0:1, :])
        middle[here, :] = back
        return carry

    lax.fori_loop(0, images, step_backward, 0)

    def pack(start, place):
        wide[start:start + P_SIZE, :] = made[place:place + P_SIZE, :]
        input_grad_ref[start:start + P_SIZE, :] = middle[place:place + P_SIZE, :]

    at_own_rows(pack)
    out_ref[...] = wide[:total, :].astype(BF)
    attn_grad_ref[0] = dot_tn(grad_query[...], normed[...])
    attn_grad_ref[1] = dot_tn(grad_key[...], normed[...])
    attn_grad_ref[2] = dot_tn(grad_value[...], normed[...])
    attn_grad_ref[3] = dot_tn(mixed[...], grad_mid_low[...])


def block(core, nbr_valid, tokens, cotangent, near, norms, attn, mlp):
    total, width = tokens.shape
    images = nbr_valid.shape[0] // mlp.shape[1]
    rows = images * ROWS
    padded = total + 16 - total % 8
    f32 = jnp.float32
    vmem = pl.BlockSpec(memory_space=pltpu.VMEM)
    smem = pl.BlockSpec(memory_space=pltpu.SMEM)
    heads = width // HEAD
    flat_f = pltpu.VMEM((rows, width), f32)
    flat_low = pltpu.VMEM((rows, width), BF)
    column = pltpu.VMEM((rows, 1), f32)
    return pl.pallas_call(
        functools.partial(block_kernel, images),
        in_specs=[smem] * 2 + [vmem] * 6,
        out_specs=[vmem] * 5,
        out_shape=[
            jax.ShapeDtypeStruct((total, width), BF),
            jax.ShapeDtypeStruct((total, width), f32),
            jax.ShapeDtypeStruct(attn.shape, f32),
            jax.ShapeDtypeStruct(mlp.shape, f32),
            jax.ShapeDtypeStruct((4, width), f32),
        ],
        scratch_shapes=[
            pltpu.VMEM((padded, width), f32),
            pltpu.VMEM(near.shape, f32),
            flat_f,
            flat_low, flat_f, column, flat_low, flat_low, flat_low,
            pltpu.VMEM((images * heads, ROWS, ROWS), f32),
            flat_low,
            flat_f, flat_f, column, flat_low, flat_low, flat_f, flat_f,
            flat_low, flat_low, flat_low, flat_low,
        ],
        compiler_params=pltpu.CompilerParams(vmem_limit_bytes=60 * 1024 * 1024),
        name="block_both_ways",
    )(core, nbr_valid, tokens, cotangent, near, norms, attn, mlp)


MESH = pl.DeviceIdType.MESH


def fetch_kernel(
    chips, picks,
    wanted_ref, queue_ref, attn_ref, mlp_ref,
    near_ref, attn_out, mlp_out,
    asked, given, parts, ask_send, ask_recv, give_send, give_recv, swap_send, swap_recv,
):
    me = lax.axis_index("dp")
    core = lax.axis_index("mp")
    other = 1 - core
    depth = queue_ref.shape[0]
    barrier = pltpu.get_barrier_semaphore()
    pl.semaphore_signal(barrier, inc=1, device_id=(me, other), device_id_type=MESH)

    def greet(hop, carry):
        pl.semaphore_signal(
            barrier, inc=1, device_id=(lax.rem(me + hop, chips), core), device_id_type=MESH
        )
        return carry

    lax.fori_loop(1, chips, greet, 0)
    attn_out[:, core] = attn_ref[...].astype(BF)
    mlp_out[:, core] = mlp_ref[...].astype(BF)
    pl.semaphore_wait(barrier, chips)

    def ask(hop):
        return pltpu.make_async_remote_copy(
            src_ref=wanted_ref.at[core],
            dst_ref=asked.at[hop],
            send_sem=ask_send.at[hop],
            recv_sem=ask_recv.at[hop],
            device_id=(lax.rem(me + hop, chips), core),
            device_id_type=MESH,
        )

    def give(hop):
        return pltpu.make_async_remote_copy(
            src_ref=parts.at[hop],
            dst_ref=given.at[hop],
            send_sem=give_send.at[hop],
            recv_sem=give_recv.at[hop],
            device_id=(lax.rem(me + chips - hop, chips), core),
            device_id_type=MESH,
        )

    def start_ask(hop, carry):
        ask(hop).start()
        return carry

    lax.fori_loop(1, chips, start_ask, 0)
    swaps = [
        pltpu.make_async_remote_copy(
            src_ref=out.at[:, core],
            dst_ref=out.at[:, core],
            send_sem=swap_send.at[place],
            recv_sem=swap_recv.at[place],
            device_id=(me, other),
            device_id_type=MESH,
        )
        for place, out in enumerate((attn_out, mlp_out))
    ]
    for swap in swaps:
        swap.start()
    places = lax.broadcasted_iota(jnp.int32, (picks, depth), 1) + me * depth

    def choose(wanted):
        chooser = jnp.where(wanted == places, 1.0, 0.0).astype(BF)
        return dot_nn(chooser, queue_ref[...]).astype(BF)

    given[0] = choose(wanted_ref[core])

    def answer(hop, carry):
        ask(hop).wait_recv()
        parts[hop] = choose(asked[hop])
        give(hop).start()
        return carry

    lax.fori_loop(1, chips, answer, 0)

    def collect(hop, total):
        give(hop).wait_recv()
        return total + given[hop].astype(jnp.float32)

    total = lax.fori_loop(1, chips, collect, given[0].astype(jnp.float32))
    near_ref[...] = total.astype(BF)

    def finish(hop, carry):
        ask(hop).wait_send()
        give(hop).wait_send()
        return carry

    lax.fori_loop(1, chips, finish, 0)
    for swap in swaps:
        swap.wait()


def fetch(chips, wanted, queue, attn, mlp):
    cores, picks, lanes = wanted.shape
    vmem = pl.BlockSpec(memory_space=pltpu.VMEM)
    width = queue.shape[1]
    return pl.pallas_call(
        functools.partial(fetch_kernel, chips, picks),
        in_specs=[vmem] * 4,
        out_specs=[vmem] * 3,
        out_shape=[
            jax.ShapeDtypeStruct((picks, width), BF),
            jax.ShapeDtypeStruct((attn.shape[0], cores) + attn.shape[1:], BF),
            jax.ShapeDtypeStruct((mlp.shape[0], cores) + mlp.shape[1:], BF),
        ],
        scratch_shapes=[
            pltpu.VMEM((chips, picks, lanes), jnp.int32),
            pltpu.VMEM((chips, picks, width), BF),
            pltpu.VMEM((chips, picks, width), BF),
            pltpu.SemaphoreType.DMA((chips,)),
            pltpu.SemaphoreType.DMA((chips,)),
            pltpu.SemaphoreType.DMA((chips,)),
            pltpu.SemaphoreType.DMA((chips,)),
            pltpu.SemaphoreType.DMA((2,)),
            pltpu.SemaphoreType.DMA((2,)),
        ],
        compiler_params=pltpu.CompilerParams(
            collective_id=0, has_side_effects=True, vmem_limit_bytes=48 * 1024 * 1024
        ),
        name="fetch",
    )(wanted, queue, attn, mlp)


HALVINGS = 4


def orders(bits):
    base = list(range(bits))
    if bits < 3:
        return [base, base[::-1], base]
    low = base[:2]
    return [base, low[::-1] + base[2:], base[2:4] + low + base[4:]]


def sum_kernel(
    bits,
    attn_ref, mlp_ref, norm_ref,
    done, norm_out,
    total, first_send, first_recv, sent, recv, norm_recv, norm_work,
    swap_send, swap_recv, step_send, step_recv, spread_send, spread_recv, norm_send, norm_sem,
):
    me = lax.axis_index("dp")
    core = lax.axis_index("mp")
    other = 1 - core
    slots, cores, rows, width = attn_ref.shape
    height = slots * rows
    halvings = min(HALVINGS, bits)
    plan = orders(bits)
    parts = 3

    def mate(bit):
        return me + (1 - 2 * ((me // 2**bit) % 2)) * 2**bit

    barrier = pltpu.get_barrier_semaphore()
    pl.semaphore_signal(barrier, inc=1, device_id=(me, other), device_id_type=MESH)
    for bit in range(bits):
        pl.semaphore_signal(barrier, inc=1, device_id=(mate(bit), core), device_id_type=MESH)

    def fill(target, part, whose, cast):
        if part < 2:
            for block in range(mlp_ref.shape[3] // width):
                target[part, block * mlp_ref.shape[2]:(block + 1) * mlp_ref.shape[2], :] = mlp_ref[
                    part, whose, :, block * width:(block + 1) * width
                ].astype(cast)
        else:
            for slot in range(slots):
                target[part, slot * rows:(slot + 1) * rows, :] = attn_ref[slot, whose].astype(cast)

    for part in range(parts):
        fill(first_send, part, other, BF)
    pl.semaphore_wait(barrier, bits + 1)

    def copy(src, dst, send, recv, device):
        return pltpu.make_async_remote_copy(
            src_ref=src, dst_ref=dst, send_sem=send, recv_sem=recv, device_id=device, device_id_type=MESH
        )

    pending = []
    swaps = []
    for part in range(parts):
        swap = copy(first_send.at[part], first_recv.at[part], swap_send.at[part], swap_recv.at[part], (me, other))
        swap.start()
        swaps.append(swap)
    norm_work[0] = norm_ref[...]
    norm_copy = copy(norm_work.at[0], norm_recv.at[0], norm_send.at[0], norm_sem.at[0], (me, other))
    norm_copy.start()
    for part in range(parts):
        fill(total, part, core, jnp.float32)

    offsets = [0] * parts
    size = height
    copies = [None] * parts
    for step in range(halvings + 1):
        half = size // 2
        for part in range(parts):
            held = pl.ds(pl.multiple_of(offsets[part], 16), size)
            if step == 0:
                swaps[part].wait_recv()
                arrived = first_recv.at[part]
            else:
                copies[part].wait_recv()
                arrived = recv.at[part, pl.ds(height - 2 * size, size)]
            total[part, held, :] += arrived[...].astype(jnp.float32)
            if step < halvings:
                bit = plan[part][step]
                mine = (me // 2**bit) % 2
                away = pl.multiple_of(offsets[part] + (1 - mine) * half, 16)
                slot = pl.ds(height - 2 * half, half)
                sent[part, slot, :] = total[part, pl.ds(away, half), :].astype(BF)
                copies[part] = copy(
                    sent.at[part, slot],
                    recv.at[part, slot],
                    step_send.at[part, step],
                    step_recv.at[part, step],
                    (mate(bit), core),
                )
                copies[part].start()
                pending.append(copies[part])
                offsets[part] = offsets[part] + mine * half
        if step < halvings:
            size = half
    for step in range(bits + 1):
        norm_copy.wait()
        if step < bits:
            norm_work[step + 1] = norm_work[step] + norm_recv[step]
            norm_copy = copy(
                norm_work.at[step + 1],
                norm_recv.at[step + 1],
                norm_send.at[step + 1],
                norm_sem.at[step + 1],
                (mate(step), core),
            )
            norm_copy.start()
        else:
            norm_out[...] = norm_work[step] + norm_recv[step]
    for step in range(halvings, bits):
        for part in range(parts):
            bit = plan[part][step]
            held = pl.ds(pl.multiple_of(offsets[part], 16), size)
            place = height + (step - halvings) * size
            slot = pl.ds(place, size)
            sent[part, slot, :] = total[part, held, :].astype(BF)
            copies[part] = copy(
                sent.at[part, slot],
                recv.at[part, slot],
                step_send.at[part, step],
                step_recv.at[part, step],
                (mate(bit), core),
            )
            copies[part].start()
            pending.append(copies[part])
        for part in range(parts):
            held = pl.ds(pl.multiple_of(offsets[part], 16), size)
            slot = pl.ds(height + (step - halvings) * size, size)
            copies[part].wait_recv()
            total[part, held, :] = sent[part, slot, :].astype(jnp.float32) + recv[part, slot, :].astype(jnp.float32)
    for part in range(parts):
        held = pl.ds(pl.multiple_of(offsets[part], 16), size)
        done[part, held, :] = total[part, held, :].astype(BF)
    for back in range(halvings):
        step = halvings - 1 - back
        for part in range(parts):
            bit = plan[part][step]
            held = pl.ds(pl.multiple_of(offsets[part], 16), size)
            copies[part] = copy(
                done.at[part, held],
                done.at[part, held],
                spread_send.at[part, step],
                spread_recv.at[part, step],
                (mate(bit), core),
            )
            if back > 0:
                previous[part].wait_recv()
            copies[part].start()
            pending.append(copies[part])
            mine = (me // 2**bit) % 2
            offsets[part] = offsets[part] - mine * size
        previous = list(copies)
        size = size * 2
    for part in range(parts):
        previous[part].wait_recv()
    for one in swaps + pending:
        one.wait_send()


def sum_grads(chips, attn, mlp, norm):
    bits = chips.bit_length() - 1
    slots, cores, rows, width = attn.shape
    height = slots * rows
    halvings = min(HALVINGS, bits)
    tall = height + (bits - halvings) * (height >> halvings)
    vmem = pl.BlockSpec(memory_space=pltpu.VMEM)
    f32 = jnp.float32
    dma = pltpu.SemaphoreType.DMA
    return pl.pallas_call(
        functools.partial(sum_kernel, bits),
        in_specs=[vmem] * 3,
        out_specs=[vmem] * 2,
        out_shape=[
            jax.ShapeDtypeStruct((3, height, width), BF),
            jax.ShapeDtypeStruct(norm.shape, f32),
        ],
        scratch_shapes=[
            pltpu.VMEM((3, height, width), f32),
            pltpu.VMEM((3, height, width), BF),
            pltpu.VMEM((3, height, width), BF),
            pltpu.VMEM((3, tall, width), BF),
            pltpu.VMEM((3, tall, width), BF),
            pltpu.VMEM((bits + 1,) + norm.shape, f32),
            pltpu.VMEM((bits + 1,) + norm.shape, f32),
            dma((3,)), dma((3,)),
            dma((3, bits)), dma((3, bits)),
            dma((3, halvings)), dma((3, halvings)),
            dma((bits + 1,)), dma((bits + 1,)),
        ],
        compiler_params=pltpu.CompilerParams(
            collective_id=1, has_side_effects=True, vmem_limit_bytes=60 * 1024 * 1024
        ),
        name="sum_grads",
    )(attn, mlp, norm)


RATE_NORM = 0.6


def body(
    chips,
    tokens,
    cotangent,
    queue,
    nbr_index,
    nbr_valid,
    norm_params,
    norm_first,
    norm_second,
    attn_weight,
    mlp_weight,
    attn_first,
    attn_second,
    mlp_first,
    mlp_second,
    attn_left,
    attn_right,
    mlp_left,
    mlp_right,
):
    def flip(value):
        return value.transpose(0, 2, 1)

    core = lax.axis_index("mp").reshape(1)
    cores = attn_weight.shape[1] // attn_weight.shape[2]
    picks = nbr_index.size // cores
    wanted = jnp.broadcast_to(nbr_index.reshape(cores, picks, 1), (cores, picks, queue.shape[0]))
    attn_own = flip(attn_weight)
    near, attn_low, mlp_low = fetch(chips, wanted, queue, attn_own, mlp_weight)
    width = queue.shape[1]
    block_out, input_grad, attn_part, mlp_part, norm_part = block(
        core,
        nbr_valid,
        tokens,
        cotangent,
        near,
        norm_params,
        attn_low.reshape(attn_low.shape[0], width, width),
        mlp_low,
    )
    summed, norm_grad = sum_grads(chips, attn_part.reshape(attn_low.shape), mlp_part, norm_part)
    block_out = lax.psum(block_out, "mp")
    input_grad = lax.psum(input_grad, "mp")
    norm_first_new = BETA_FIRST * norm_first + (1.0 - BETA_FIRST) * norm_grad
    norm_second_new = BETA_SECOND * norm_second + (1.0 - BETA_SECOND) * norm_grad * norm_grad
    norm_new = norm_params - RATE_NORM * (norm_first_new / (1.0 - BETA_FIRST**STEP)) / (
        jnp.sqrt(norm_second_new / (1.0 - BETA_SECOND**STEP)) + EPSILON
    )
    slots, rows, width = attn_own.shape
    (
        mlp_grad,
        mlp_new,
        mlp_copy,
        mlp_first_new,
        mlp_second_new,
        mlp_left_new,
        mlp_right_new,
    ) = update_stack(
        summed, 0, 1, mlp_weight, mlp_first, mlp_second, mlp_left, mlp_right
    )
    (
        attn_grad,
        attn_new,
        attn_copy,
        attn_first_new,
        attn_second_new,
        attn_right_new,
        attn_left_new,
    ) = update_stack(
        summed.reshape(-1, rows, width),
        2 * slots,
        2,
        attn_own,
        flip(attn_first),
        flip(attn_second),
        attn_right,
        attn_left,
    )
    return (
        block_out,
        input_grad,
        norm_grad,
        flip(attn_grad),
        mlp_grad,
        norm_first_new,
        norm_second_new,
        norm_new,
        flip(attn_first_new),
        flip(attn_second_new),
        mlp_first_new,
        mlp_second_new,
        attn_left_new,
        attn_right_new,
        mlp_left_new,
        mlp_right_new,
        flip(attn_new),
        flip(attn_copy),
        mlp_new,
        mlp_copy,
    )


def solution(mesh):
    return jax.shard_map(
        functools.partial(body, mesh.shape["dp"]),
        mesh=mesh,
        in_specs=(
            P("dp", None),
            P("dp", None),
            P("dp", None),
            P("dp", None),
            P("dp", None),
            P(),
            P(),
            P(),
            P(None, None, "mp"),
            P(None, None, "mp"),
            P(None, None, "mp"),
            P(None, None, "mp"),
            P(None, None, "mp"),
            P(None, None, "mp"),
            P(None, "mp", None),
            P(None, "mp", None),
            P(None, "mp", None),
            P(None, "mp", None),
        ),
        out_specs=(
            P("dp", None),
            P("dp", None),
            P(),
            P(None, None, "mp"),
            P(None, None, "mp"),
            P(),
            P(),
            P(),
            P(None, None, "mp"),
            P(None, None, "mp"),
            P(None, None, "mp"),
            P(None, None, "mp"),
            P(None, "mp", None),
            P(None, "mp", None),
            P(None, "mp", None),
            P(None, "mp", None),
            P(None, None, "mp"),
            P(None, None, "mp"),
            P(None, None, "mp"),
            P(None, None, "mp"),
        ),
        check_vma=False,
    )
```

```python
import functools
import math

import jax
import jax.numpy as jnp
from jax import lax
from jax.experimental import pallas as pl
from jax.experimental.pallas import tpu as pltpu
from jax.sharding import PartitionSpec as P

BETA_FIRST = 0.9
BETA_SECOND = 0.95
EPSILON = 1e-08
RATE_MATRIX = 0.15
DECAY_RATE = 0.05
TURN_RATE = 4.0
STEP = 10
BLOCK = 256
ROUNDS = 3
NEAR = 0.01
PIECE = 128

BF = jnp.bfloat16
F32 = jnp.float32


def dot_nn(a, b):
    return lax.dot_general(a, b, (((1,), (0,)), ((), ())), preferred_element_type=F32)


def dot_nt(a, b):
    return lax.dot_general(a, b, (((1,), (1,)), ((), ())), preferred_element_type=F32)


def dot_tn(a, b):
    return lax.dot_general(a, b, (((0,), (0,)), ((), ())), preferred_element_type=F32)


def split(a):
    high = a.astype(BF)
    return high, (a - high.astype(F32)).astype(BF)


def three(dot, a, b):
    return dot(a[0], b[0]) + (dot(a[0], b[1]) + dot(a[1], b[0]))


def below(size):
    row = lax.broadcasted_iota(jnp.int32, (size, size), 0)
    col = lax.broadcasted_iota(jnp.int32, (size, size), 1)
    return row > col, row == col


def in_step(chains):
    chains = list(chains)
    while chains:
        kept = []
        for chain in chains:
            try:
                next(chain)
                kept.append(chain)
            except StopIteration:
                pass
        chains = kept


def renew_chain(base_ref, out_ref, rest_ref, misses):
    width = base_ref.shape[1]
    source = base_ref
    for at in range(0, width, BLOCK):
        size = min(BLOCK, width - at)
        lower, same = below(size)
        eye = jnp.where(same, 1.0, 0.0)
        low = source[:, at:at + size].astype(BF)
        gram = dot_tn(low, low)
        yield
        on_diag = jnp.where(same, gram, 0.0)
        s_col = lax.rsqrt(jnp.maximum(jnp.sum(on_diag, axis=1, keepdims=True), 1e-30))
        s_row = lax.rsqrt(jnp.maximum(jnp.sum(on_diag, axis=0, keepdims=True), 1e-30))
        state = gram * s_col * s_row
        made = jnp.where(same, s_col, 0.0).astype(BF)
        for turn in range(ROUNDS):
            under = jnp.where(lower, state, 0.0)
            moved = dot_nn(under.astype(BF), state.astype(BF))
            mass = jnp.sum(under * under, axis=1, keepdims=True)
            yield
            curve = jnp.sum(moved * under, axis=1, keepdims=True)
            pace = jnp.where(curve > mass, mass / jnp.maximum(curve, 1e-30), 1.0)
            left = 1.0 - 2.0 * pace * mass + pace * pace * curve
            scale = lax.rsqrt(jnp.maximum(left, 1e-6))
            step = (scale * (eye - pace * under)).astype(BF)
            if turn + 1 < ROUNDS:
                state = dot_nt((scale * (state - pace * moved)).astype(BF), step)
            made = dot_nn(step, made).astype(BF)
            yield
        high, low = split(source[:, at:at + size])
        block = dot_nt(high, made) + dot_nt(low, made)
        yield
        pair = split(block)
        gram = three(dot_tn, pair, pair)
        yield
        off = jnp.where(lower, gram, 0.0) + jnp.where(same, 0.5 * (gram - 1.0), 0.0)
        misses.append(jnp.sum(off * off) * (1.0 / size))
        block = block - dot_nt(pair[0], off.astype(BF))
        out_ref[:, at:at + size] = block
        yield
        if at + size < width:
            pair = split(block)
            rest = source[:, at + size:]
            shared = split(three(dot_tn, pair, split(rest)))
            yield
            rest_ref[:, at + size:] = rest - three(dot_nn, pair, shared)
            source = rest_ref
            yield


def renew_rows(base_ref, out_ref, work_ref):
    size = base_ref.shape[0]
    group = 64
    work_ref[...] = base_ref[...].T

    def take(turn, carry):
        row = work_ref[pl.ds(turn, 1), :]
        row = row * lax.rsqrt(jnp.sum(row * row, axis=1, keepdims=True))
        work_ref[pl.ds(turn, 1), :] = row

        def clear(which, inner):
            here = pl.ds(pl.multiple_of(which * group, group), group)
            rows = work_ref[here, :]
            later = lax.broadcasted_iota(jnp.int32, (group, 1), 0) + which * group > turn
            share = jnp.where(later, jnp.sum(rows * row, axis=1, keepdims=True), 0.0)
            work_ref[here, :] = rows - share * row
            return inner

        return lax.fori_loop(turn // group, size // group, clear, carry)

    lax.fori_loop(0, size, take, 0)
    out_ref[...] = work_ref[...].T


def move_chain(grad, left_pair, right_pair, weight_ref, first_ref, second_ref, new_ref, copy_ref, first_new_ref, second_new_ref, move_ref):
    rows = grad.shape[0]
    for at in range(0, rows, PIECE):
        size = min(PIECE, rows - at)
        part = slice(at, at + size)
        half = dot_tn(left_pair[0][:, part], grad) + dot_tn(left_pair[1][:, part], grad)
        yield
        turned = three(dot_nn, split(half), right_pair)
        yield
        first_new = BETA_FIRST * first_ref[part, :] + (1.0 - BETA_FIRST) * turned
        second_new = BETA_SECOND * second_ref[part, :] + (1.0 - BETA_SECOND) * turned * turned
        first_new_ref[part, :] = first_new
        second_new_ref[part, :] = second_new
        move_ref[part, :] = (
            first_new
            / (1.0 - BETA_FIRST**STEP)
            / (jnp.sqrt(second_new / (1.0 - BETA_SECOND**STEP)) + EPSILON)
        ).astype(BF)
        yield
    for at in range(0, rows, PIECE):
        part = slice(at, min(at + PIECE, rows))
        back = dot_nn(left_pair[0][part, :], move_ref[...]).astype(BF)
        yield
        new = weight_ref[part, :] * (1.0 - RATE_MATRIX * DECAY_RATE) - RATE_MATRIX * dot_nt(back, right_pair[0])
        new_ref[part, :] = new
        copy_ref[part, :] = new.astype(BF)
        yield


def update_kernel(
    together,
    grad_ref, weight_ref, first_ref, second_ref, left_ref, right_ref,
    grad_out_ref, new_ref, copy_ref, first_new_ref, second_new_ref, left_new_ref, right_new_ref,
    left_base, right_base, left_rest, right_rest, move_ref,
):
    chains = []
    misses = []
    for which in range(together):
        grad = grad_ref[which]
        width = weight_ref.shape[2]
        if grad.shape[1] != width:
            height = weight_ref.shape[1]
            grad = jnp.concatenate([grad[at:at + height] for at in range(0, grad.shape[0], height)], axis=1)
        grad_out_ref[which] = grad.astype(F32)
        left = left_ref[which]
        right = right_ref[which]
        left_pair = split(left)
        right_pair = split(right)
        gram = dot_nt(grad, grad)
        pace = TURN_RATE / (jnp.sqrt(jnp.sum(gram * gram)) + 1e-06)
        left_base[which] = left + dot_nn(gram.astype(BF), left_pair[0]) * pace
        right_base[which] = right + dot_tn(grad, dot_nn(grad, right_pair[0]).astype(BF)) * pace
        misses.append(([], []))
        chains.append(renew_chain(right_base.at[which], right_new_ref.at[which], right_rest.at[which], misses[which][1]))
        chains.append(renew_chain(left_base.at[which], left_new_ref.at[which], left_rest.at[which], misses[which][0]))
        chains.append(
            move_chain(
                grad, left_pair, right_pair, weight_ref.at[which], first_ref.at[which], second_ref.at[which],
                new_ref.at[which], copy_ref.at[which], first_new_ref.at[which], second_new_ref.at[which],
                move_ref.at[which],
            )
        )
    in_step(chains)
    for which in range(together):
        for missed, base, out, rest in zip(
            misses[which], (left_base, right_base), (left_new_ref, right_new_ref), (left_rest, right_rest)
        ):
            worst = functools.reduce(jnp.maximum, missed)

            @pl.when(jnp.logical_not(worst < NEAR))
            def _(base=base, out=out, rest=rest):
                renew_rows(base.at[which], out.at[which], rest.at[which])


def update_stack(grad, skip, together, weight, first, second, left, right):
    slots, rows, width = weight.shape

    def spec(shape):
        return pl.BlockSpec((together,) + shape, lambda slot: (slot, 0, 0))

    flat = spec((rows, width))
    return pl.pallas_call(
        functools.partial(update_kernel, together),
        grid=(slots // together,),
        in_specs=[pl.BlockSpec((together,) + grad.shape[1:], lambda slot: (skip // together + slot, 0, 0))]
        + [flat] * 3 + [spec((rows, rows)), spec((width, width))],
        out_specs=[flat] * 5 + [spec((rows, rows)), spec((width, width))],
        out_shape=[
            jax.ShapeDtypeStruct(weight.shape, F32),
            jax.ShapeDtypeStruct(weight.shape, F32),
            jax.ShapeDtypeStruct(weight.shape, BF),
            jax.ShapeDtypeStruct(weight.shape, F32),
            jax.ShapeDtypeStruct(weight.shape, F32),
            jax.ShapeDtypeStruct(left.shape, F32),
            jax.ShapeDtypeStruct(right.shape, F32),
        ],
        scratch_shapes=[
            pltpu.VMEM((together, rows, rows), F32),
            pltpu.VMEM((together, width, width), F32),
            pltpu.VMEM((together, rows, rows), F32),
            pltpu.VMEM((together, width, width), F32),
            pltpu.VMEM((together, rows, width), BF),
        ],
        compiler_params=pltpu.CompilerParams(vmem_limit_bytes=60 * 1024 * 1024),
        name="rotated_update_%d" % width,
    )(grad, weight, first, second, left, right)


MESH = pl.DeviceIdType.MESH
P_SIZE = 197
NBR = 8
HEAD = 64
ROWS = 208
FAR = 200
CHUNK = 256
RADIX = 4
PARTS = 3


def layer_norm(values, gain, shift):
    centre = values - jnp.mean(values, axis=-1, keepdims=True)
    scale = lax.rsqrt(jnp.mean(centre * centre, axis=-1, keepdims=True) + 1e-06)
    normal = centre * scale
    return (normal * gain + shift, normal, scale)


def norm_back(grad, normal, scale, gain):
    shaped = grad * gain
    return scale * (
        shaped
        - jnp.mean(shaped, axis=-1, keepdims=True)
        - normal * jnp.mean(shaped * normal, axis=-1, keepdims=True)
    )


def gelu_pair(value):
    size = jnp.abs(value) * (1.0 / math.sqrt(2.0))
    bell = jnp.exp(-0.5 * value * value)
    part = 1.0 / (1.0 + 0.3275911 * size)
    series = part * (
        0.254829592
        + part * (-0.284496736 + part * (1.421413741 + part * (-1.453152027 + part * 1.061405429)))
    )
    tail = 0.5 * series * bell
    share = jnp.where(value < 0.0, tail, 1.0 - tail)
    return value * share, share + value * bell * (1.0 / math.sqrt(2.0 * math.pi))


def remote(src, dst, send, recv, device):
    return pltpu.make_async_remote_copy(
        src_ref=src, dst_ref=dst, send_sem=send, recv_sem=recv, device_id=device, device_id_type=MESH
    )


def block_kernel(
    chips, images,
    index_ref, valid_ref,
    tokens_ref, cotangent_ref, queue_ref, norms_ref, attn_own, mlp_own,
    out_ref, input_grad_ref, done, norm_out,
    attn_ref, mlp_ref,
    asked, parts_out, given, far_f,
    wide, tokens_f, normed, normal_one, scale_one, query, key, value, probs, mixed,
    middle, normal_two, scale_two, normed_two, cot_low, made,
    mlp_mine, mlp_away, square, both_out, both_grad,
    total, first_send, first_recv, sent, recv, norm_sum, norm_pair, norm_slots,
    ask_send, ask_recv, give_send, give_recv, swap_send, swap_recv,
    first_s, first_r, step_s, step_r, spread_s, spread_r, norm_s, norm_r, join_s, join_r,
):
    me = lax.axis_index("dp")
    core = lax.axis_index("mp")
    other = 1 - core
    count = tokens_ref.shape[0]
    width = tokens_ref.shape[1]
    depth = queue_ref.shape[0]
    picks = images * NBR
    pairs = width // (2 * HEAD)
    bits = chips.bit_length() - 1
    height = done.shape[1]
    grad_two = tokens_f
    grad_query, grad_key, grad_value, grad_mid_low = query, key, value, normed_two

    barrier = pltpu.get_barrier_semaphore()
    pl.semaphore_signal(barrier, inc=1, device_id=(me, other), device_id_type=MESH)

    def greet(hop, carry):
        pl.semaphore_signal(
            barrier, inc=1, device_id=(lax.rem(me + hop, chips), core), device_id_type=MESH
        )
        return carry

    lax.fori_loop(1, chips, greet, 0)
    pick_row = lax.broadcasted_iota(jnp.int32, (picks, depth), 0)
    wanted = jnp.zeros((picks, depth), jnp.int32)
    for pick in range(picks):
        wanted = jnp.where(
            pick_row == pick, index_ref[core * images + pick // NBR, pick % NBR], wanted
        )
    asked[0] = wanted
    attn_ref[:, core] = attn_own[...].astype(BF)
    mlp_ref[:, core] = mlp_own[...].astype(BF)
    pl.semaphore_wait(barrier, chips)

    def ask(hop):
        return remote(
            asked.at[0], asked.at[hop], ask_send.at[hop], ask_recv.at[hop],
            (lax.rem(me + hop, chips), core),
        )

    def give(hop):
        return remote(
            parts_out.at[hop], given.at[hop], give_send.at[hop], give_recv.at[hop],
            (lax.rem(me + chips - hop, chips), core),
        )

    def start_ask(hop, carry):
        ask(hop).start()
        return carry

    lax.fori_loop(1, chips, start_ask, 0)
    swaps = [
        remote(ref.at[:, core], ref.at[:, core], swap_send.at[place], swap_recv.at[place], (me, other))
        for place, ref in enumerate((attn_ref, mlp_ref))
    ]
    for swap in swaps:
        swap.start()

    def spread(source, target):
        for which in range(count // (images * P_SIZE)):

            @pl.when(core == which)
            def _(which=which):
                for image in range(images):
                    start = (which * images + image) * P_SIZE
                    target[image * ROWS:(image + 1) * ROWS, :] = source[start:start + ROWS, :]

    wide[:count, :] = tokens_ref[...].astype(F32)
    wide[count:, :] = jnp.zeros((wide.shape[0] - count, width), F32)
    spread(wide, tokens_f)

    places = lax.broadcasted_iota(jnp.int32, (picks, depth), 1) + me * depth

    def choose(wish):
        chooser = jnp.where(wish == places, 1.0, 0.0).astype(BF)
        return dot_nn(chooser, queue_ref[...]).astype(BF)

    def answer(hop, carry):
        ask(hop).wait_recv()
        parts_out[hop] = choose(asked[hop])
        give(hop).start()
        return carry

    lax.fori_loop(1, chips, answer, 0)
    given[0] = choose(wanted)
    wide[:count, :] = cotangent_ref[...].astype(F32)
    spread(wide, made)
    own_row = lax.broadcasted_iota(jnp.int32, (ROWS, 1), 0) < P_SIZE
    lane = lax.broadcasted_iota(jnp.int32, (1, 2 * HEAD), 1)
    first_head = lane < HEAD
    key_lane = lax.broadcasted_iota(jnp.int32, (1, ROWS), 1)

    def halves(pair):
        zero = jnp.zeros_like(pair)
        return jnp.where(first_head, pair, zero), jnp.where(first_head, zero, pair)

    def place_of(image):
        return pl.ds(pl.multiple_of(image * ROWS, ROWS), ROWS)

    def step_norm(image, carry):
        here = place_of(image)
        cot_low[here, :] = jnp.where(own_row, made[here, :], 0.0).astype(BF)
        normed_f, normal, scale = layer_norm(tokens_f[here, :], norms_ref[0:1, :], norms_ref[1:2, :])
        normal_one[here, :] = normal
        scale_one[here, :] = scale
        made[here, :] = jnp.where(own_row, normed_f, 0.0)
        return carry

    lax.fori_loop(0, images, step_norm, 0)

    def collect(hop, sums):
        give(hop).wait_recv()
        return sums + given[hop].astype(F32)

    far_f[...] = lax.fori_loop(1, chips, collect, given[0].astype(F32))
    for swap in swaps:
        swap.wait_recv()

    def weight(slot):
        return attn_ref[slot].reshape(width, width)

    def step_forward(image, carry):
        here = place_of(image)
        x = tokens_f[here, :]
        far = far_f[pl.ds(pl.multiple_of(image * NBR, NBR), NBR), :]
        full = jnp.concatenate([made[here, :][:FAR, :], far], axis=0).astype(BF)
        normed[here, :] = full
        q = dot_nt(full, weight(0)).astype(BF)
        k = dot_nt(full, weight(1)).astype(BF)
        v = dot_nt(full, weight(2)).astype(BF)
        query[here, :] = q
        key[here, :] = k
        value[here, :] = v
        bias = jnp.where(key_lane < P_SIZE, 0.0, -1e30)
        for slot in range(NBR):
            okay = valid_ref[core * images + image, slot] > 0
            bias = jnp.where(key_lane == FAR + slot, jnp.where(okay, 0.0, -1e30), bias)
        parts = []
        for pair in range(pairs):
            cols = slice(pair * 2 * HEAD, (pair + 1) * 2 * HEAD)
            k_pair = k[:, cols]
            sums = 0.0
            for head, (q_one, v_one) in enumerate(zip(halves(q[:, cols]), halves(v[:, cols]))):
                scores = dot_nt(q_one, k_pair) * 0.125 + bias
                top = jnp.max(scores, axis=-1, keepdims=True)
                powers = jnp.exp(scores - top)
                prob = powers / jnp.sum(powers, axis=-1, keepdims=True)
                probs[image * 2 * pairs + 2 * pair + head] = prob
                sums = sums + dot_nn(prob.astype(BF), v_one)
            parts.append(sums.astype(BF))
        mix = jnp.concatenate(parts, axis=1)
        mixed[here, :] = mix
        mid = x + dot_nn(mix, weight(3))
        middle[here, :] = mid
        two_f, normal, scale = layer_norm(mid, norms_ref[2:3, :], norms_ref[3:4, :])
        normal_two[here, :] = normal
        scale_two[here, :] = scale
        normed_two[here, :] = two_f.astype(BF)
        return carry

    lax.fori_loop(0, images, step_forward, 0)

    made[...] = jnp.zeros_like(made)
    grad_two[...] = jnp.zeros_like(grad_two)
    chunks = mlp_ref.shape[3] // CHUNK

    def step_mlp(half, target):
        def step(turn, carry):
            cols = pl.ds(pl.multiple_of(turn * CHUNK, CHUNK), CHUNK)
            w_one = mlp_ref[0, half, :, cols]
            w_two = mlp_ref[1, half, :, cols]
            two = normed_two[...]
            cot = cot_low[...]
            hidden, slope = gelu_pair(dot_nn(two, w_one))
            hidden = hidden.astype(BF)
            grad_inner = (dot_nn(cot, w_two) * slope).astype(BF)
            made[...] += dot_nt(hidden, w_two)
            grad_two[...] += dot_nt(grad_inner, w_one)
            target[0, :, cols] = dot_tn(two, grad_inner).astype(target.dtype)
            target[1, :, cols] = dot_tn(cot, hidden).astype(target.dtype)
            return carry

        lax.fori_loop(0, chunks, step, 0)

    lo = me % RADIX
    hi = me // RADIX % RADIX
    peers = (lambda hop: me - lo + (lo + hop) % RADIX, lambda hop: me - RADIX * hi + RADIX * ((hi + hop) % RADIX))
    digits = (lo, hi)
    plan = ((0, 1), (1, 0), (0, 1))
    quarter, shard = height // RADIX, height // RADIX**2
    extra = list(range(4, bits))
    pending = []
    waits = [[] for unused in range(PARTS)]

    def send(part, src, dst, pair, device):
        copy = remote(src, dst, pair[0], pair[1], device)
        copy.start()
        pending.append(copy)
        waits[part].append(copy)

    def arrived(part):
        for copy in waits[part]:
            copy.wait_recv()
        waits[part].clear()

    def rows(start, size):
        return pl.ds(pl.multiple_of(start, 16), size)

    def copy_blocks(target, source, part):
        tall = source.shape[1]
        for block in range(source.shape[2] // width):
            target[part, block * tall:(block + 1) * tall, :] = source[
                part, :, block * width:(block + 1) * width
            ]

    def begin(part):
        send(part, first_send.at[part], first_recv.at[part], (first_s.at[part], first_r.at[part]), (me, other))

    def reduce_one(part):
        arrived(part)
        axis = plan[part][0]
        for hop in range(1, RADIX):
            away = rows((digits[axis] + hop) % RADIX * quarter, quarter)
            slot = pl.ds((hop - 1) * quarter, quarter)
            sent[part, slot, :] = (total[part, away, :] + first_recv[part, away, :].astype(F32)).astype(BF)
            send(
                part, sent.at[part, slot], recv.at[part, slot],
                (step_s.at[part, hop - 1], step_r.at[part, hop - 1]), (peers[axis](hop), core),
            )
        held = rows(digits[axis] * quarter, quarter)
        total[part, held, :] += first_recv[part, held, :].astype(F32)

    def reduce_two(part):
        arrived(part)
        first, second = plan[part]
        start = digits[first] * quarter

        def summed(at, size):
            sums = total[part, rows(start + at, size), :]
            for hop in range(1, RADIX):
                sums = sums + recv[part, rows((hop - 1) * quarter + at, size), :].astype(F32)
            return sums

        base = (RADIX - 1) * quarter
        for hop in range(1, RADIX):
            slot = pl.ds(base + (hop - 1) * shard, shard)
            sent[part, slot, :] = summed((digits[second] + hop) % RADIX * shard, shard).astype(BF)
            send(
                part, sent.at[part, slot], recv.at[part, slot],
                (step_s.at[part, RADIX - 2 + hop], step_r.at[part, RADIX - 2 + hop]),
                (peers[second](hop), core),
            )
        at = digits[second] * shard
        total[part, rows(start + at, shard), :] = summed(at, shard)

    def spread_one(part):
        arrived(part)
        first, second = plan[part]
        start = digits[first] * quarter + digits[second] * shard
        held = rows(start, shard)
        sums = total[part, held, :]
        base = (RADIX - 1) * quarter
        for hop in range(1, RADIX):
            sums = sums + recv[part, pl.ds(base + (hop - 1) * shard, shard), :].astype(F32)
        base = base + (RADIX - 1) * shard
        for turn, bit in enumerate(extra):
            slot = pl.ds(base + turn * shard, shard)
            sent[part, slot, :] = sums.astype(BF)
            mate = me + (1 - 2 * (me // 2**bit % 2)) * 2**bit
            at = 2 * (RADIX - 1) + turn
            send(part, sent.at[part, slot], recv.at[part, slot], (step_s.at[part, at], step_r.at[part, at]), (mate, core))
            arrived(part)
            sums = sent[part, slot, :].astype(F32) + recv[part, slot, :].astype(F32)
        done[part, held, :] = sums.astype(BF)
        for hop in range(1, RADIX):
            send(
                part, done.at[part, held], done.at[part, held],
                (spread_s.at[part, hop - 1], spread_r.at[part, hop - 1]), (peers[second](hop), core),
            )

    def spread_two(part):
        arrived(part)
        axis = plan[part][0]
        held = rows(digits[axis] * quarter, quarter)
        for hop in range(1, RADIX):
            send(
                part, done.at[part, held], done.at[part, held],
                (spread_s.at[part, RADIX - 2 + hop], spread_r.at[part, RADIX - 2 + hop]),
                (peers[axis](hop), core),
            )

    step_mlp(other, mlp_away)
    for part in range(2):
        copy_blocks(first_send, mlp_away, part)
        begin(part)
    step_mlp(core, mlp_mine)
    for part in range(2):
        copy_blocks(total, mlp_mine, part)
        reduce_one(part)

    norm_sum[...] = jnp.zeros_like(norm_sum)

    def step_backward(image, carry):
        here = place_of(image)
        made[here, :] += middle[here, :]
        both_out[core, here, :] = made[here, :].astype(BF)
        grad_n = grad_two[here, :]
        normal = normal_two[here, :]
        norm_sum[2:3, :] += jnp.sum(grad_n * normal, axis=0, keepdims=True)
        norm_sum[3:4, :] += jnp.sum(grad_n, axis=0, keepdims=True)
        grad_mid = cot_low[here, :].astype(F32) + norm_back(
            grad_n, normal, scale_two[here, :], norms_ref[2:3, :]
        )
        low = grad_mid.astype(BF)
        grad_mid_low[here, :] = low
        grad_mix = dot_nt(low, weight(3)).astype(BF)
        q = query[here, :]
        k = key[here, :]
        v = value[here, :]
        parts_q, parts_k, parts_v = [], [], []
        for pair in range(pairs):
            cols = slice(pair * 2 * HEAD, (pair + 1) * 2 * HEAD)
            gm_pair = grad_mix[:, cols]
            sum_q = sum_k = sum_v = 0.0
            for head, (q_one, k_one, v_one, gm_one) in enumerate(
                zip(halves(q[:, cols]), halves(k[:, cols]), halves(v[:, cols]), halves(gm_pair))
            ):
                prob = probs[image * 2 * pairs + 2 * pair + head]
                grad_prob = dot_nt(gm_pair, v_one)
                sum_v = sum_v + dot_tn(prob.astype(BF), gm_one)
                weighed = prob * grad_prob
                grad_score = (
                    weighed - prob * jnp.sum(weighed, axis=-1, keepdims=True)
                ).astype(BF)
                sum_q = sum_q + dot_nn(grad_score, k_one)
                sum_k = sum_k + dot_tn(grad_score, q_one)
            parts_q.append((sum_q * 0.125).astype(BF))
            parts_k.append((sum_k * 0.125).astype(BF))
            parts_v.append(sum_v.astype(BF))
        gq = jnp.concatenate(parts_q, axis=1)
        gk = jnp.concatenate(parts_k, axis=1)
        gv = jnp.concatenate(parts_v, axis=1)
        grad_query[here, :] = gq
        grad_key[here, :] = gk
        grad_value[here, :] = gv
        grad_n = dot_nn(gq, weight(0)) + dot_nn(gk, weight(1)) + dot_nn(gv, weight(2))
        grad_n = jnp.where(own_row, grad_n, 0.0)
        normal = normal_one[here, :]
        norm_sum[0:1, :] += jnp.sum(grad_n * normal, axis=0, keepdims=True)
        norm_sum[1:2, :] += jnp.sum(grad_n, axis=0, keepdims=True)
        both_grad[core, here, :] = grad_mid + norm_back(
            grad_n, normal, scale_one[here, :], norms_ref[0:1, :]
        )
        return carry

    lax.fori_loop(0, images // 2, step_backward, 0)
    for part in range(2):
        reduce_two(part)
    lax.fori_loop(images // 2, images, step_backward, 0)

    def norm_send(src, dst, place, device):
        copy = remote(src, dst, norm_s.at[place], norm_r.at[place], device)
        copy.start()
        pending.append(copy)
        return copy

    norm_pair[core] = norm_sum[...]
    norm_wait = [norm_send(norm_pair.at[core], norm_pair.at[core], 0, (me, other))]
    joins = [
        remote(ref.at[core], ref.at[core], join_s.at[place], join_r.at[place], (me, other))
        for place, ref in enumerate((both_out, both_grad))
    ]
    for join in joins:
        join.start()

    tall = attn_own.shape[1]
    for slot, (left, right) in enumerate(
        ((grad_query, normed), (grad_key, normed), (grad_value, normed), (mixed, grad_mid_low))
    ):
        square[...] = dot_tn(left[...], right[...])
        place = pl.ds(slot * tall, tall)
        first_send[2, place, :] = square[rows(other * tall, tall), :].astype(BF)
        total[2, place, :] = square[rows(core * tall, tall), :]
    begin(2)
    for part in range(2):
        spread_one(part)
    reduce_one(2)

    norm_wait[0].wait_recv()
    norm_sum[...] = norm_pair[0] + norm_pair[1]
    norm_slots[0, lo] = norm_sum[...]
    norm_wait = [
        norm_send(norm_slots.at[0, lo], norm_slots.at[0, lo], hop, (peers[0](hop), core))
        for hop in range(1, RADIX)
    ]
    for part in range(2):
        spread_two(part)
    reduce_two(2)

    for one in norm_wait:
        one.wait_recv()
    norm_sum[...] = (norm_slots[0, 0] + norm_slots[0, 1]) + (norm_slots[0, 2] + norm_slots[0, 3])
    norm_slots[1, hi] = norm_sum[...]
    norm_wait = [
        norm_send(norm_slots.at[1, hi], norm_slots.at[1, hi], RADIX - 1 + hop, (peers[1](hop), core))
        for hop in range(1, RADIX)
    ]
    spread_one(2)

    for join in joins:
        join.wait_recv()
    wide[...] = jnp.zeros_like(wide)
    for image in range(count // P_SIZE):
        which, at = image // images, image % images * ROWS
        span = slice(image * P_SIZE, (image + 1) * P_SIZE)
        wide[span, :] = both_out[which, at:at + ROWS, :].astype(F32)[:P_SIZE, :]
        input_grad_ref[span, :] = both_grad[which, at:at + P_SIZE, :]
    out_ref[...] = wide[:count, :].astype(BF)

    for one in norm_wait:
        one.wait_recv()
    norm_sum[...] = (norm_slots[1, 0] + norm_slots[1, 1]) + (norm_slots[1, 2] + norm_slots[1, 3])
    for turn, bit in enumerate(extra):
        mate = me + (1 - 2 * (me // 2**bit % 2)) * 2**bit
        norm_slots[2 + turn, 0] = norm_sum[...]
        norm_send(norm_slots.at[2 + turn, 0], norm_slots.at[2 + turn, 1], 2 * RADIX - 1 + turn, (mate, core)).wait_recv()
        norm_sum[...] = norm_slots[2 + turn, 0] + norm_slots[2 + turn, 1]
    norm_out[...] = norm_sum[...]

    spread_two(2)
    for part in range(PARTS):
        arrived(part)
    for one in pending + joins + swaps:
        one.wait_send()

    def finish(hop, carry):
        ask(hop).wait_send()
        give(hop).wait_send()
        return carry

    lax.fori_loop(1, chips, finish, 0)


def block(chips, nbr_index, nbr_valid, tokens, cotangent, queue, norms, attn, mlp):
    count, width = tokens.shape
    cores = width // attn.shape[1]
    images = nbr_valid.shape[0] // cores
    tall = images * ROWS
    padded = count + 16 - count % 8
    heads = width // HEAD
    picks = images * NBR
    bits = chips.bit_length() - 1
    extra = max(0, bits - 4)
    height = attn.shape[0] * attn.shape[1]
    quarter, shard = height // RADIX, height // RADIX**2
    moving = (RADIX - 1) * (quarter + shard) + extra * shard
    vmem = pl.BlockSpec(memory_space=pltpu.VMEM)
    smem = pl.BlockSpec(memory_space=pltpu.SMEM)
    dma = pltpu.SemaphoreType.DMA
    flat_f = pltpu.VMEM((tall, width), F32)
    flat_low = pltpu.VMEM((tall, width), BF)
    column = pltpu.VMEM((tall, 1), F32)
    steps = 2 * (RADIX - 1)
    return pl.pallas_call(
        functools.partial(block_kernel, chips, images),
        in_specs=[smem] * 2 + [vmem] * 6,
        out_specs=[vmem] * 4,
        out_shape=[
            jax.ShapeDtypeStruct((count, width), BF),
            jax.ShapeDtypeStruct((count, width), F32),
            jax.ShapeDtypeStruct((PARTS, height, width), BF),
            jax.ShapeDtypeStruct(norms.shape, F32),
        ],
        scratch_shapes=[
            pltpu.VMEM((attn.shape[0], cores) + attn.shape[1:], BF),
            pltpu.VMEM((mlp.shape[0], cores) + mlp.shape[1:], BF),
            pltpu.VMEM((chips, picks, queue.shape[0]), jnp.int32),
            pltpu.VMEM((chips, picks, width), BF),
            pltpu.VMEM((chips, picks, width), BF),
            pltpu.VMEM((picks, width), F32),
            pltpu.VMEM((padded, width), F32),
            flat_f, flat_low, flat_f, column, flat_low, flat_low, flat_low,
            pltpu.VMEM((images * heads, ROWS, ROWS), F32),
            flat_low,
            flat_f, flat_f, column, flat_low, flat_low, flat_f,
            pltpu.VMEM(mlp.shape, F32),
            pltpu.VMEM(mlp.shape, BF),
            pltpu.VMEM((width, width), F32),
            pltpu.VMEM((cores, tall, width), BF),
            pltpu.VMEM((cores, tall, width), F32),
            pltpu.VMEM((PARTS, height, width), F32),
            pltpu.VMEM((PARTS, height, width), BF),
            pltpu.VMEM((PARTS, height, width), BF),
            pltpu.VMEM((PARTS, moving, width), BF),
            pltpu.VMEM((PARTS, moving, width), BF),
            pltpu.VMEM(norms.shape, F32),
            pltpu.VMEM((cores,) + norms.shape, F32),
            pltpu.VMEM((2 + extra, RADIX) + norms.shape, F32),
            dma((chips,)), dma((chips,)), dma((chips,)), dma((chips,)),
            dma((2,)), dma((2,)),
            dma((PARTS,)), dma((PARTS,)),
            dma((PARTS, steps + extra)), dma((PARTS, steps + extra)),
            dma((PARTS, steps)), dma((PARTS, steps)),
            dma((steps + 1 + extra,)), dma((steps + 1 + extra,)),
            dma((2,)), dma((2,)),
        ],
        compiler_params=pltpu.CompilerParams(
            collective_id=0, has_side_effects=True, vmem_limit_bytes=62 * 1024 * 1024
        ),
        name="block_both_ways",
    )(nbr_index, nbr_valid, tokens, cotangent, queue, norms, attn, mlp)


RATE_NORM = 0.6


def body(
    chips,
    tokens,
    cotangent,
    queue,
    nbr_index,
    nbr_valid,
    norm_params,
    norm_first,
    norm_second,
    attn_weight,
    mlp_weight,
    attn_first,
    attn_second,
    mlp_first,
    mlp_second,
    attn_left,
    attn_right,
    mlp_left,
    mlp_right,
):
    def flip(value):
        return value.transpose(0, 2, 1)

    attn_own = flip(attn_weight)
    block_out, input_grad, summed, norm_grad = block(
        chips, nbr_index, nbr_valid, tokens, cotangent, queue, norm_params, attn_own, mlp_weight
    )
    norm_first_new = BETA_FIRST * norm_first + (1.0 - BETA_FIRST) * norm_grad
    norm_second_new = BETA_SECOND * norm_second + (1.0 - BETA_SECOND) * norm_grad * norm_grad
    norm_new = norm_params - RATE_NORM * (norm_first_new / (1.0 - BETA_FIRST**STEP)) / (
        jnp.sqrt(norm_second_new / (1.0 - BETA_SECOND**STEP)) + EPSILON
    )
    slots, rows, width = attn_own.shape
    (
        mlp_grad,
        mlp_new,
        mlp_copy,
        mlp_first_new,
        mlp_second_new,
        mlp_left_new,
        mlp_right_new,
    ) = update_stack(
        summed, 0, 1, mlp_weight, mlp_first, mlp_second, mlp_left, mlp_right
    )
    (
        attn_grad,
        attn_new,
        attn_copy,
        attn_first_new,
        attn_second_new,
        attn_right_new,
        attn_left_new,
    ) = update_stack(
        summed.reshape(-1, rows, width),
        2 * slots,
        2,
        attn_own,
        flip(attn_first),
        flip(attn_second),
        attn_right,
        attn_left,
    )
    return (
        block_out,
        input_grad,
        norm_grad,
        flip(attn_grad),
        mlp_grad,
        norm_first_new,
        norm_second_new,
        norm_new,
        flip(attn_first_new),
        flip(attn_second_new),
        mlp_first_new,
        mlp_second_new,
        attn_left_new,
        attn_right_new,
        mlp_left_new,
        mlp_right_new,
        flip(attn_new),
        flip(attn_copy),
        mlp_new,
        mlp_copy,
    )


def solution(mesh):
    return jax.shard_map(
        functools.partial(body, mesh.shape["dp"]),
        mesh=mesh,
        in_specs=(
            P("dp", None),
            P("dp", None),
            P("dp", None),
            P("dp", None),
            P("dp", None),
            P(),
            P(),
            P(),
            P(None, None, "mp"),
            P(None, None, "mp"),
            P(None, None, "mp"),
            P(None, None, "mp"),
            P(None, None, "mp"),
            P(None, None, "mp"),
            P(None, "mp", None),
            P(None, "mp", None),
            P(None, "mp", None),
            P(None, "mp", None),
        ),
        out_specs=(
            P("dp", None),
            P("dp", None),
            P(),
            P(None, None, "mp"),
            P(None, None, "mp"),
            P(),
            P(),
            P(),
            P(None, None, "mp"),
            P(None, None, "mp"),
            P(None, None, "mp"),
            P(None, None, "mp"),
            P(None, "mp", None),
            P(None, "mp", None),
            P(None, "mp", None),
            P(None, "mp", None),
            P(None, None, "mp"),
            P(None, None, "mp"),
            P(None, None, "mp"),
            P(None, None, "mp"),
        ),
        check_vma=False,
    )
```

```python
import functools
import math

import jax
import jax.numpy as jnp
from jax import lax
from jax.experimental import pallas as pl
from jax.experimental.pallas import tpu as pltpu
from jax.sharding import PartitionSpec as P

BETA_FIRST = 0.9
BETA_SECOND = 0.95
EPSILON = 1e-08
RATE_MATRIX = 0.15
DECAY_RATE = 0.05
TURN_RATE = 4.0
STEP = 10
BLOCK = 256
ROUNDS = 3
NEAR = 0.01
PIECE = 128
PAUSES = 40

BF = jnp.bfloat16
F32 = jnp.float32


def dot_nn(a, b):
    return lax.dot_general(a, b, (((1,), (0,)), ((), ())), preferred_element_type=F32)


def dot_nt(a, b):
    return lax.dot_general(a, b, (((1,), (1,)), ((), ())), preferred_element_type=F32)


def dot_tn(a, b):
    return lax.dot_general(a, b, (((0,), (0,)), ((), ())), preferred_element_type=F32)


def split(a):
    high = a.astype(BF)
    return high, (a - high.astype(F32)).astype(BF)


def three(dot, a, b):
    return dot(a[0], b[0]) + (dot(a[0], b[1]) + dot(a[1], b[0]))


def below(size):
    row = lax.broadcasted_iota(jnp.int32, (size, size), 0)
    col = lax.broadcasted_iota(jnp.int32, (size, size), 1)
    return row > col, row == col


def in_step(chains):
    chains = list(chains)
    while chains:
        kept = []
        for chain in chains:
            try:
                next(chain)
                kept.append(chain)
            except StopIteration:
                pass
        chains = kept


def renew_chain(base_ref, out_ref, rest_ref, misses):
    width = base_ref.shape[1]
    source = base_ref
    for at in range(0, width, BLOCK):
        size = min(BLOCK, width - at)
        lower, same = below(size)
        eye = jnp.where(same, 1.0, 0.0)
        low = source[:, at:at + size].astype(BF)
        gram = dot_tn(low, low)
        yield
        on_diag = jnp.where(same, gram, 0.0)
        s_col = lax.rsqrt(jnp.maximum(jnp.sum(on_diag, axis=1, keepdims=True), 1e-30))
        s_row = lax.rsqrt(jnp.maximum(jnp.sum(on_diag, axis=0, keepdims=True), 1e-30))
        state = gram * s_col * s_row
        made = jnp.where(same, s_col, 0.0).astype(BF)
        for turn in range(ROUNDS):
            under = jnp.where(lower, state, 0.0)
            moved = dot_nn(under.astype(BF), state.astype(BF))
            mass = jnp.sum(under * under, axis=1, keepdims=True)
            yield
            curve = jnp.sum(moved * under, axis=1, keepdims=True)
            pace = jnp.where(curve > mass, mass / jnp.maximum(curve, 1e-30), 1.0)
            left = 1.0 - 2.0 * pace * mass + pace * pace * curve
            scale = lax.rsqrt(jnp.maximum(left, 1e-6))
            step = (scale * (eye - pace * under)).astype(BF)
            if turn + 1 < ROUNDS:
                state = dot_nt((scale * (state - pace * moved)).astype(BF), step)
            made = dot_nn(step, made).astype(BF)
            yield
        high, low = split(source[:, at:at + size])
        block = dot_nt(high, made) + dot_nt(low, made)
        yield
        pair = split(block)
        gram = three(dot_tn, pair, pair)
        yield
        off = jnp.where(lower, gram, 0.0) + jnp.where(same, 0.5 * (gram - 1.0), 0.0)
        misses.append(jnp.sum(off * off) * (1.0 / size))
        block = block - dot_nt(pair[0], off.astype(BF))
        out_ref[:, at:at + size] = block
        yield
        if at + size < width:
            pair = split(block)
            rest = source[:, at + size:]
            shared = split(three(dot_tn, pair, split(rest)))
            yield
            rest_ref[:, at + size:] = rest - three(dot_nn, pair, shared)
            source = rest_ref
            yield


def renew_rows(base_ref, out_ref, work_ref):
    size = base_ref.shape[0]
    group = 64
    work_ref[...] = base_ref[...].T

    def take(turn, carry):
        row = work_ref[pl.ds(turn, 1), :]
        row = row * lax.rsqrt(jnp.sum(row * row, axis=1, keepdims=True))
        work_ref[pl.ds(turn, 1), :] = row

        def clear(which, inner):
            here = pl.ds(pl.multiple_of(which * group, group), group)
            rows = work_ref[here, :]
            later = lax.broadcasted_iota(jnp.int32, (group, 1), 0) + which * group > turn
            share = jnp.where(later, jnp.sum(rows * row, axis=1, keepdims=True), 0.0)
            work_ref[here, :] = rows - share * row
            return inner

        return lax.fori_loop(turn // group, size // group, clear, carry)

    lax.fori_loop(0, size, take, 0)
    out_ref[...] = work_ref[...].T


def move_chain(grad, left_pair, right_pair, weight_ref, first_ref, second_ref, new_ref, copy_ref, first_new_ref, second_new_ref, move_ref):
    rows = grad.shape[0]
    for at in range(0, rows, PIECE):
        size = min(PIECE, rows - at)
        part = slice(at, at + size)
        half = dot_tn(left_pair[0][:, part], grad) + dot_tn(left_pair[1][:, part], grad)
        yield
        turned = three(dot_nn, split(half), right_pair)
        yield
        first_new = BETA_FIRST * first_ref[part, :] + (1.0 - BETA_FIRST) * turned
        second_new = BETA_SECOND * second_ref[part, :] + (1.0 - BETA_SECOND) * turned * turned
        first_new_ref[part, :] = first_new
        second_new_ref[part, :] = second_new
        move_ref[part, :] = (
            first_new
            / (1.0 - BETA_FIRST**STEP)
            / (jnp.sqrt(second_new / (1.0 - BETA_SECOND**STEP)) + EPSILON)
        ).astype(BF)
        yield
    for at in range(0, rows, PIECE):
        part = slice(at, min(at + PIECE, rows))
        back = dot_nn(left_pair[0][part, :], move_ref[...]).astype(BF)
        yield
        new = weight_ref[part, :] * (1.0 - RATE_MATRIX * DECAY_RATE) - RATE_MATRIX * dot_nt(back, right_pair[0])
        new_ref[part, :] = new
        copy_ref[part, :] = new.astype(BF)
        yield


RATE_NORM = 0.6


MESH = pl.DeviceIdType.MESH
RADIX = 4


def remote(src, dst, send, recv, device):
    return pltpu.make_async_remote_copy(
        src_ref=src, dst_ref=dst, send_sem=send, recv_sem=recv, device_id=device, device_id_type=MESH
    )


def set_bases(grad, left, right, left_low, right_low, left_base, right_base):
    gram = dot_nt(grad, grad)
    pace = TURN_RATE / (jnp.sqrt(jnp.sum(gram * gram)) + 1e-06)
    left_base[...] = left + dot_nn(gram.astype(BF), left_low) * pace
    right_base[...] = right + dot_tn(grad, dot_nn(grad, right_low).astype(BF)) * pace


def side_by_side(grad, height):
    return jnp.concatenate([grad[at:at + height] for at in range(0, grad.shape[0], height)], axis=1)


def spread_chain(chips, partial_ref, attn_grad, sent, recv, sems):
    me = lax.axis_index("dp")
    core = lax.axis_index("mp")
    count = RADIX**2
    seat = me % count
    shard = partial_ref.shape[0]
    spread_s, spread_r, extra_s, extra_r = sems
    extra = list(range(4, chips.bit_length() - 1))
    held = pl.ds(pl.multiple_of((seat % RADIX * RADIX + seat // RADIX) * shard, 16), shard)

    def peer(hop):
        return (me - seat + (seat + hop) % count, core)

    def mate(bit):
        return (me + (1 - 2 * (me // 2**bit % 2)) * 2**bit, core)

    def spread(hop):
        return remote(attn_grad.at[held], attn_grad.at[held], spread_s.at[hop], spread_r.at[hop], peer(hop))

    barrier = pltpu.get_barrier_semaphore()

    def greet(hop, carry):
        pl.semaphore_signal(barrier, inc=1, device_id=peer(hop), device_id_type=MESH)
        return carry

    lax.fori_loop(1, count, greet, 0)
    for bit in extra:
        pl.semaphore_signal(barrier, inc=1, device_id=mate(bit), device_id_type=MESH)
    yield
    pl.semaphore_wait(barrier, count - 1 + len(extra))
    sums = partial_ref[...]
    for turn, bit in enumerate(extra):
        sent[turn] = sums.astype(BF)
        copy = remote(sent.at[turn], recv.at[turn], extra_s.at[turn], extra_r.at[turn], mate(bit))
        copy.start()
        copy.wait()
        sums = sent[turn].astype(F32) + recv[turn].astype(F32)
    attn_grad[held, :] = sums.astype(BF)

    def start(hop, carry):
        spread(hop).start()
        return carry

    lax.fori_loop(1, count, start, 0)
    for unused in range(PAUSES):
        yield

    def finish(hop, carry):
        spread(hop).wait()
        return carry

    lax.fori_loop(1, count, finish, 0)


def turn_mlp_kernel(
    chips, grad_ref, left_ref, right_ref, partial_ref,
    left_new_ref, right_new_ref, miss_ref, attn_grad,
    left_base, right_base, left_rest, right_rest, sent, recv, *sems,
):
    slots, rows = left_ref.shape[:2]
    chains = [spread_chain(chips, partial_ref, attn_grad, sent, recv, sems)]
    next(chains[0])
    misses = []
    for which in range(slots):
        grad = side_by_side(grad_ref[which], rows)
        left = left_ref[which]
        right = right_ref[which]
        set_bases(grad, left, right, left.astype(BF), right.astype(BF), left_base.at[which], right_base.at[which])
        misses.append(([], []))
        for side, (base, out, rest) in enumerate(
            ((left_base, left_new_ref, left_rest), (right_base, right_new_ref, right_rest))
        ):
            chains.append(renew_chain(base.at[which], out.at[which], rest.at[which], misses[which][side]))
    in_step(chains)
    for which in range(slots):
        for side in range(2):
            miss_ref[which, side] = functools.reduce(jnp.maximum, misses[which][side])


def turn_mlp(chips, grad, left, right, partial):
    extra = max(0, chips.bit_length() - 1 - 4)
    shard, width = partial.shape
    vmem = pl.BlockSpec(memory_space=pltpu.VMEM)
    like = jax.ShapeDtypeStruct
    moving = pltpu.VMEM((max(1, extra), shard, width), BF)
    peer_sems = pltpu.SemaphoreType.DMA((RADIX**2,))
    extra_sems = pltpu.SemaphoreType.DMA((max(1, extra),))
    return pl.pallas_call(
        functools.partial(turn_mlp_kernel, chips),
        in_specs=[vmem] * 4,
        out_specs=[vmem, vmem, pl.BlockSpec(memory_space=pltpu.SMEM), vmem],
        out_shape=[
            like(left.shape, F32),
            like(right.shape, F32),
            like((left.shape[0], 2), F32),
            like((RADIX**2 * shard, width), BF),
        ],
        scratch_shapes=[
            pltpu.VMEM(left.shape, F32),
            pltpu.VMEM(right.shape, F32),
            pltpu.VMEM(left.shape, F32),
            pltpu.VMEM(right.shape, F32),
            moving,
            moving,
        ]
        + [peer_sems] * 2
        + [extra_sems] * 2,
        compiler_params=pltpu.CompilerParams(
            collective_id=1, has_side_effects=True, vmem_limit_bytes=60 * 1024 * 1024
        ),
        name="turn_mlp",
    )(grad, left, right, partial)


def update_kernel(
    together,
    miss_ref, mlp_grad_ref, mlp_weight_ref, mlp_first_ref, mlp_second_ref, mlp_left_ref, mlp_right_ref,
    grad_ref, weight_ref, first_ref, second_ref, left_ref, right_ref,
    norm_grad_ref, norm_ref, norm_first_ref, norm_second_ref,
    mlp_left_made, mlp_right_made, block_ref, input_grad_ref,
    mlp_grad_out, mlp_new_ref, mlp_copy_ref, mlp_first_new_ref, mlp_second_new_ref,
    grad_out_ref, new_ref, copy_ref, first_new_ref, second_new_ref, left_new_ref, right_new_ref,
    norm_grad_out, norm_new, norm_first_new, norm_second_new,
    mlp_left_out, mlp_right_out, block_out, input_grad_out,
    mlp_move, left_base, right_base, left_rest, right_rest, move_ref, left_held, right_held, work,
    block_held, input_grad_held, sems_in, sems_out,
):
    slot = pl.program_id(0)
    last = pl.num_programs(0) - 1

    def copies(passed, at):
        return (
            [pltpu.make_async_copy(src, held, sems_in.at[at + place]) for place, (src, held, dst) in enumerate(passed)],
            [pltpu.make_async_copy(held, dst, sems_out.at[at + place]) for place, (src, held, dst) in enumerate(passed)],
        )

    bases = copies(
        ((mlp_left_made.at[slot], left_held, mlp_left_out.at[slot]), (mlp_right_made.at[slot], right_held, mlp_right_out.at[slot])), 0
    )
    wide = copies(((block_ref, block_held, block_out), (input_grad_ref, input_grad_held, input_grad_out)), 2)

    @pl.when(slot == 0)
    def _():
        for copy in wide[0]:
            copy.start()
        grad = norm_grad_ref[...]
        first = BETA_FIRST * norm_first_ref[...] + (1.0 - BETA_FIRST) * grad
        second = BETA_SECOND * norm_second_ref[...] + (1.0 - BETA_SECOND) * grad * grad
        norm_grad_out[...] = grad
        norm_first_new[...] = first
        norm_second_new[...] = second
        norm_new[...] = norm_ref[...] - RATE_NORM * (first / (1.0 - BETA_FIRST**STEP)) / (
            jnp.sqrt(second / (1.0 - BETA_SECOND**STEP)) + EPSILON
        )

    for copy in bases[0]:
        copy.start()
    mlp_grad = side_by_side(mlp_grad_ref[0], mlp_weight_ref.shape[1])
    mlp_grad_out[0] = mlp_grad.astype(F32)
    chains = []
    misses = []
    for which in range(together):
        grad = grad_ref[which]
        grad_out_ref[which] = grad.astype(F32)
        left = left_ref[which]
        right = right_ref[which]
        left_pair = split(left)
        right_pair = split(right)
        set_bases(grad, left, right, left_pair[0], right_pair[0], left_base.at[which], right_base.at[which])
        misses.append(([], []))
        chains.append(renew_chain(right_base.at[which], right_new_ref.at[which], right_rest.at[which], misses[which][1]))
        chains.append(renew_chain(left_base.at[which], left_new_ref.at[which], left_rest.at[which], misses[which][0]))
        chains.append(
            move_chain(
                grad, left_pair, right_pair, weight_ref.at[which], first_ref.at[which], second_ref.at[which],
                new_ref.at[which], copy_ref.at[which], first_new_ref.at[which], second_new_ref.at[which],
                move_ref.at[which],
            )
        )
    chains.append(
        move_chain(
            mlp_grad, split(mlp_left_ref[0]), split(mlp_right_ref[0]),
            mlp_weight_ref.at[0], mlp_first_ref.at[0], mlp_second_ref.at[0],
            mlp_new_ref.at[0], mlp_copy_ref.at[0], mlp_first_new_ref.at[0], mlp_second_new_ref.at[0], mlp_move,
        )
    )
    in_step(chains)
    for copy in bases[0]:
        copy.wait()
    poor = jnp.logical_not(jnp.maximum(miss_ref[slot, 0], miss_ref[slot, 1]) < NEAR)

    @pl.when(poor)
    def _():
        left = mlp_left_ref[0]
        right = mlp_right_ref[0]
        size = left.shape[0]
        set_bases(mlp_grad, left, right, left.astype(BF), right.astype(BF), left_held, right_held)
        renew_rows(left_held, left_held, work.at[pl.ds(0, size), pl.ds(0, size)])
        renew_rows(right_held, right_held, work)

    for copy in bases[1]:
        copy.start()
    for which in range(together):
        for missed, base, out, rest in zip(
            misses[which], (left_base, right_base), (left_new_ref, right_new_ref), (left_rest, right_rest)
        ):
            worst = functools.reduce(jnp.maximum, missed)

            @pl.when(jnp.logical_not(worst < NEAR))
            def _(base=base, out=out, rest=rest):
                renew_rows(base.at[which], out.at[which], rest.at[which])

    @pl.when(slot == 0)
    def _():
        for copy in wide[0]:
            copy.wait()
        for copy in wide[1]:
            copy.start()

    @pl.when(slot == last)
    def _():
        for copy in wide[1]:
            copy.wait()

    for copy in bases[1]:
        copy.wait()


def update(miss, mlp, attn, norms, passed):
    like = jax.ShapeDtypeStruct
    slots = mlp[1].shape[0]
    together = attn[1].shape[0] // slots

    def spec(count, value):
        return pl.BlockSpec((count,) + value.shape[1:], lambda slot: (slot, 0, 0))

    def made(value):
        return [like(value.shape, F32)] * 2 + [like(value.shape, BF)] + [like(value.shape, F32)] * 2

    whole = pl.BlockSpec(norms[0].shape, lambda slot: (0, 0))
    anywhere = pl.BlockSpec(memory_space=pl.ANY)
    rows, width = attn[1].shape[1:]
    sides = [pltpu.VMEM((together, rows, rows), F32), pltpu.VMEM((together, width, width), F32)]
    held = [pltpu.VMEM(value.shape[1:], F32) for value in passed[:2]]
    return pl.pallas_call(
        functools.partial(update_kernel, together),
        grid=(slots,),
        in_specs=[pl.BlockSpec(memory_space=pltpu.SMEM)]
        + [spec(1, value) for value in mlp]
        + [spec(together, value) for value in attn]
        + [whole] * 4
        + [anywhere] * 4,
        out_specs=[spec(1, mlp[1])] * 5
        + [spec(together, attn[1])] * 5
        + [spec(together, attn[4]), spec(together, attn[5])]
        + [whole] * 4
        + [anywhere] * 4,
        out_shape=made(mlp[1])
        + made(attn[1])
        + [like(attn[4].shape, F32), like(attn[5].shape, F32)]
        + [like(norms[0].shape, F32)] * 4
        + [like(value.shape, value.dtype) for value in passed],
        scratch_shapes=[pltpu.VMEM(mlp[1].shape[1:], BF)]
        + sides * 2
        + [pltpu.VMEM((together, rows, width), BF)]
        + held
        + [held[1]]
        + [pltpu.VMEM(value.shape, value.dtype) for value in passed[2:]]
        + [pltpu.SemaphoreType.DMA((len(passed),)), pltpu.SemaphoreType.DMA((len(passed),))],
        compiler_params=pltpu.CompilerParams(vmem_limit_bytes=62 * 1024 * 1024),
        name="update",
    )(miss, *mlp, *attn, *norms, *passed)


P_SIZE = 197
NBR = 8
HEAD = 64
ROWS = 208
FAR = 200
CHUNK = 256
LANES = 128
PARTS = 3


def layer_norm(values, gain, shift):
    centre = values - jnp.mean(values, axis=-1, keepdims=True)
    scale = lax.rsqrt(jnp.mean(centre * centre, axis=-1, keepdims=True) + 1e-06)
    normal = centre * scale
    return (normal * gain + shift, normal, scale)


def norm_back(grad, normal, scale, gain):
    shaped = grad * gain
    return scale * (
        shaped
        - jnp.mean(shaped, axis=-1, keepdims=True)
        - normal * jnp.mean(shaped * normal, axis=-1, keepdims=True)
    )


def gelu_pair(value):
    size = jnp.abs(value) * (1.0 / math.sqrt(2.0))
    bell = jnp.exp(-0.5 * value * value)
    part = 1.0 / (1.0 + 0.3275911 * size)
    series = part * (
        0.254829592
        + part * (-0.284496736 + part * (1.421413741 + part * (-1.453152027 + part * 1.061405429)))
    )
    tail = 0.5 * series * bell
    share = jnp.where(value < 0.0, tail, 1.0 - tail)
    return value * share, share + value * bell * (1.0 / math.sqrt(2.0 * math.pi))


def block_kernel(
    chips, images,
    index_ref, valid_ref,
    tokens_ref, cotangent_ref, queue_ref, norms_ref, attn_own, mlp_own,
    out_ref, input_grad_ref, whole, partial, norm_out,
    attn_ref, mlp_ref,
    asked, parts_out, given, far_f, far_key, far_value,
    wide, tokens_f, normed, normal_one, scale_one, query, key, value, probs, mixed,
    middle, normal_two, scale_two, normed_two, cot_low, made,
    mlp_mine, mlp_away, square, both_out, both_grad,
    total, first_send, first_recv, sent, recv, norm_sum, norm_pair, norm_slots,
    ask_send, ask_recv, give_send, give_recv, swap_send, swap_recv,
    first_s, first_r, step_s, step_r, spread_s, spread_r, norm_s, norm_r, join_s, join_r,
):
    me = lax.axis_index("dp")
    core = lax.axis_index("mp")
    other = 1 - core
    count = tokens_ref.shape[0]
    width = tokens_ref.shape[1]
    depth = queue_ref.shape[0]
    picks = images * NBR
    group = LANES // picks
    pairs = width // (2 * HEAD)
    bits = chips.bit_length() - 1
    height = whole.shape[1]
    grad_two = tokens_f
    grad_query, grad_key, grad_value, grad_mid_low = query, key, value, normed_two

    barrier = pltpu.get_barrier_semaphore()
    pl.semaphore_signal(barrier, inc=1, device_id=(me, other), device_id_type=MESH)

    def greet(hop, carry):
        pl.semaphore_signal(
            barrier, inc=1, device_id=(lax.rem(me + hop, chips), core), device_id_type=MESH
        )
        return carry

    lax.fori_loop(1, chips, greet, 0)
    pick_lane = lax.broadcasted_iota(jnp.int32, (8, LANES), 1)
    wanted = jnp.full((8, LANES), -1, jnp.int32)
    for pick in range(picks):
        wanted = jnp.where(
            pick_lane % picks == pick, index_ref[core * images + pick // NBR, pick % NBR], wanted
        )
    asked[0] = wanted
    attn_ref[:, core] = attn_own[...].astype(BF)
    mlp_ref[:, core] = mlp_own[...].astype(BF)
    pl.semaphore_wait(barrier, chips)

    def ask(hop):
        return remote(
            asked.at[0], asked.at[hop], ask_send.at[hop], ask_recv.at[hop],
            (lax.rem(me + hop, chips), core),
        )

    def give(hop):
        return remote(
            parts_out.at[hop], given.at[hop], give_send.at[hop], give_recv.at[hop],
            (lax.rem(me + chips - hop, chips), core),
        )

    def start_ask(hop, carry):
        ask(hop).start()
        return carry

    lax.fori_loop(1, chips, start_ask, 0)
    swaps = [
        remote(ref.at[:, core], ref.at[:, core], swap_send.at[place], swap_recv.at[place], (me, other))
        for place, ref in enumerate((attn_ref, mlp_ref))
    ]
    for swap in swaps:
        swap.start()

    def spread(source, target):
        for which in range(count // (images * P_SIZE)):

            @pl.when(core == which)
            def _(which=which):
                for image in range(images):
                    start = (which * images + image) * P_SIZE
                    target[image * ROWS:(image + 1) * ROWS, :] = source[start:start + ROWS, :]

    places = lax.broadcasted_iota(jnp.int32, (depth, LANES), 0) + me * depth
    lane_group = lax.broadcasted_iota(jnp.int32, (1, LANES), 1) // picks

    def answer(turn, carry):
        wish = jnp.zeros((1, LANES), jnp.int32)
        for step in range(group):
            hop = turn * group + step

            @pl.when(hop > 0)
            def _(hop=hop):
                ask(hop).wait_recv()

            wish = jnp.where(lane_group == step, asked[hop][:1, :], wish)
        chooser = jnp.where(wish == places, 1.0, 0.0).astype(BF)
        picked = dot_tn(chooser, queue_ref[...]).astype(BF)
        parts_out[pl.ds(turn * group, group)] = picked.reshape(group, picks, width)
        for step in range(group):
            hop = turn * group + step

            @pl.when(hop > 0)
            def _(hop=hop):
                give(hop).start()

        return carry

    wide[:count, :] = tokens_ref[...].astype(F32)
    wide[count:, :] = jnp.zeros((wide.shape[0] - count, width), F32)
    spread(wide, tokens_f)
    lax.fori_loop(0, chips // group, answer, 0)
    wide[:count, :] = cotangent_ref[...].astype(F32)
    spread(wide, made)
    own_row = lax.broadcasted_iota(jnp.int32, (ROWS, 1), 0) < P_SIZE
    lane = lax.broadcasted_iota(jnp.int32, (1, 2 * HEAD), 1)
    first_head = lane < HEAD
    key_lane = lax.broadcasted_iota(jnp.int32, (1, ROWS), 1)

    def halves(pair):
        zero = jnp.zeros_like(pair)
        return jnp.where(first_head, pair, zero), jnp.where(first_head, zero, pair)

    def place_of(image):
        return pl.ds(pl.multiple_of(image * ROWS, ROWS), ROWS)

    def weight(slot):
        return attn_ref[slot].reshape(width, width)

    def step_norm(image, carry):
        here = place_of(image)
        cot_low[here, :] = jnp.where(own_row, made[here, :], 0.0).astype(BF)
        normed_f, normal, scale = layer_norm(tokens_f[here, :], norms_ref[0:1, :], norms_ref[1:2, :])
        normal_one[here, :] = normal
        scale_one[here, :] = scale
        made[here, :] = jnp.where(own_row, normed_f, 0.0)
        return carry

    lax.fori_loop(0, images, step_norm, 0)
    swaps[0].wait_recv()

    def step_own(image, carry):
        here = place_of(image)
        low = made[here, :].astype(BF)
        query[here, :] = dot_nt(low, weight(0)).astype(BF)
        middle[here, :] = dot_nt(low, weight(1))
        normal_two[here, :] = dot_nt(low, weight(2))
        return carry

    lax.fori_loop(0, images, step_own, 0)

    def collect(hop, sums):
        give(hop).wait_recv()
        return sums + given[hop].astype(F32)

    far_f[...] = lax.fori_loop(1, chips, collect, parts_out[0].astype(F32))
    far_low = far_f[...].astype(BF)
    far_key[...] = dot_nt(far_low, weight(1))
    far_value[...] = dot_nt(far_low, weight(2))

    def step_forward(image, carry):
        here = place_of(image)
        x = tokens_f[here, :]
        near = pl.ds(pl.multiple_of(image * NBR, NBR), NBR)

        def with_far(own, far):
            return jnp.concatenate([own[here, :][:FAR, :], far[near, :]], axis=0).astype(BF)

        normed[here, :] = with_far(made, far_f)
        q = query[here, :]
        k = with_far(middle, far_key)
        v = with_far(normal_two, far_value)
        key[here, :] = k
        value[here, :] = v
        bias = jnp.where(key_lane < P_SIZE, 0.0, -1e30)
        for slot in range(NBR):
            okay = valid_ref[core * images + image, slot] > 0
            bias = jnp.where(key_lane == FAR + slot, jnp.where(okay, 0.0, -1e30), bias)
        parts = []
        for pair in range(pairs):
            cols = slice(pair * 2 * HEAD, (pair + 1) * 2 * HEAD)
            k_pair = k[:, cols]
            sums = 0.0
            for head, (q_one, v_one) in enumerate(zip(halves(q[:, cols]), halves(v[:, cols]))):
                scores = dot_nt(q_one, k_pair) * 0.125 + bias
                top = jnp.max(scores, axis=-1, keepdims=True)
                powers = jnp.exp(scores - top)
                prob = powers / jnp.sum(powers, axis=-1, keepdims=True)
                probs[image * 2 * pairs + 2 * pair + head] = prob
                sums = sums + dot_nn(prob.astype(BF), v_one)
            parts.append(sums.astype(BF))
        mix = jnp.concatenate(parts, axis=1)
        mixed[here, :] = mix
        mid = x + dot_nn(mix, weight(3))
        middle[here, :] = mid
        two_f, normal, scale = layer_norm(mid, norms_ref[2:3, :], norms_ref[3:4, :])
        normal_two[here, :] = normal
        scale_two[here, :] = scale
        normed_two[here, :] = two_f.astype(BF)
        return carry

    lax.fori_loop(0, images, step_forward, 0)

    made[...] = jnp.zeros_like(made)
    grad_two[...] = jnp.zeros_like(grad_two)
    chunks = mlp_ref.shape[3] // CHUNK

    def step_mlp(half, target):
        def step(turn, carry):
            cols = pl.ds(pl.multiple_of(turn * CHUNK, CHUNK), CHUNK)
            w_one = mlp_ref[0, half, :, cols]
            w_two = mlp_ref[1, half, :, cols]
            two = normed_two[...]
            cot = cot_low[...]
            hidden, slope = gelu_pair(dot_nn(two, w_one))
            hidden = hidden.astype(BF)
            grad_inner = (dot_nn(cot, w_two) * slope).astype(BF)
            made[...] += dot_nt(hidden, w_two)
            grad_two[...] += dot_nt(grad_inner, w_one)
            target[0, :, cols] = dot_tn(two, grad_inner).astype(target.dtype)
            target[1, :, cols] = dot_tn(cot, hidden).astype(target.dtype)
            return carry

        lax.fori_loop(0, chunks, step, 0)

    lo = me % RADIX
    hi = me // RADIX % RADIX
    peers = (lambda hop: me - lo + (lo + hop) % RADIX, lambda hop: me - RADIX * hi + RADIX * ((hi + hop) % RADIX))
    digits = (lo, hi)
    plan = ((0, 1), (1, 0), (0, 1))
    quarter, shard = height // RADIX, height // RADIX**2
    extra = list(range(4, bits))
    pending = []
    waits = [[] for unused in range(PARTS)]

    def send(part, src, dst, pair, device):
        copy = remote(src, dst, pair[0], pair[1], device)
        copy.start()
        pending.append(copy)
        waits[part].append(copy)

    def arrived(part):
        for copy in waits[part]:
            copy.wait_recv()
        waits[part].clear()

    def rows(start, size):
        return pl.ds(pl.multiple_of(start, 16), size)

    def copy_blocks(target, source, part):
        tall = source.shape[1]
        for block in range(source.shape[2] // width):
            target[part, block * tall:(block + 1) * tall, :] = source[
                part, :, block * width:(block + 1) * width
            ]

    def begin(part):
        send(part, first_send.at[part], first_recv.at[part], (first_s.at[part], first_r.at[part]), (me, other))

    def reduce_one(part):
        arrived(part)
        axis = plan[part][0]
        for hop in range(1, RADIX):
            away = rows((digits[axis] + hop) % RADIX * quarter, quarter)
            slot = pl.ds((hop - 1) * quarter, quarter)
            sent[part, slot, :] = (total[part, away, :] + first_recv[part, away, :].astype(F32)).astype(BF)
            send(
                part, sent.at[part, slot], recv.at[part, slot],
                (step_s.at[part, hop - 1], step_r.at[part, hop - 1]), (peers[axis](hop), core),
            )
        held = rows(digits[axis] * quarter, quarter)
        total[part, held, :] += first_recv[part, held, :].astype(F32)

    def reduce_two(part):
        arrived(part)
        first, second = plan[part]
        start = digits[first] * quarter

        def summed(at, size):
            sums = total[part, rows(start + at, size), :]
            for hop in range(1, RADIX):
                sums = sums + recv[part, rows((hop - 1) * quarter + at, size), :].astype(F32)
            return sums

        base = (RADIX - 1) * quarter
        for hop in range(1, RADIX):
            slot = pl.ds(base + (hop - 1) * shard, shard)
            sent[part, slot, :] = summed((digits[second] + hop) % RADIX * shard, shard).astype(BF)
            send(
                part, sent.at[part, slot], recv.at[part, slot],
                (step_s.at[part, RADIX - 2 + hop], step_r.at[part, RADIX - 2 + hop]),
                (peers[second](hop), core),
            )
        at = digits[second] * shard
        total[part, rows(start + at, shard), :] = summed(at, shard)

    def spread_one(part):
        arrived(part)
        first, second = plan[part]
        start = digits[first] * quarter + digits[second] * shard
        held = rows(start, shard)
        sums = total[part, held, :]
        base = (RADIX - 1) * quarter
        for hop in range(1, RADIX):
            sums = sums + recv[part, pl.ds(base + (hop - 1) * shard, shard), :].astype(F32)
        base = base + (RADIX - 1) * shard
        for turn, bit in enumerate(extra):
            slot = pl.ds(base + turn * shard, shard)
            sent[part, slot, :] = sums.astype(BF)
            mate = me + (1 - 2 * (me // 2**bit % 2)) * 2**bit
            at = 2 * (RADIX - 1) + turn
            send(part, sent.at[part, slot], recv.at[part, slot], (step_s.at[part, at], step_r.at[part, at]), (mate, core))
            arrived(part)
            sums = sent[part, slot, :].astype(F32) + recv[part, slot, :].astype(F32)
        done = whole.at[part]
        done[held, :] = sums.astype(BF)
        for hop in range(1, RADIX):
            send(
                part, done.at[held], done.at[held],
                (spread_s.at[part, hop - 1], spread_r.at[part, hop - 1]), (peers[second](hop), core),
            )

    def spread_two(part):
        arrived(part)
        axis = plan[part][0]
        held = rows(digits[axis] * quarter, quarter)
        done = whole.at[part]
        for hop in range(1, RADIX):
            send(
                part, done.at[held], done.at[held],
                (spread_s.at[part, RADIX - 2 + hop], spread_r.at[part, RADIX - 2 + hop]),
                (peers[axis](hop), core),
            )

    swaps[1].wait_recv()
    step_mlp(other, mlp_away)
    for part in range(2):
        copy_blocks(first_send, mlp_away, part)
        begin(part)
    step_mlp(core, mlp_mine)
    for part in range(2):
        copy_blocks(total, mlp_mine, part)
        reduce_one(part)

    norm_sum[...] = jnp.zeros_like(norm_sum)

    def step_backward(image, carry):
        here = place_of(image)
        made[here, :] += middle[here, :]
        both_out[core, here, :] = made[here, :].astype(BF)
        grad_n = grad_two[here, :]
        normal = normal_two[here, :]
        norm_sum[2:3, :] += jnp.sum(grad_n * normal, axis=0, keepdims=True)
        norm_sum[3:4, :] += jnp.sum(grad_n, axis=0, keepdims=True)
        grad_mid = cot_low[here, :].astype(F32) + norm_back(
            grad_n, normal, scale_two[here, :], norms_ref[2:3, :]
        )
        low = grad_mid.astype(BF)
        grad_mid_low[here, :] = low
        grad_mix = dot_nt(low, weight(3)).astype(BF)
        q = query[here, :]
        k = key[here, :]
        v = value[here, :]
        parts_q, parts_k, parts_v = [], [], []
        for pair in range(pairs):
            cols = slice(pair * 2 * HEAD, (pair + 1) * 2 * HEAD)
            gm_pair = grad_mix[:, cols]
            sum_q = sum_k = sum_v = 0.0
            for head, (q_one, k_one, v_one, gm_one) in enumerate(
                zip(halves(q[:, cols]), halves(k[:, cols]), halves(v[:, cols]), halves(gm_pair))
            ):
                prob = probs[image * 2 * pairs + 2 * pair + head]
                grad_prob = dot_nt(gm_pair, v_one)
                sum_v = sum_v + dot_tn(prob.astype(BF), gm_one)
                weighed = prob * grad_prob
                grad_score = (
                    weighed - prob * jnp.sum(weighed, axis=-1, keepdims=True)
                ).astype(BF)
                sum_q = sum_q + dot_nn(grad_score, k_one)
                sum_k = sum_k + dot_tn(grad_score, q_one)
            parts_q.append((sum_q * 0.125).astype(BF))
            parts_k.append((sum_k * 0.125).astype(BF))
            parts_v.append(sum_v.astype(BF))
        gq = jnp.concatenate(parts_q, axis=1)
        gk = jnp.concatenate(parts_k, axis=1)
        gv = jnp.concatenate(parts_v, axis=1)
        grad_query[here, :] = gq
        grad_key[here, :] = gk
        grad_value[here, :] = gv
        grad_n = dot_nn(gq, weight(0)) + dot_nn(gk, weight(1)) + dot_nn(gv, weight(2))
        grad_n = jnp.where(own_row, grad_n, 0.0)
        normal = normal_one[here, :]
        norm_sum[0:1, :] += jnp.sum(grad_n * normal, axis=0, keepdims=True)
        norm_sum[1:2, :] += jnp.sum(grad_n, axis=0, keepdims=True)
        both_grad[core, here, :] = grad_mid + norm_back(
            grad_n, normal, scale_one[here, :], norms_ref[0:1, :]
        )
        return carry

    lax.fori_loop(0, images, step_backward, 0)
    reduce_two(0)

    def norm_send(src, dst, place, device):
        copy = remote(src, dst, norm_s.at[place], norm_r.at[place], device)
        copy.start()
        pending.append(copy)
        return copy

    norm_pair[core] = norm_sum[...]
    norm_wait = [norm_send(norm_pair.at[core], norm_pair.at[core], 0, (me, other))]
    joins = [
        remote(ref.at[core], ref.at[core], join_s.at[place], join_r.at[place], (me, other))
        for place, ref in enumerate((both_out, both_grad))
    ]
    for join in joins:
        join.start()

    tall = attn_own.shape[1]
    for slot, (left, right) in enumerate(
        ((grad_query, normed), (grad_key, normed), (grad_value, normed), (mixed, grad_mid_low))
    ):
        square[...] = dot_tn(left[...], right[...])
        place = pl.ds(slot * tall, tall)
        first_send[2, place, :] = square[rows(other * tall, tall), :].astype(BF)
        total[2, place, :] = square[rows(core * tall, tall), :]
    begin(2)
    reduce_two(1)
    spread_one(0)
    reduce_one(2)
    spread_one(1)

    norm_wait[0].wait_recv()
    norm_sum[...] = norm_pair[0] + norm_pair[1]
    norm_slots[0, lo] = norm_sum[...]
    norm_wait = [
        norm_send(norm_slots.at[0, lo], norm_slots.at[0, lo], hop, (peers[0](hop), core))
        for hop in range(1, RADIX)
    ]
    for part in range(2):
        spread_two(part)
    reduce_two(2)

    for one in norm_wait:
        one.wait_recv()
    norm_sum[...] = (norm_slots[0, 0] + norm_slots[0, 1]) + (norm_slots[0, 2] + norm_slots[0, 3])
    norm_slots[1, hi] = norm_sum[...]
    norm_wait = [
        norm_send(norm_slots.at[1, hi], norm_slots.at[1, hi], RADIX - 1 + hop, (peers[1](hop), core))
        for hop in range(1, RADIX)
    ]

    for join in joins:
        join.wait_recv()
    wide[...] = jnp.zeros_like(wide)
    for image in range(count // P_SIZE):
        which, at = image // images, image % images * ROWS
        span = slice(image * P_SIZE, (image + 1) * P_SIZE)
        wide[span, :] = both_out[which, at:at + ROWS, :].astype(F32)[:P_SIZE, :]
        input_grad_ref[span, :] = both_grad[which, at:at + P_SIZE, :]
    out_ref[...] = wide[:count, :].astype(BF)

    for one in norm_wait:
        one.wait_recv()
    norm_sum[...] = (norm_slots[1, 0] + norm_slots[1, 1]) + (norm_slots[1, 2] + norm_slots[1, 3])
    for turn, bit in enumerate(extra):
        mate = me + (1 - 2 * (me // 2**bit % 2)) * 2**bit
        norm_slots[2 + turn, 0] = norm_sum[...]
        norm_send(norm_slots.at[2 + turn, 0], norm_slots.at[2 + turn, 1], 2 * RADIX - 1 + turn, (mate, core)).wait_recv()
        norm_sum[...] = norm_slots[2 + turn, 0] + norm_slots[2 + turn, 1]
    norm_out[...] = norm_sum[...]

    arrived(2)
    sums = total[2, rows(lo * quarter + hi * shard, shard), :]
    for hop in range(1, RADIX):
        sums = sums + recv[2, pl.ds((RADIX - 1) * quarter + (hop - 1) * shard, shard), :].astype(F32)
    partial[...] = sums
    for part in range(2):
        arrived(part)
    for one in pending + joins + swaps:
        one.wait_send()

    def finish(hop, carry):
        ask(hop).wait_send()
        give(hop).wait_send()
        return carry

    lax.fori_loop(1, chips, finish, 0)


def block(chips, nbr_index, nbr_valid, tokens, cotangent, queue, norms, attn, mlp):
    count, width = tokens.shape
    cores = width // attn.shape[1]
    images = nbr_valid.shape[0] // cores
    tall = images * ROWS
    padded = count + 16 - count % 8
    heads = width // HEAD
    picks = images * NBR
    bits = chips.bit_length() - 1
    extra = max(0, bits - 4)
    height = attn.shape[0] * attn.shape[1]
    quarter, shard = height // RADIX, height // RADIX**2
    moving = (RADIX - 1) * (quarter + shard) + extra * shard
    vmem = pl.BlockSpec(memory_space=pltpu.VMEM)
    smem = pl.BlockSpec(memory_space=pltpu.SMEM)
    dma = pltpu.SemaphoreType.DMA
    flat_f = pltpu.VMEM((tall, width), F32)
    flat_low = pltpu.VMEM((tall, width), BF)
    column = pltpu.VMEM((tall, 1), F32)
    steps = 2 * (RADIX - 1)
    return pl.pallas_call(
        functools.partial(block_kernel, chips, images),
        in_specs=[smem] * 2 + [vmem] * 6,
        out_specs=[vmem] * 5,
        out_shape=[
            jax.ShapeDtypeStruct((count, width), BF),
            jax.ShapeDtypeStruct((count, width), F32),
            jax.ShapeDtypeStruct((2, height, width), BF),
            jax.ShapeDtypeStruct((shard, width), F32),
            jax.ShapeDtypeStruct(norms.shape, F32),
        ],
        scratch_shapes=[
            pltpu.VMEM((attn.shape[0], cores) + attn.shape[1:], BF),
            pltpu.VMEM((mlp.shape[0], cores) + mlp.shape[1:], BF),
            pltpu.VMEM((chips, 8, LANES), jnp.int32),
            pltpu.VMEM((chips, picks, width), BF),
            pltpu.VMEM((chips, picks, width), BF),
            pltpu.VMEM((picks, width), F32),
            pltpu.VMEM((picks, width), F32),
            pltpu.VMEM((picks, width), F32),
            pltpu.VMEM((padded, width), F32),
            flat_f, flat_low, flat_f, column, flat_low, flat_low, flat_low,
            pltpu.VMEM((images * heads, ROWS, ROWS), F32),
            flat_low,
            flat_f, flat_f, column, flat_low, flat_low, flat_f,
            pltpu.VMEM(mlp.shape, F32),
            pltpu.VMEM(mlp.shape, BF),
            pltpu.VMEM((width, width), F32),
            pltpu.VMEM((cores, tall, width), BF),
            pltpu.VMEM((cores, tall, width), F32),
            pltpu.VMEM((PARTS, height, width), F32),
            pltpu.VMEM((PARTS, height, width), BF),
            pltpu.VMEM((PARTS, height, width), BF),
            pltpu.VMEM((PARTS, moving, width), BF),
            pltpu.VMEM((PARTS, moving, width), BF),
            pltpu.VMEM(norms.shape, F32),
            pltpu.VMEM((cores,) + norms.shape, F32),
            pltpu.VMEM((2 + extra, RADIX) + norms.shape, F32),
            dma((chips,)), dma((chips,)), dma((chips,)), dma((chips,)),
            dma((2,)), dma((2,)),
            dma((PARTS,)), dma((PARTS,)),
            dma((PARTS, steps + extra)), dma((PARTS, steps + extra)),
            dma((PARTS, steps)), dma((PARTS, steps)),
            dma((steps + 1 + extra,)), dma((steps + 1 + extra,)),
            dma((2,)), dma((2,)),
        ],
        compiler_params=pltpu.CompilerParams(
            collective_id=0, has_side_effects=True, vmem_limit_bytes=62 * 1024 * 1024
        ),
        name="block_both_ways",
    )(nbr_index, nbr_valid, tokens, cotangent, queue, norms, attn, mlp)


def body(
    chips,
    tokens,
    cotangent,
    queue,
    nbr_index,
    nbr_valid,
    norm_params,
    norm_first,
    norm_second,
    attn_weight,
    mlp_weight,
    attn_first,
    attn_second,
    mlp_first,
    mlp_second,
    attn_left,
    attn_right,
    mlp_left,
    mlp_right,
):
    def flip(value):
        return value.transpose(0, 2, 1)

    attn_own = flip(attn_weight)
    block_out, input_grad, summed, partial, norm_grad = block(
        chips, nbr_index, nbr_valid, tokens, cotangent, queue, norm_params, attn_own, mlp_weight
    )
    left_made, right_made, miss, attn_summed = turn_mlp(chips, summed, mlp_left, mlp_right, partial)
    (
        mlp_grad,
        mlp_new,
        mlp_copy,
        mlp_first_new,
        mlp_second_new,
        attn_grad,
        attn_new,
        attn_copy,
        attn_first_new,
        attn_second_new,
        attn_right_new,
        attn_left_new,
        norm_grad,
        norm_new,
        norm_first_new,
        norm_second_new,
        mlp_left_new,
        mlp_right_new,
        block_out,
        input_grad,
    ) = update(
        miss,
        (summed, mlp_weight, mlp_first, mlp_second, mlp_left, mlp_right),
        (
            attn_summed.reshape(attn_own.shape),
            attn_own,
            flip(attn_first),
            flip(attn_second),
            attn_right,
            attn_left,
        ),
        (norm_grad, norm_params, norm_first, norm_second),
        (left_made, right_made, block_out, input_grad),
    )
    return (
        block_out,
        input_grad,
        norm_grad,
        flip(attn_grad),
        mlp_grad,
        norm_first_new,
        norm_second_new,
        norm_new,
        flip(attn_first_new),
        flip(attn_second_new),
        mlp_first_new,
        mlp_second_new,
        attn_left_new,
        attn_right_new,
        mlp_left_new,
        mlp_right_new,
        flip(attn_new),
        flip(attn_copy),
        mlp_new,
        mlp_copy,
    )


def solution(mesh):
    return jax.shard_map(
        functools.partial(body, mesh.shape["dp"]),
        mesh=mesh,
        in_specs=(
            P("dp", None),
            P("dp", None),
            P("dp", None),
            P("dp", None),
            P("dp", None),
            P(),
            P(),
            P(),
            P(None, None, "mp"),
            P(None, None, "mp"),
            P(None, None, "mp"),
            P(None, None, "mp"),
            P(None, None, "mp"),
            P(None, None, "mp"),
            P(None, "mp", None),
            P(None, "mp", None),
            P(None, "mp", None),
            P(None, "mp", None),
        ),
        out_specs=(
            P("dp", None),
            P("dp", None),
            P(),
            P(None, None, "mp"),
            P(None, None, "mp"),
            P(),
            P(),
            P(),
            P(None, None, "mp"),
            P(None, None, "mp"),
            P(None, None, "mp"),
            P(None, None, "mp"),
            P(None, "mp", None),
            P(None, "mp", None),
            P(None, "mp", None),
            P(None, "mp", None),
            P(None, None, "mp"),
            P(None, None, "mp"),
            P(None, None, "mp"),
            P(None, None, "mp"),
        ),
        check_vma=False,
    )
```

```python
import functools
import math

import jax
import jax.numpy as jnp
from jax import lax
from jax.experimental import pallas as pl
from jax.experimental.pallas import tpu as pltpu
from jax.sharding import PartitionSpec as P

BETA_FIRST = 0.9
BETA_SECOND = 0.95
EPSILON = 1e-08
RATE_MATRIX = 0.15
DECAY_RATE = 0.05
TURN_RATE = 4.0
STEP = 10
BLOCK = 256
ROUNDS = 3
NEAR = 0.01
PIECE = 128
PAUSES = 40

BF = jnp.bfloat16
F32 = jnp.float32


def dot_nn(a, b):
    return lax.dot_general(a, b, (((1,), (0,)), ((), ())), preferred_element_type=F32)


def dot_nt(a, b):
    return lax.dot_general(a, b, (((1,), (1,)), ((), ())), preferred_element_type=F32)


def dot_tn(a, b):
    return lax.dot_general(a, b, (((0,), (0,)), ((), ())), preferred_element_type=F32)


def split(a):
    high = a.astype(BF)
    return high, (a - high.astype(F32)).astype(BF)


def three(dot, a, b):
    return dot(a[0], b[0]) + (dot(a[0], b[1]) + dot(a[1], b[0]))


def below(size):
    row = lax.broadcasted_iota(jnp.int32, (size, size), 0)
    col = lax.broadcasted_iota(jnp.int32, (size, size), 1)
    return row > col, row == col


def in_step(chains):
    chains = list(chains)
    while chains:
        kept = []
        for chain in chains:
            try:
                next(chain)
                kept.append(chain)
            except StopIteration:
                pass
        chains = kept


def renew_chain(base_ref, out_ref, misses):
    width = base_ref.shape[1]
    source = base_ref
    for at in range(0, width, BLOCK):
        size = min(BLOCK, width - at)
        lower, same = below(size)
        eye = jnp.where(same, 1.0, 0.0)
        low = source[:, at:at + size].astype(BF)
        gram = dot_tn(low, low)
        yield
        on_diag = jnp.where(same, gram, 0.0)
        s_col = lax.rsqrt(jnp.maximum(jnp.sum(on_diag, axis=1, keepdims=True), 1e-30))
        s_row = lax.rsqrt(jnp.maximum(jnp.sum(on_diag, axis=0, keepdims=True), 1e-30))
        state = gram * s_col * s_row
        made = jnp.where(same, s_col, 0.0).astype(BF)
        for turn in range(ROUNDS):
            under = jnp.where(lower, state, 0.0)
            moved = dot_nn(under.astype(BF), state.astype(BF))
            mass = jnp.sum(under * under, axis=1, keepdims=True)
            yield
            curve = jnp.sum(moved * under, axis=1, keepdims=True)
            pace = jnp.where(curve > mass, mass / jnp.maximum(curve, 1e-30), 1.0)
            left = 1.0 - 2.0 * pace * mass + pace * pace * curve
            scale = lax.rsqrt(jnp.maximum(left, 1e-6))
            step = (scale * (eye - pace * under)).astype(BF)
            if turn + 1 < ROUNDS:
                state = dot_nt((scale * (state - pace * moved)).astype(BF), step)
            made = dot_nn(step, made).astype(BF)
            yield
        high, low = split(source[:, at:at + size])
        block = dot_nt(high, made) + dot_nt(low, made)
        yield
        pair = split(block)
        gram = three(dot_tn, pair, pair)
        yield
        off = jnp.where(lower, gram, 0.0) + jnp.where(same, 0.5 * (gram - 1.0), 0.0)
        misses.append(jnp.sum(off * off) * (1.0 / size))
        block = block - dot_nt(pair[0], off.astype(BF))
        out_ref[:, at:at + size] = block
        yield
        if at + size < width:
            pair = split(block)
            rest = source[:, at + size:]
            shared = split(three(dot_tn, pair, split(rest)))
            yield
            out_ref[:, at + size:] = rest - three(dot_nn, pair, shared)
            source = out_ref
            yield


def renew_rows(base_ref, out_ref, work_ref):
    size = base_ref.shape[0]
    group = 64
    work_ref[...] = base_ref[...].T

    def take(turn, carry):
        row = work_ref[pl.ds(turn, 1), :]
        row = row * lax.rsqrt(jnp.sum(row * row, axis=1, keepdims=True))
        work_ref[pl.ds(turn, 1), :] = row

        def clear(which, inner):
            here = pl.ds(pl.multiple_of(which * group, group), group)
            rows = work_ref[here, :]
            later = lax.broadcasted_iota(jnp.int32, (group, 1), 0) + which * group > turn
            share = jnp.where(later, jnp.sum(rows * row, axis=1, keepdims=True), 0.0)
            work_ref[here, :] = rows - share * row
            return inner

        return lax.fori_loop(turn // group, size // group, clear, carry)

    lax.fori_loop(0, size, take, 0)
    out_ref[...] = work_ref[...].T


def move_chain(grad, left_pair, right_pair, weight_ref, first_ref, second_ref, new_ref, copy_ref, first_new_ref, second_new_ref, move_ref):
    rows = grad.shape[0]
    for at in range(0, rows, PIECE):
        size = min(PIECE, rows - at)
        part = slice(at, at + size)
        half = dot_tn(left_pair[0][:, part], grad) + dot_tn(left_pair[1][:, part], grad)
        yield
        turned = three(dot_nn, split(half), right_pair)
        yield
        first_new = BETA_FIRST * first_ref[part, :] + (1.0 - BETA_FIRST) * turned
        second_new = BETA_SECOND * second_ref[part, :] + (1.0 - BETA_SECOND) * turned * turned
        first_new_ref[part, :] = first_new
        second_new_ref[part, :] = second_new
        move_ref[part, :] = (
            first_new
            / (1.0 - BETA_FIRST**STEP)
            / (jnp.sqrt(second_new / (1.0 - BETA_SECOND**STEP)) + EPSILON)
        ).astype(BF)
        yield
    for at in range(0, rows, PIECE):
        part = slice(at, min(at + PIECE, rows))
        back = dot_nn(left_pair[0][part, :], move_ref[...]).astype(BF)
        yield
        new = weight_ref[part, :] * (1.0 - RATE_MATRIX * DECAY_RATE) - RATE_MATRIX * dot_nt(back, right_pair[0])
        new_ref[part, :] = new
        copy_ref[part, :] = new.astype(BF)
        yield


RATE_NORM = 0.6


MESH = pl.DeviceIdType.MESH
RADIX = 4


def remote(src, dst, send, recv, device):
    return pltpu.make_async_remote_copy(
        src_ref=src, dst_ref=dst, send_sem=send, recv_sem=recv, device_id=device, device_id_type=MESH
    )


def set_bases(grad, left, right, left_low, right_low, left_base, right_base):
    gram = dot_nt(grad, grad)
    pace = TURN_RATE / (jnp.sqrt(jnp.sum(gram * gram)) + 1e-06)
    left_base[...] = left + dot_nn(gram.astype(BF), left_low) * pace
    right_base[...] = right + dot_tn(grad, dot_nn(grad, right_low).astype(BF)) * pace


def side_by_side(grad, height):
    return jnp.concatenate([grad[at:at + height] for at in range(0, grad.shape[0], height)], axis=1)


def update_kernel(
    together,
    miss_ref, mlp_grad_ref, mlp_weight_ref, mlp_first_ref, mlp_second_ref, mlp_left_ref, mlp_right_ref,
    grad_ref, weight_ref, first_ref, second_ref, left_ref, right_ref,
    norm_grad_ref, norm_ref, norm_first_ref, norm_second_ref,
    mlp_left_made, mlp_right_made, block_ref, input_grad_ref,
    mlp_grad_out, mlp_new_ref, mlp_copy_ref, mlp_first_new_ref, mlp_second_new_ref,
    grad_out_ref, new_ref, copy_ref, first_new_ref, second_new_ref, left_new_ref, right_new_ref,
    norm_grad_out, norm_new, norm_first_new, norm_second_new,
    mlp_left_out, mlp_right_out, block_out, input_grad_out,
    mlp_move, left_base, right_base, move_ref, left_held, right_held, work, work_small,
    block_held, input_grad_held, sems_in, sems_out,
):
    slot = pl.program_id(0)
    last = pl.num_programs(0) - 1

    def copies(passed, at):
        return (
            [pltpu.make_async_copy(src, held, sems_in.at[at + place]) for place, (src, held, dst) in enumerate(passed)],
            [pltpu.make_async_copy(held, dst, sems_out.at[at + place]) for place, (src, held, dst) in enumerate(passed)],
        )

    bases = copies(
        ((mlp_left_made.at[slot], left_held, mlp_left_out.at[slot]), (mlp_right_made.at[slot], right_held, mlp_right_out.at[slot])), 0
    )
    wide = copies(((block_ref, block_held, block_out), (input_grad_ref, input_grad_held, input_grad_out)), 2)

    @pl.when(slot == 0)
    def _():
        for copy in wide[0]:
            copy.start()
        grad = norm_grad_ref[...]
        first = BETA_FIRST * norm_first_ref[...] + (1.0 - BETA_FIRST) * grad
        second = BETA_SECOND * norm_second_ref[...] + (1.0 - BETA_SECOND) * grad * grad
        norm_grad_out[...] = grad
        norm_first_new[...] = first
        norm_second_new[...] = second
        norm_new[...] = norm_ref[...] - RATE_NORM * (first / (1.0 - BETA_FIRST**STEP)) / (
            jnp.sqrt(second / (1.0 - BETA_SECOND**STEP)) + EPSILON
        )

    for copy in bases[0]:
        copy.start()
    mlp_grad = side_by_side(mlp_grad_ref[0], mlp_weight_ref.shape[1])
    mlp_grad_out[0] = mlp_grad.astype(F32)
    chains = []
    misses = []
    for which in range(together):
        grad = grad_ref[which]
        grad_out_ref[which] = grad.astype(F32)
        left = left_ref[which]
        right = right_ref[which]
        left_pair = split(left)
        right_pair = split(right)
        set_bases(grad, left, right, left_pair[0], right_pair[0], left_base.at[which], right_base.at[which])
        misses.append(([], []))
        chains.append(renew_chain(right_base.at[which], right_new_ref.at[which], misses[which][1]))
        chains.append(renew_chain(left_base.at[which], left_new_ref.at[which], misses[which][0]))
        chains.append(
            move_chain(
                grad, left_pair, right_pair, weight_ref.at[which], first_ref.at[which], second_ref.at[which],
                new_ref.at[which], copy_ref.at[which], first_new_ref.at[which], second_new_ref.at[which],
                move_ref.at[which],
            )
        )
    chains.append(
        move_chain(
            mlp_grad, split(mlp_left_ref[0]), split(mlp_right_ref[0]),
            mlp_weight_ref.at[0], mlp_first_ref.at[0], mlp_second_ref.at[0],
            mlp_new_ref.at[0], mlp_copy_ref.at[0], mlp_first_new_ref.at[0], mlp_second_new_ref.at[0], mlp_move,
        )
    )
    in_step(chains)
    for copy in bases[0]:
        copy.wait()
    poor = jnp.logical_not(jnp.maximum(miss_ref[slot, 0], miss_ref[slot, 1]) < NEAR)

    @pl.when(poor)
    def _():
        left = mlp_left_ref[0]
        right = mlp_right_ref[0]
        size = left.shape[0]
        set_bases(mlp_grad, left, right, left.astype(BF), right.astype(BF), left_held, right_held)
        renew_rows(left_held, left_held, work.at[pl.ds(0, size), pl.ds(0, size)])
        renew_rows(right_held, right_held, work)

    for copy in bases[1]:
        copy.start()
    for which in range(together):
        for missed, base, out in zip(misses[which], (left_base, right_base), (left_new_ref, right_new_ref)):
            worst = functools.reduce(jnp.maximum, missed)

            @pl.when(jnp.logical_not(worst < NEAR))
            def _(base=base, out=out):
                size = base.shape[1]
                space = work_small if size == work_small.shape[0] else work.at[pl.ds(0, size), pl.ds(0, size)]
                renew_rows(base.at[which], out.at[which], space)

    @pl.when(slot == 0)
    def _():
        for copy in wide[0]:
            copy.wait()
        for copy in wide[1]:
            copy.start()

    @pl.when(slot == last)
    def _():
        for copy in wide[1]:
            copy.wait()

    for copy in bases[1]:
        copy.wait()


def update(miss, mlp, attn, norms, passed):
    like = jax.ShapeDtypeStruct
    slots = mlp[1].shape[0]
    together = attn[1].shape[0] // slots

    def spec(count, value):
        return pl.BlockSpec((count,) + value.shape[1:], lambda slot: (slot, 0, 0))

    def made(value):
        return [like(value.shape, F32)] * 2 + [like(value.shape, BF)] + [like(value.shape, F32)] * 2

    whole = pl.BlockSpec(norms[0].shape, lambda slot: (0, 0))
    anywhere = pl.BlockSpec(memory_space=pl.ANY)
    rows, width = attn[1].shape[1:]
    sides = [pltpu.VMEM((together, rows, rows), F32), pltpu.VMEM((together, width, width), F32)]
    held = [pltpu.VMEM(value.shape[1:], F32) for value in passed[:2]]
    return pl.pallas_call(
        functools.partial(update_kernel, together),
        grid=(slots,),
        in_specs=[pl.BlockSpec(memory_space=pltpu.SMEM)]
        + [spec(1, value) for value in mlp]
        + [spec(together, value) for value in attn]
        + [whole] * 4
        + [anywhere] * 4,
        out_specs=[spec(1, mlp[1])] * 5
        + [spec(together, attn[1])] * 5
        + [spec(together, attn[4]), spec(together, attn[5])]
        + [whole] * 4
        + [anywhere] * 4,
        out_shape=made(mlp[1])
        + made(attn[1])
        + [like(attn[4].shape, F32), like(attn[5].shape, F32)]
        + [like(norms[0].shape, F32)] * 4
        + [like(value.shape, value.dtype) for value in passed],
        scratch_shapes=[pltpu.VMEM(mlp[1].shape[1:], BF)]
        + sides
        + [pltpu.VMEM((together, rows, width), BF)]
        + held
        + [held[1], pltpu.VMEM((rows, rows), F32)]
        + [pltpu.VMEM(value.shape, value.dtype) for value in passed[2:]]
        + [pltpu.SemaphoreType.DMA((len(passed),)), pltpu.SemaphoreType.DMA((len(passed),))],
        compiler_params=pltpu.CompilerParams(vmem_limit_bytes=62 * 1024 * 1024),
        name="update",
    )(miss, *mlp, *attn, *norms, *passed)


P_SIZE = 197
NBR = 8
HEAD = 64
ROWS = 208
FAR = 200
CHUNK = 256
LANES = 128
DELAY = 4
AHEAD = 12
PARTS = 3


def layer_norm(values, gain, shift):
    centre = values - jnp.mean(values, axis=-1, keepdims=True)
    scale = lax.rsqrt(jnp.mean(centre * centre, axis=-1, keepdims=True) + 1e-06)
    normal = centre * scale
    return (normal * gain + shift, normal, scale)


def norm_back(grad, normal, scale, gain):
    shaped = grad * gain
    return scale * (
        shaped
        - jnp.mean(shaped, axis=-1, keepdims=True)
        - normal * jnp.mean(shaped * normal, axis=-1, keepdims=True)
    )


def gelu_pair(value):
    size = jnp.abs(value) * (1.0 / math.sqrt(2.0))
    bell = jnp.exp(-0.5 * value * value)
    part = 1.0 / (1.0 + 0.3275911 * size)
    series = part * (
        0.254829592
        + part * (-0.284496736 + part * (1.421413741 + part * (-1.453152027 + part * 1.061405429)))
    )
    tail = 0.5 * series * bell
    share = jnp.where(value < 0.0, tail, 1.0 - tail)
    return value * share, share + value * bell * (1.0 / math.sqrt(2.0 * math.pi))


def block_kernel(
    chips, images,
    index_ref, valid_ref,
    tokens_ref, cotangent_ref, queue_ref, norms_ref, attn_own, mlp_own, mlp_left, mlp_right,
    out_ref, input_grad_ref, whole, attn_grad, norm_out, miss_ref, mlp_left_new, mlp_right_new,
    attn_ref, mlp_ref, asked, parts_out, given, wide, both_out, both_grad,
    total, first_send, first_recv, sent, recv, norm_sum, norm_pair, norm_slots,
    ask_send, ask_recv, give_send, give_recv, swap_send, swap_recv,
    first_s, first_r, step_s, step_r, spread_s, spread_r, norm_s, norm_r, join_s, join_r, direct_s, direct_r, load_s, store_s,
):
    me = lax.axis_index("dp")
    core = lax.axis_index("mp")
    other = 1 - core
    count = tokens_ref.shape[0]
    width = tokens_ref.shape[1]
    depth = queue_ref.shape[0]
    picks = images * NBR
    group = LANES // picks
    pairs = width // (2 * HEAD)
    bits = chips.bit_length() - 1
    height = whole.shape[1]

    barrier = pltpu.get_barrier_semaphore()
    pl.semaphore_signal(barrier, inc=1, device_id=(me, other), device_id_type=MESH)

    def greet(hop, carry):
        pl.semaphore_signal(
            barrier, inc=1, device_id=(lax.rem(me + hop, chips), core), device_id_type=MESH
        )
        return carry

    lax.fori_loop(1, chips, greet, 0)
    pick_lane = lax.broadcasted_iota(jnp.int32, (8, LANES), 1)
    wanted = jnp.full((8, LANES), -1, jnp.int32)
    for pick in range(picks):
        wanted = jnp.where(
            pick_lane % picks == pick, index_ref[core * images + pick // NBR, pick % NBR], wanted
        )
    asked[0] = wanted
    attn_ref[:, core] = attn_own[...].astype(BF)
    mlp_ref[:, core] = mlp_own[...].astype(BF)
    pl.semaphore_wait(barrier, chips)

    def ask(hop):
        return remote(
            asked.at[0], asked.at[hop], ask_send.at[hop], ask_recv.at[hop],
            (lax.rem(me + hop, chips), core),
        )

    def give(hop):
        return remote(
            parts_out.at[hop], given.at[hop], give_send.at[hop], give_recv.at[hop],
            (lax.rem(me + chips - hop, chips), core),
        )

    def start_ask(hop, carry):
        ask(hop).start()
        return carry

    lax.fori_loop(1, chips, start_ask, 0)
    def swap(which):
        ref = (attn_ref, mlp_ref)[which]
        return remote(ref.at[:, core], ref.at[:, core], swap_send.at[which], swap_recv.at[which], (me, other))

    for which in range(2):
        swap(which).start()

    seat = me % RADIX**2
    lo = me % RADIX
    hi = me // RADIX % RADIX
    peers = (lambda hop: me - lo + (lo + hop) % RADIX, lambda hop: me - RADIX * hi + RADIX * ((hi + hop) % RADIX))
    digits = (lo, hi)
    plan = ((0, 1), (1, 0), (0, 1))
    quarter, shard = height // RADIX, height // RADIX**2
    extra = list(range(4, bits))

    def mate(bit):
        return me + (1 - 2 * (me // 2**bit % 2)) * 2**bit

    pending = []
    waits = [[] for unused in range(PARTS)]

    def send(part, make):
        make().start()
        pending.append(make)
        waits[part].append(make)

    def arrived(part):
        for make in waits[part]:
            make().wait_recv()
        waits[part].clear()

    def rows(start, size):
        return pl.ds(pl.multiple_of(start, 16), size)

    def copy_blocks(target, source, part):
        tall = source.shape[1]
        for block in range(source.shape[2] // width):
            target[part, block * tall:(block + 1) * tall, :] = source[
                part, :, block * width:(block + 1) * width
            ]

    def begin(part):
        send(
            part,
            lambda: remote(
                first_send.at[part], first_recv.at[part], first_s.at[part], first_r.at[part], (me, other)
            ),
        )

    def reduce_one(part):
        arrived(part)
        axis = plan[part][0]
        for hop in range(1, RADIX):
            away = rows((digits[axis] + hop) % RADIX * quarter, quarter)
            slot = pl.ds((hop - 1) * quarter, quarter)
            sent[part, slot, :] = (total[part, away, :] + first_recv[part, away, :].astype(F32)).astype(BF)
            send(
                part,
                lambda hop=hop, slot=slot: remote(
                    sent.at[part, slot], recv.at[part, slot],
                    step_s.at[part, hop - 1], step_r.at[part, hop - 1], (peers[axis](hop), core),
                ),
            )
        held = rows(digits[axis] * quarter, quarter)
        total[part, held, :] += first_recv[part, held, :].astype(F32)

    def reduce_two(part):
        arrived(part)
        first, second = plan[part]
        start = digits[first] * quarter

        def summed(at, size):
            sums = total[part, rows(start + at, size), :]
            for hop in range(1, RADIX):
                sums = sums + recv[part, rows((hop - 1) * quarter + at, size), :].astype(F32)
            return sums

        base = (RADIX - 1) * quarter
        for hop in range(1, RADIX):
            slot = pl.ds(base + (hop - 1) * shard, shard)
            sent[part, slot, :] = summed((digits[second] + hop) % RADIX * shard, shard).astype(BF)
            send(
                part,
                lambda hop=hop, slot=slot: remote(
                    sent.at[part, slot], recv.at[part, slot],
                    step_s.at[part, RADIX - 2 + hop], step_r.at[part, RADIX - 2 + hop], (peers[second](hop), core),
                ),
            )
        at = digits[second] * shard
        total[part, rows(start + at, shard), :] = summed(at, shard)

    def place(part):
        first, second = plan[part]
        return rows(digits[first] * quarter + digits[second] * shard, shard)

    def last_sum(part):
        arrived(part)
        sums = total[part, place(part), :]
        base = (RADIX - 1) * quarter
        for hop in range(1, RADIX):
            sums = sums + recv[part, pl.ds(base + (hop - 1) * shard, shard), :].astype(F32)
        base = base + (RADIX - 1) * shard
        for turn, bit in enumerate(extra):
            slot = pl.ds(base + turn * shard, shard)
            sent[part, slot, :] = sums.astype(BF)
            at = 2 * (RADIX - 1) + turn
            send(
                part,
                lambda bit=bit, slot=slot, at=at: remote(
                    sent.at[part, slot], recv.at[part, slot], step_s.at[part, at], step_r.at[part, at],
                    (mate(bit), core),
                ),
            )
            arrived(part)
            sums = sent[part, slot, :].astype(F32) + recv[part, slot, :].astype(F32)
        return sums.astype(BF)

    def spread_one(part):
        whole[part, place(part), :] = last_sum(part)
        for hop in range(1, RADIX):
            send(
                part,
                lambda hop=hop: remote(
                    whole.at[part, place(part)], whole.at[part, place(part)],
                    spread_s.at[part, hop - 1], spread_r.at[part, hop - 1], (peers[plan[part][1]](hop), core),
                ),
            )

    def direct(hop):
        return remote(
            attn_grad.at[place(2)], attn_grad.at[place(2)], direct_s.at[hop], direct_r.at[hop],
            (me - seat + (seat + hop) % RADIX**2, core),
        )

    def spread_direct():
        attn_grad[place(2), :] = last_sum(2)

        def start(hop, carry):
            direct(hop).start()
            return carry

        lax.fori_loop(1, RADIX**2, start, 0)

    def spread_two(part):
        arrived(part)
        axis = plan[part][0]
        for hop in range(1, RADIX):

            def make(hop=hop):
                held = rows(digits[axis] * quarter, quarter)
                return remote(
                    whole.at[part, held], whole.at[part, held],
                    spread_s.at[part, RADIX - 2 + hop], spread_r.at[part, RADIX - 2 + hop],
                    (peers[axis](hop), core),
                )

            send(part, make)

    def first_phase(
        far_f, far_key, far_value, tokens_f, normed, normal_one, scale_one, query, key, value, probs, mixed,
        middle, normal_two, scale_two, normed_two, cot_low, made, mlp_mine, mlp_away, square,
    ):
        grad_two = tokens_f
        grad_query, grad_key, grad_value, grad_mid_low = query, key, value, normed_two

        def spread(source, target):
            for which in range(count // (images * P_SIZE)):

                @pl.when(core == which)
                def _(which=which):
                    for image in range(images):
                        start = (which * images + image) * P_SIZE
                        target[image * ROWS:(image + 1) * ROWS, :] = source[start:start + ROWS, :]

        places = lax.broadcasted_iota(jnp.int32, (depth, LANES), 0) + me * depth
        lane_group = lax.broadcasted_iota(jnp.int32, (1, LANES), 1) // picks

        def answer(turn, carry):
            wish = jnp.zeros((1, LANES), jnp.int32)
            for step in range(group):
                hop = turn * group + step

                @pl.when(hop > 0)
                def _(hop=hop):
                    ask(hop).wait_recv()

                wish = jnp.where(lane_group == step, asked[hop][:1, :], wish)
            chooser = jnp.where(wish == places, 1.0, 0.0).astype(BF)
            picked = dot_tn(chooser, queue_ref[...]).astype(BF)
            parts_out[pl.ds(turn * group, group)] = picked.reshape(group, picks, width)
            for step in range(group):
                hop = turn * group + step

                @pl.when(hop > 0)
                def _(hop=hop):
                    give(hop).start()

            return carry

        wide[:count, :] = tokens_ref[...].astype(F32)
        wide[count:, :] = jnp.zeros((wide.shape[0] - count, width), F32)
        spread(wide, tokens_f)
        lax.fori_loop(0, chips // group, answer, 0)
        wide[:count, :] = cotangent_ref[...].astype(F32)
        spread(wide, made)
        own_row = lax.broadcasted_iota(jnp.int32, (ROWS, 1), 0) < P_SIZE
        lane = lax.broadcasted_iota(jnp.int32, (1, 2 * HEAD), 1)
        first_head = lane < HEAD
        key_lane = lax.broadcasted_iota(jnp.int32, (1, ROWS), 1)

        def halves(pair):
            zero = jnp.zeros_like(pair)
            return jnp.where(first_head, pair, zero), jnp.where(first_head, zero, pair)

        def place_of(image):
            return pl.ds(pl.multiple_of(image * ROWS, ROWS), ROWS)

        def weight(slot):
            return attn_ref[slot].reshape(width, width)

        def step_norm(image, carry):
            here = place_of(image)
            cot_low[here, :] = jnp.where(own_row, made[here, :], 0.0).astype(BF)
            normed_f, normal, scale = layer_norm(tokens_f[here, :], norms_ref[0:1, :], norms_ref[1:2, :])
            normal_one[here, :] = normal
            scale_one[here, :] = scale
            made[here, :] = jnp.where(own_row, normed_f, 0.0)
            return carry

        lax.fori_loop(0, images, step_norm, 0)
        swap(0).wait_recv()

        def step_own(image, carry):
            here = place_of(image)
            low = made[here, :].astype(BF)
            query[here, :] = dot_nt(low, weight(0)).astype(BF)
            middle[here, :] = dot_nt(low, weight(1))
            normal_two[here, :] = dot_nt(low, weight(2))
            return carry

        lax.fori_loop(0, images, step_own, 0)

        def collect(hop, sums):
            give(hop).wait_recv()
            return sums + given[hop].astype(F32)

        far_f[...] = lax.fori_loop(1, chips, collect, parts_out[0].astype(F32))
        far_low = far_f[...].astype(BF)
        far_key[...] = dot_nt(far_low, weight(1))
        far_value[...] = dot_nt(far_low, weight(2))

        def step_forward(image, carry):
            here = place_of(image)
            x = tokens_f[here, :]
            near = pl.ds(pl.multiple_of(image * NBR, NBR), NBR)

            def with_far(own, far):
                return jnp.concatenate([own[here, :][:FAR, :], far[near, :]], axis=0).astype(BF)

            normed[here, :] = with_far(made, far_f)
            q = query[here, :]
            k = with_far(middle, far_key)
            v = with_far(normal_two, far_value)
            key[here, :] = k
            value[here, :] = v
            bias = jnp.where(key_lane < P_SIZE, 0.0, -1e30)
            for slot in range(NBR):
                okay = valid_ref[core * images + image, slot] > 0
                bias = jnp.where(key_lane == FAR + slot, jnp.where(okay, 0.0, -1e30), bias)
            parts = []
            for pair in range(pairs):
                cols = slice(pair * 2 * HEAD, (pair + 1) * 2 * HEAD)
                k_pair = k[:, cols]
                sums = 0.0
                for head, (q_one, v_one) in enumerate(zip(halves(q[:, cols]), halves(v[:, cols]))):
                    scores = dot_nt(q_one, k_pair) * 0.125 + bias
                    top = jnp.max(scores, axis=-1, keepdims=True)
                    powers = jnp.exp(scores - top)
                    prob = powers / jnp.sum(powers, axis=-1, keepdims=True)
                    probs[image * 2 * pairs + 2 * pair + head] = prob
                    sums = sums + dot_nn(prob.astype(BF), v_one)
                parts.append(sums.astype(BF))
            mix = jnp.concatenate(parts, axis=1)
            mixed[here, :] = mix
            mid = x + dot_nn(mix, weight(3))
            middle[here, :] = mid
            two_f, normal, scale = layer_norm(mid, norms_ref[2:3, :], norms_ref[3:4, :])
            normal_two[here, :] = normal
            scale_two[here, :] = scale
            normed_two[here, :] = two_f.astype(BF)
            return carry

        lax.fori_loop(0, images, step_forward, 0)

        made[...] = jnp.zeros_like(made)
        grad_two[...] = jnp.zeros_like(grad_two)
        chunks = mlp_ref.shape[3] // CHUNK

        def step_mlp(half, target):
            def step(turn, carry):
                cols = pl.ds(pl.multiple_of(turn * CHUNK, CHUNK), CHUNK)
                w_one = mlp_ref[0, half, :, cols]
                w_two = mlp_ref[1, half, :, cols]
                two = normed_two[...]
                cot = cot_low[...]
                hidden, slope = gelu_pair(dot_nn(two, w_one))
                hidden = hidden.astype(BF)
                grad_inner = (dot_nn(cot, w_two) * slope).astype(BF)
                made[...] += dot_nt(hidden, w_two)
                grad_two[...] += dot_nt(grad_inner, w_one)
                target[0, :, cols] = dot_tn(two, grad_inner).astype(target.dtype)
                target[1, :, cols] = dot_tn(cot, hidden).astype(target.dtype)
                return carry

            lax.fori_loop(0, chunks, step, 0)

        swap(1).wait_recv()
        step_mlp(other, mlp_away)
        for part in range(2):
            copy_blocks(first_send, mlp_away, part)
            begin(part)
        step_mlp(core, mlp_mine)
        for part in range(2):
            copy_blocks(total, mlp_mine, part)
            reduce_one(part)

        norm_sum[...] = jnp.zeros_like(norm_sum)

        def step_backward(image, carry):
            here = place_of(image)
            made[here, :] += middle[here, :]
            both_out[core, here, :] = made[here, :].astype(BF)
            grad_n = grad_two[here, :]
            normal = normal_two[here, :]
            norm_sum[2:3, :] += jnp.sum(grad_n * normal, axis=0, keepdims=True)
            norm_sum[3:4, :] += jnp.sum(grad_n, axis=0, keepdims=True)
            grad_mid = cot_low[here, :].astype(F32) + norm_back(
                grad_n, normal, scale_two[here, :], norms_ref[2:3, :]
            )
            low = grad_mid.astype(BF)
            grad_mid_low[here, :] = low
            grad_mix = dot_nt(low, weight(3)).astype(BF)
            q = query[here, :]
            k = key[here, :]
            v = value[here, :]
            parts_q, parts_k, parts_v = [], [], []
            for pair in range(pairs):
                cols = slice(pair * 2 * HEAD, (pair + 1) * 2 * HEAD)
                gm_pair = grad_mix[:, cols]
                sum_q = sum_k = sum_v = 0.0
                for head, (q_one, k_one, v_one, gm_one) in enumerate(
                    zip(halves(q[:, cols]), halves(k[:, cols]), halves(v[:, cols]), halves(gm_pair))
                ):
                    prob = probs[image * 2 * pairs + 2 * pair + head]
                    grad_prob = dot_nt(gm_pair, v_one)
                    sum_v = sum_v + dot_tn(prob.astype(BF), gm_one)
                    weighed = prob * grad_prob
                    grad_score = (
                        weighed - prob * jnp.sum(weighed, axis=-1, keepdims=True)
                    ).astype(BF)
                    sum_q = sum_q + dot_nn(grad_score, k_one)
                    sum_k = sum_k + dot_tn(grad_score, q_one)
                parts_q.append((sum_q * 0.125).astype(BF))
                parts_k.append((sum_k * 0.125).astype(BF))
                parts_v.append(sum_v.astype(BF))
            gq = jnp.concatenate(parts_q, axis=1)
            gk = jnp.concatenate(parts_k, axis=1)
            gv = jnp.concatenate(parts_v, axis=1)
            grad_query[here, :] = gq
            grad_key[here, :] = gk
            grad_value[here, :] = gv
            grad_n = dot_nn(gq, weight(0)) + dot_nn(gk, weight(1)) + dot_nn(gv, weight(2))
            grad_n = jnp.where(own_row, grad_n, 0.0)
            normal = normal_one[here, :]
            norm_sum[0:1, :] += jnp.sum(grad_n * normal, axis=0, keepdims=True)
            norm_sum[1:2, :] += jnp.sum(grad_n, axis=0, keepdims=True)
            both_grad[core, here, :] = grad_mid + norm_back(
                grad_n, normal, scale_one[here, :], norms_ref[0:1, :]
            )
            return carry

        lax.fori_loop(0, images, step_backward, 0)
        reduce_two(0)
        tall = attn_own.shape[1]
        for slot, (left, right) in enumerate(
            ((grad_query, normed), (grad_key, normed), (grad_value, normed), (mixed, grad_mid_low))
        ):
            square[...] = dot_tn(left[...], right[...])
            span = pl.ds(slot * tall, tall)
            first_send[2, span, :] = square[rows(other * tall, tall), :].astype(BF)
            total[2, span, :] = square[rows(core * tall, tall), :]
        begin(2)


    tall_rows = images * ROWS
    flat_f = pltpu.VMEM((tall_rows, width), F32)
    flat_low = pltpu.VMEM((tall_rows, width), BF)
    column = pltpu.VMEM((tall_rows, 1), F32)
    near = pltpu.VMEM((picks, width), F32)
    pl.run_scoped(
        first_phase,
        near, near, near, flat_f, flat_low, flat_f, column, flat_low, flat_low, flat_low,
        pltpu.VMEM((images * width // HEAD, ROWS, ROWS), F32),
        flat_low, flat_f, flat_f, column, flat_low, flat_low, flat_f,
        pltpu.VMEM(mlp_own.shape, F32),
        pltpu.VMEM(mlp_own.shape, BF),
        pltpu.VMEM((width, width), F32),
    )

    def norm_send(make):
        make().start()
        pending.append(make)
        return make

    def join(which):
        ref = (both_out, both_grad)[which]
        return remote(ref.at[core], ref.at[core], join_s.at[which], join_r.at[which], (me, other))

    def norm_first():
        norm_pair[core] = norm_sum[...]
        return [norm_send(lambda: remote(norm_pair.at[core], norm_pair.at[core], norm_s.at[0], norm_r.at[0], (me, other)))]

    def norm_group(stage, digit, waited):
        for make in waited:
            make().wait_recv()
        if stage == 0:
            norm_sum[...] = norm_pair[0] + norm_pair[1]
        else:
            norm_sum[...] = (norm_slots[0, 0] + norm_slots[0, 1]) + (norm_slots[0, 2] + norm_slots[0, 3])
        norm_slots[stage, digit] = norm_sum[...]
        return [
            norm_send(
                lambda hop=hop, at=stage * (RADIX - 1) + hop: remote(
                    norm_slots.at[stage, digit], norm_slots.at[stage, digit], norm_s.at[at], norm_r.at[at],
                    (peers[stage](hop), core),
                )
            )
            for hop in range(1, RADIX)
        ]

    def norm_last(waited):
        for make in waited:
            make().wait_recv()
        norm_sum[...] = (norm_slots[1, 0] + norm_slots[1, 1]) + (norm_slots[1, 2] + norm_slots[1, 3])
        for turn, bit in enumerate(extra):
            norm_slots[2 + turn, 0] = norm_sum[...]
            make = norm_send(
                lambda bit=bit, turn=turn: remote(
                    norm_slots.at[2 + turn, 0], norm_slots.at[2 + turn, 1],
                    norm_s.at[2 * RADIX - 1 + turn], norm_r.at[2 * RADIX - 1 + turn], (mate(bit), core),
                )
            )
            make().wait_recv()
            norm_sum[...] = norm_slots[2 + turn, 0] + norm_slots[2 + turn, 1]
        norm_out[...] = norm_sum[...]

    def second_phase(left_in, right_in, left_base, right_base, left_made, right_made):
        def loads(slot):
            return [
                pltpu.make_async_copy(src.at[slot], dst.at[slot], load_s.at[side, slot])
                for side, (src, dst) in enumerate(((mlp_left, left_in), (mlp_right, right_in)))
            ]

        def stores(slot):
            return [
                pltpu.make_async_copy(src.at[slot], dst.at[slot], store_s.at[side, slot])
                for side, (src, dst) in enumerate(((left_made, mlp_left_new), (right_made, mlp_right_new)))
            ]

        slots = left_in.shape[0]
        for slot in range(slots):
            for copy in loads(slot):
                copy.start()
        for which in range(2):
            join(which).start()
        norm_wait = norm_first()
        reduce_two(1)
        spread_one(0)
        reduce_one(2)
        norm_wait = norm_group(0, lo, norm_wait)
        spread_one(1)
        spread_two(0)
        norm_wait = norm_group(1, hi, norm_wait)
        spread_two(1)

        for which in range(2):
            join(which).wait_recv()
        wide[...] = jnp.zeros_like(wide)
        for image in range(count // P_SIZE):
            which, at = image // images, image % images * ROWS
            span = slice(image * P_SIZE, (image + 1) * P_SIZE)
            wide[span, :] = both_out[which, at:at + ROWS, :].astype(F32)[:P_SIZE, :]
            input_grad_ref[span, :] = both_grad[which, at:at + P_SIZE, :]
        out_ref[...] = wide[:count, :].astype(BF)
        norm_last(norm_wait)
        reduce_two(2)

        misses = [([], []) for unused in range(slots)]

        def begin_slot(slot):
            for copy in loads(slot):
                copy.wait()
            arrived(slot)
            grad = side_by_side(whole[slot], left_in.shape[1])
            left = left_in[slot]
            right = right_in[slot]
            set_bases(
                grad, left, right, left.astype(BF), right.astype(BF), left_base.at[slot], right_base.at[slot]
            )
            return [
                renew_chain(right_base.at[slot], right_made.at[slot], misses[slot][1]),
                renew_chain(left_base.at[slot], left_made.at[slot], misses[slot][0]),
            ]

        def attn_chain():
            for unused in range(DELAY):
                yield
            spread_direct()

        chains = begin_slot(0)
        for unused in range(AHEAD):
            for chain in chains:
                next(chain)
        for slot in range(1, slots):
            chains = chains + begin_slot(slot)
        in_step(chains + [attn_chain()])
        for slot in range(slots):
            for side in range(2):
                miss_ref[slot, side] = functools.reduce(jnp.maximum, misses[slot][side])
            for copy in stores(slot):
                copy.start()

        def finish_direct(hop, carry):
            direct(hop).wait()
            return carry

        lax.fori_loop(1, RADIX**2, finish_direct, 0)
        for slot in range(slots):
            for copy in stores(slot):
                copy.wait()

    both_left = pltpu.VMEM(mlp_left.shape, F32)
    both_right = pltpu.VMEM(mlp_right.shape, F32)
    pl.run_scoped(
        second_phase, *([both_left, both_right] * 3)
    )
    for make in pending:
        make().wait_send()
    for which in range(2):
        join(which).wait_send()
        swap(which).wait_send()

    def finish(hop, carry):
        ask(hop).wait_send()
        give(hop).wait_send()
        return carry

    lax.fori_loop(1, chips, finish, 0)


def block(chips, nbr_index, nbr_valid, tokens, cotangent, queue, norms, attn, mlp, mlp_left, mlp_right):
    count, width = tokens.shape
    cores = width // attn.shape[1]
    images = nbr_valid.shape[0] // cores
    tall = images * ROWS
    padded = count + 16 - count % 8
    picks = images * NBR
    bits = chips.bit_length() - 1
    extra = max(0, bits - 4)
    height = attn.shape[0] * attn.shape[1]
    quarter, shard = height // RADIX, height // RADIX**2
    moving = (RADIX - 1) * (quarter + shard) + extra * shard
    vmem = pl.BlockSpec(memory_space=pltpu.VMEM)
    smem = pl.BlockSpec(memory_space=pltpu.SMEM)
    anywhere = pl.BlockSpec(memory_space=pl.ANY)
    dma = pltpu.SemaphoreType.DMA
    like = jax.ShapeDtypeStruct
    steps = 2 * (RADIX - 1)
    slots = mlp.shape[0]
    return pl.pallas_call(
        functools.partial(block_kernel, chips, images),
        in_specs=[smem] * 2 + [vmem] * 6 + [anywhere] * 2,
        out_specs=[vmem] * 5 + [smem] + [anywhere] * 2,
        out_shape=[
            like((count, width), BF),
            like((count, width), F32),
            like((2, height, width), BF),
            like((height, width), BF),
            like(norms.shape, F32),
            like((slots, 2), F32),
            like(mlp_left.shape, F32),
            like(mlp_right.shape, F32),
        ],
        scratch_shapes=[
            pltpu.VMEM((attn.shape[0], cores) + attn.shape[1:], BF),
            pltpu.VMEM((mlp.shape[0], cores) + mlp.shape[1:], BF),
            pltpu.VMEM((chips, 8, LANES), jnp.int32),
            pltpu.VMEM((chips, picks, width), BF),
            pltpu.VMEM((chips, picks, width), BF),
            pltpu.VMEM((padded, width), F32),
            pltpu.VMEM((cores, tall, width), BF),
            pltpu.VMEM((cores, tall, width), F32),
            pltpu.VMEM((PARTS, height, width), F32),
            pltpu.VMEM((PARTS, height, width), BF),
            pltpu.VMEM((PARTS, height, width), BF),
            pltpu.VMEM((PARTS, moving, width), BF),
            pltpu.VMEM((PARTS, moving, width), BF),
            pltpu.VMEM(norms.shape, F32),
            pltpu.VMEM((cores,) + norms.shape, F32),
            pltpu.VMEM((2 + extra, RADIX) + norms.shape, F32),
            dma((chips,)), dma((chips,)), dma((chips,)), dma((chips,)),
            dma((2,)), dma((2,)),
            dma((PARTS,)), dma((PARTS,)),
            dma((PARTS, steps + extra)), dma((PARTS, steps + extra)),
            dma((PARTS, steps)), dma((PARTS, steps)),
            dma((steps + 1 + extra,)), dma((steps + 1 + extra,)),
            dma((2,)), dma((2,)),
            dma((RADIX**2,)), dma((RADIX**2,)),
            dma((2, slots)), dma((2, slots)),
        ],
        compiler_params=pltpu.CompilerParams(
            collective_id=0, has_side_effects=True, vmem_limit_bytes=62 * 1024 * 1024
        ),
        name="block_both_ways",
    )(nbr_index, nbr_valid, tokens, cotangent, queue, norms, attn, mlp, mlp_left, mlp_right)


def body(
    chips,
    tokens,
    cotangent,
    queue,
    nbr_index,
    nbr_valid,
    norm_params,
    norm_first,
    norm_second,
    attn_weight,
    mlp_weight,
    attn_first,
    attn_second,
    mlp_first,
    mlp_second,
    attn_left,
    attn_right,
    mlp_left,
    mlp_right,
):
    def flip(value):
        return value.transpose(0, 2, 1)

    attn_own = flip(attn_weight)
    block_out, input_grad, summed, attn_summed, norm_grad, miss, left_made, right_made = block(
        chips,
        nbr_index,
        nbr_valid,
        tokens,
        cotangent,
        queue,
        norm_params,
        attn_own,
        mlp_weight,
        mlp_left,
        mlp_right,
    )
    (
        mlp_grad,
        mlp_new,
        mlp_copy,
        mlp_first_new,
        mlp_second_new,
        attn_grad,
        attn_new,
        attn_copy,
        attn_first_new,
        attn_second_new,
        attn_right_new,
        attn_left_new,
        norm_grad,
        norm_new,
        norm_first_new,
        norm_second_new,
        mlp_left_new,
        mlp_right_new,
        block_out,
        input_grad,
    ) = update(
        miss,
        (summed, mlp_weight, mlp_first, mlp_second, mlp_left, mlp_right),
        (
            attn_summed.reshape(attn_own.shape),
            attn_own,
            flip(attn_first),
            flip(attn_second),
            attn_right,
            attn_left,
        ),
        (norm_grad, norm_params, norm_first, norm_second),
        (left_made, right_made, block_out, input_grad),
    )
    return (
        block_out,
        input_grad,
        norm_grad,
        flip(attn_grad),
        mlp_grad,
        norm_first_new,
        norm_second_new,
        norm_new,
        flip(attn_first_new),
        flip(attn_second_new),
        mlp_first_new,
        mlp_second_new,
        attn_left_new,
        attn_right_new,
        mlp_left_new,
        mlp_right_new,
        flip(attn_new),
        flip(attn_copy),
        mlp_new,
        mlp_copy,
    )


def solution(mesh):
    return jax.shard_map(
        functools.partial(body, mesh.shape["dp"]),
        mesh=mesh,
        in_specs=(
            P("dp", None),
            P("dp", None),
            P("dp", None),
            P("dp", None),
            P("dp", None),
            P(),
            P(),
            P(),
            P(None, None, "mp"),
            P(None, None, "mp"),
            P(None, None, "mp"),
            P(None, None, "mp"),
            P(None, None, "mp"),
            P(None, None, "mp"),
            P(None, "mp", None),
            P(None, "mp", None),
            P(None, "mp", None),
            P(None, "mp", None),
        ),
        out_specs=(
            P("dp", None),
            P("dp", None),
            P(),
            P(None, None, "mp"),
            P(None, None, "mp"),
            P(),
            P(),
            P(),
            P(None, None, "mp"),
            P(None, None, "mp"),
            P(None, None, "mp"),
            P(None, None, "mp"),
            P(None, "mp", None),
            P(None, "mp", None),
            P(None, "mp", None),
            P(None, "mp", None),
            P(None, None, "mp"),
            P(None, None, "mp"),
            P(None, None, "mp"),
            P(None, None, "mp"),
        ),
        check_vma=False,
    )
```

```python
import functools
import math

import jax
import jax.numpy as jnp
from jax import lax
from jax.experimental import pallas as pl
from jax.experimental.pallas import tpu as pltpu
from jax.sharding import PartitionSpec as P

BETA_FIRST = 0.9
BETA_SECOND = 0.95
EPSILON = 1e-08
RATE_MATRIX = 0.15
DECAY_RATE = 0.05
TURN_RATE = 4.0
STEP = 10
BLOCK = 256
ROUNDS = 3
NEAR = 0.01
PIECE = 128
PAUSES = 40

BF = jnp.bfloat16
F32 = jnp.float32


def dot_nn(a, b):
    return lax.dot_general(a, b, (((1,), (0,)), ((), ())), preferred_element_type=F32)


def dot_nt(a, b):
    return lax.dot_general(a, b, (((1,), (1,)), ((), ())), preferred_element_type=F32)


def dot_tn(a, b):
    return lax.dot_general(a, b, (((0,), (0,)), ((), ())), preferred_element_type=F32)


def split(a):
    high = a.astype(BF)
    return high, (a - high.astype(F32)).astype(BF)


def three(dot, a, b):
    return dot(a[0], b[0]) + (dot(a[0], b[1]) + dot(a[1], b[0]))


def below(size):
    row = lax.broadcasted_iota(jnp.int32, (size, size), 0)
    col = lax.broadcasted_iota(jnp.int32, (size, size), 1)
    return row > col, row == col


def in_step(chains):
    chains = list(chains)
    while chains:
        kept = []
        for chain in chains:
            try:
                next(chain)
                kept.append(chain)
            except StopIteration:
                pass
        chains = kept


def renew_chain(base_ref, out_ref, misses):
    width = base_ref.shape[1]
    source = base_ref
    for at in range(0, width, BLOCK):
        size = min(BLOCK, width - at)
        lower, same = below(size)
        eye = jnp.where(same, 1.0, 0.0)
        low = source[:, at:at + size].astype(BF)
        gram = dot_tn(low, low)
        yield
        on_diag = jnp.where(same, gram, 0.0)
        s_col = lax.rsqrt(jnp.maximum(jnp.sum(on_diag, axis=1, keepdims=True), 1e-30))
        s_row = lax.rsqrt(jnp.maximum(jnp.sum(on_diag, axis=0, keepdims=True), 1e-30))
        state = gram * s_col * s_row
        made = jnp.where(same, s_col, 0.0).astype(BF)
        for turn in range(ROUNDS):
            under = jnp.where(lower, state, 0.0)
            moved = dot_nn(under.astype(BF), state.astype(BF))
            mass = jnp.sum(under * under, axis=1, keepdims=True)
            yield
            curve = jnp.sum(moved * under, axis=1, keepdims=True)
            pace = jnp.where(curve > mass, mass / jnp.maximum(curve, 1e-30), 1.0)
            left = 1.0 - 2.0 * pace * mass + pace * pace * curve
            scale = lax.rsqrt(jnp.maximum(left, 1e-6))
            step = (scale * (eye - pace * under)).astype(BF)
            if turn + 1 < ROUNDS:
                state = dot_nt((scale * (state - pace * moved)).astype(BF), step)
            made = dot_nn(step, made).astype(BF)
            yield
        high, low = split(source[:, at:at + size])
        block = dot_nt(high, made) + dot_nt(low, made)
        yield
        pair = split(block)
        gram = three(dot_tn, pair, pair)
        yield
        off = jnp.where(lower, gram, 0.0) + jnp.where(same, 0.5 * (gram - 1.0), 0.0)
        misses.append(jnp.sum(off * off) * (1.0 / size))
        block = block - dot_nt(pair[0], off.astype(BF))
        out_ref[:, at:at + size] = block
        yield
        if at + size < width:
            pair = split(block)
            rest = source[:, at + size:]
            shared = split(three(dot_tn, pair, split(rest)))
            yield
            out_ref[:, at + size:] = rest - three(dot_nn, pair, shared)
            source = out_ref
            yield


def renew_rows(base_ref, out_ref, work_ref):
    size = base_ref.shape[0]
    group = 64
    work_ref[...] = base_ref[...].T

    def take(turn, carry):
        row = work_ref[pl.ds(turn, 1), :]
        row = row * lax.rsqrt(jnp.sum(row * row, axis=1, keepdims=True))
        work_ref[pl.ds(turn, 1), :] = row

        def clear(which, inner):
            here = pl.ds(pl.multiple_of(which * group, group), group)
            rows = work_ref[here, :]
            later = lax.broadcasted_iota(jnp.int32, (group, 1), 0) + which * group > turn
            share = jnp.where(later, jnp.sum(rows * row, axis=1, keepdims=True), 0.0)
            work_ref[here, :] = rows - share * row
            return inner

        return lax.fori_loop(turn // group, size // group, clear, carry)

    lax.fori_loop(0, size, take, 0)
    out_ref[...] = work_ref[...].T


def move_chain(grad, left_pair, right_pair, weight_ref, first_ref, second_ref, new_ref, copy_ref, first_new_ref, second_new_ref, move_ref):
    rows = grad.shape[0]
    for at in range(0, rows, PIECE):
        size = min(PIECE, rows - at)
        part = slice(at, at + size)
        half = dot_tn(left_pair[0][:, part], grad) + dot_tn(left_pair[1][:, part], grad)
        yield
        turned = three(dot_nn, split(half), right_pair)
        yield
        first_new = BETA_FIRST * first_ref[part, :] + (1.0 - BETA_FIRST) * turned
        second_new = BETA_SECOND * second_ref[part, :] + (1.0 - BETA_SECOND) * turned * turned
        first_new_ref[part, :] = first_new
        second_new_ref[part, :] = second_new
        move_ref[part, :] = (
            first_new
            / (1.0 - BETA_FIRST**STEP)
            / (jnp.sqrt(second_new / (1.0 - BETA_SECOND**STEP)) + EPSILON)
        ).astype(BF)
        yield
    for at in range(0, rows, PIECE):
        part = slice(at, min(at + PIECE, rows))
        back = dot_nn(left_pair[0][part, :], move_ref[...]).astype(BF)
        yield
        new = weight_ref[part, :] * (1.0 - RATE_MATRIX * DECAY_RATE) - RATE_MATRIX * dot_nt(back, right_pair[0])
        new_ref[part, :] = new
        copy_ref[part, :] = new.astype(BF)
        yield


RATE_NORM = 0.6


MESH = pl.DeviceIdType.MESH
RADIX = 4


def remote(src, dst, send, recv, device):
    return pltpu.make_async_remote_copy(
        src_ref=src, dst_ref=dst, send_sem=send, recv_sem=recv, device_id=device, device_id_type=MESH
    )


def set_bases(grad, left, right, left_low, right_low, left_base, right_base):
    gram = dot_nt(grad, grad)
    pace = TURN_RATE / (jnp.sqrt(jnp.sum(gram * gram)) + 1e-06)
    left_base[...] = left + dot_nn(gram.astype(BF), left_low) * pace
    right_base[...] = right + dot_tn(grad, dot_nn(grad, right_low).astype(BF)) * pace


def side_by_side(grad, height):
    return jnp.concatenate([grad[at:at + height] for at in range(0, grad.shape[0], height)], axis=1)


def update_kernel(
    together,
    miss_ref, mlp_grad_ref, mlp_weight_ref, mlp_first_ref, mlp_second_ref, mlp_left_ref, mlp_right_ref,
    grad_ref, weight_ref, first_ref, second_ref, left_ref, right_ref,
    norm_grad_ref, norm_ref, norm_first_ref, norm_second_ref,
    mlp_left_made, mlp_right_made, block_ref, input_grad_ref,
    mlp_grad_out, mlp_new_ref, mlp_copy_ref, mlp_first_new_ref, mlp_second_new_ref,
    grad_out_ref, new_ref, copy_ref, first_new_ref, second_new_ref, left_new_ref, right_new_ref,
    norm_grad_out, norm_new, norm_first_new, norm_second_new,
    mlp_left_out, mlp_right_out, block_out, input_grad_out,
    mlp_move, left_base, right_base, move_ref, left_held, right_held, work, work_small,
    block_held, input_grad_held, sems_in, sems_out,
):
    slot = pl.program_id(0)
    last = pl.num_programs(0) - 1

    def copies(passed, at):
        return (
            [pltpu.make_async_copy(src, held, sems_in.at[at + place]) for place, (src, held, dst) in enumerate(passed)],
            [pltpu.make_async_copy(held, dst, sems_out.at[at + place]) for place, (src, held, dst) in enumerate(passed)],
        )

    bases = copies(
        ((mlp_left_made.at[slot], left_held, mlp_left_out.at[slot]), (mlp_right_made.at[slot], right_held, mlp_right_out.at[slot])), 0
    )
    wide = copies(((block_ref, block_held, block_out), (input_grad_ref, input_grad_held, input_grad_out)), 2)

    @pl.when(slot == 0)
    def _():
        for copy in wide[0]:
            copy.start()
        grad = norm_grad_ref[...]
        first = BETA_FIRST * norm_first_ref[...] + (1.0 - BETA_FIRST) * grad
        second = BETA_SECOND * norm_second_ref[...] + (1.0 - BETA_SECOND) * grad * grad
        norm_grad_out[...] = grad
        norm_first_new[...] = first
        norm_second_new[...] = second
        norm_new[...] = norm_ref[...] - RATE_NORM * (first / (1.0 - BETA_FIRST**STEP)) / (
            jnp.sqrt(second / (1.0 - BETA_SECOND**STEP)) + EPSILON
        )

    for copy in bases[0]:
        copy.start()
    mlp_grad = side_by_side(mlp_grad_ref[0], mlp_weight_ref.shape[1])
    mlp_grad_out[0] = mlp_grad.astype(F32)
    chains = []
    misses = []
    for which in range(together):
        grad = grad_ref[which]
        grad_out_ref[which] = grad.astype(F32)
        left = left_ref[which]
        right = right_ref[which]
        left_pair = split(left)
        right_pair = split(right)
        set_bases(grad, left, right, left_pair[0], right_pair[0], left_base.at[which], right_base.at[which])
        misses.append(([], []))
        chains.append(renew_chain(right_base.at[which], right_new_ref.at[which], misses[which][1]))
        chains.append(renew_chain(left_base.at[which], left_new_ref.at[which], misses[which][0]))
        chains.append(
            move_chain(
                grad, left_pair, right_pair, weight_ref.at[which], first_ref.at[which], second_ref.at[which],
                new_ref.at[which], copy_ref.at[which], first_new_ref.at[which], second_new_ref.at[which],
                move_ref.at[which],
            )
        )
    chains.append(
        move_chain(
            mlp_grad, split(mlp_left_ref[0]), split(mlp_right_ref[0]),
            mlp_weight_ref.at[0], mlp_first_ref.at[0], mlp_second_ref.at[0],
            mlp_new_ref.at[0], mlp_copy_ref.at[0], mlp_first_new_ref.at[0], mlp_second_new_ref.at[0], mlp_move,
        )
    )
    in_step(chains)
    for copy in bases[0]:
        copy.wait()
    poor = jnp.logical_not(jnp.maximum(miss_ref[slot, 0], miss_ref[slot, 1]) < NEAR)

    @pl.when(poor)
    def _():
        left = mlp_left_ref[0]
        right = mlp_right_ref[0]
        size = left.shape[0]
        set_bases(mlp_grad, left, right, left.astype(BF), right.astype(BF), left_held, right_held)
        renew_rows(left_held, left_held, work.at[pl.ds(0, size), pl.ds(0, size)])
        renew_rows(right_held, right_held, work)

    for copy in bases[1]:
        copy.start()
    for which in range(together):
        for missed, base, out in zip(misses[which], (left_base, right_base), (left_new_ref, right_new_ref)):
            worst = functools.reduce(jnp.maximum, missed)

            @pl.when(jnp.logical_not(worst < NEAR))
            def _(base=base, out=out):
                size = base.shape[1]
                space = work_small if size == work_small.shape[0] else work.at[pl.ds(0, size), pl.ds(0, size)]
                renew_rows(base.at[which], out.at[which], space)

    @pl.when(slot == 0)
    def _():
        for copy in wide[0]:
            copy.wait()
        for copy in wide[1]:
            copy.start()

    @pl.when(slot == last)
    def _():
        for copy in wide[1]:
            copy.wait()

    for copy in bases[1]:
        copy.wait()


def update(miss, mlp, attn, norms, passed):
    like = jax.ShapeDtypeStruct
    slots = mlp[1].shape[0]
    together = attn[1].shape[0] // slots

    def spec(count, value):
        return pl.BlockSpec((count,) + value.shape[1:], lambda slot: (slot, 0, 0))

    def made(value):
        return [like(value.shape, F32)] * 2 + [like(value.shape, BF)] + [like(value.shape, F32)] * 2

    whole = pl.BlockSpec(norms[0].shape, lambda slot: (0, 0))
    anywhere = pl.BlockSpec(memory_space=pl.ANY)
    rows, width = attn[1].shape[1:]
    sides = [pltpu.VMEM((together, rows, rows), F32), pltpu.VMEM((together, width, width), F32)]
    held = [pltpu.VMEM(value.shape[1:], F32) for value in passed[:2]]
    return pl.pallas_call(
        functools.partial(update_kernel, together),
        grid=(slots,),
        in_specs=[pl.BlockSpec(memory_space=pltpu.SMEM)]
        + [spec(1, value) for value in mlp]
        + [spec(together, value) for value in attn]
        + [whole] * 4
        + [anywhere] * 4,
        out_specs=[spec(1, mlp[1])] * 5
        + [spec(together, attn[1])] * 5
        + [spec(together, attn[4]), spec(together, attn[5])]
        + [whole] * 4
        + [anywhere] * 4,
        out_shape=made(mlp[1])
        + made(attn[1])
        + [like(attn[4].shape, F32), like(attn[5].shape, F32)]
        + [like(norms[0].shape, F32)] * 4
        + [like(value.shape, value.dtype) for value in passed],
        scratch_shapes=[pltpu.VMEM(mlp[1].shape[1:], BF)]
        + sides
        + [pltpu.VMEM((together, rows, width), BF)]
        + held
        + [held[1], pltpu.VMEM((rows, rows), F32)]
        + [pltpu.VMEM(value.shape, value.dtype) for value in passed[2:]]
        + [pltpu.SemaphoreType.DMA((len(passed),)), pltpu.SemaphoreType.DMA((len(passed),))],
        compiler_params=pltpu.CompilerParams(vmem_limit_bytes=62 * 1024 * 1024),
        name="update",
    )(miss, *mlp, *attn, *norms, *passed)


P_SIZE = 197
NBR = 8
HEAD = 64
ROWS = 208
FAR = 200
CHUNK = 256
LANES = 128
DELAY = 4
AHEAD = 12
PARTS = 3


def layer_norm(values, gain, shift):
    centre = values - jnp.mean(values, axis=-1, keepdims=True)
    scale = lax.rsqrt(jnp.mean(centre * centre, axis=-1, keepdims=True) + 1e-06)
    normal = centre * scale
    return (normal * gain + shift, normal, scale)


def norm_back(grad, normal, scale, gain):
    shaped = grad * gain
    return scale * (
        shaped
        - jnp.mean(shaped, axis=-1, keepdims=True)
        - normal * jnp.mean(shaped * normal, axis=-1, keepdims=True)
    )


def gelu_pair(value):
    size = jnp.abs(value) * (1.0 / math.sqrt(2.0))
    bell = jnp.exp(-0.5 * value * value)
    part = 1.0 / (1.0 + 0.3275911 * size)
    series = part * (
        0.254829592
        + part * (-0.284496736 + part * (1.421413741 + part * (-1.453152027 + part * 1.061405429)))
    )
    tail = 0.5 * series * bell
    share = jnp.where(value < 0.0, tail, 1.0 - tail)
    return value * share, share + value * bell * (1.0 / math.sqrt(2.0 * math.pi))


def block_kernel(
    chips, images,
    index_ref, valid_ref,
    tokens_any, cotangent_any, queue_ref, norms_ref, attn_any, mlp_any, mlp_left, mlp_right,
    out_any, input_grad_any, whole_any, attn_grad, norm_out, miss_ref, mlp_left_new, mlp_right_new,
    tokens_ref, cotangent_ref, attn_own, mlp_own, out_ref, input_grad_ref, whole,
    attn_ref, mlp_ref, asked, parts_out, given, wide, both_out, both_grad,
    total, first_send, first_recv, sent, recv, norm_sum, norm_pair, norm_slots,
    ask_send, ask_recv, give_send, give_recv, swap_send, swap_recv,
    first_s, first_r, step_s, step_r, spread_s, spread_r, norm_s, norm_r, join_s, join_r, direct_s, direct_r, load_s, store_s, fill_s, drain_s,
):
    me = lax.axis_index("dp")
    core = lax.axis_index("mp")
    other = 1 - core
    count = tokens_ref.shape[0]
    width = tokens_ref.shape[1]
    depth = queue_ref.shape[0]
    picks = images * NBR
    group = LANES // picks
    pairs = width // (2 * HEAD)
    bits = chips.bit_length() - 1
    height = whole.shape[1]

    barrier = pltpu.get_barrier_semaphore()
    pl.semaphore_signal(barrier, inc=1, device_id=(me, other), device_id_type=MESH)

    def greet(hop, carry):
        pl.semaphore_signal(
            barrier, inc=1, device_id=(lax.rem(me + hop, chips), core), device_id_type=MESH
        )
        return carry

    lax.fori_loop(1, chips, greet, 0)
    fills = [
        pltpu.make_async_copy(src, dst, fill_s.at[turn])
        for turn, (src, dst) in enumerate(
            ((attn_any, attn_own), (mlp_any, mlp_own), (tokens_any, tokens_ref), (cotangent_any, cotangent_ref))
        )
    ]
    for copy in fills:
        copy.start()
    pick_lane = lax.broadcasted_iota(jnp.int32, (8, LANES), 1)
    wanted = jnp.full((8, LANES), -1, jnp.int32)
    for pick in range(picks):
        wanted = jnp.where(
            pick_lane % picks == pick, index_ref[core * images + pick // NBR, pick % NBR], wanted
        )
    asked[0] = wanted
    fills[0].wait()
    attn_ref[:, core] = attn_own[...].astype(BF)
    fills[1].wait()
    mlp_ref[:, core] = mlp_own[...].astype(BF)
    for copy in fills[2:]:
        copy.wait()
    pl.semaphore_wait(barrier, chips)

    def ask(hop):
        return remote(
            asked.at[0], asked.at[hop], ask_send.at[hop], ask_recv.at[hop],
            (lax.rem(me + hop, chips), core),
        )

    def give(hop):
        return remote(
            parts_out.at[hop], given.at[hop], give_send.at[hop], give_recv.at[hop],
            (lax.rem(me + chips - hop, chips), core),
        )

    def start_ask(hop, carry):
        ask(hop).start()
        return carry

    lax.fori_loop(1, chips, start_ask, 0)
    def swap(which):
        ref = (attn_ref, mlp_ref)[which]
        return remote(ref.at[:, core], ref.at[:, core], swap_send.at[which], swap_recv.at[which], (me, other))

    for which in range(2):
        swap(which).start()

    seat = me % RADIX**2
    lo = me % RADIX
    hi = me // RADIX % RADIX
    peers = (lambda hop: me - lo + (lo + hop) % RADIX, lambda hop: me - RADIX * hi + RADIX * ((hi + hop) % RADIX))
    digits = (lo, hi)
    plan = ((0, 1), (1, 0), (0, 1))
    quarter, shard = height // RADIX, height // RADIX**2
    extra = list(range(4, bits))

    def mate(bit):
        return me + (1 - 2 * (me // 2**bit % 2)) * 2**bit

    pending = []
    waits = [[] for unused in range(PARTS)]

    def send(part, make):
        make().start()
        pending.append(make)
        waits[part].append(make)

    def arrived(part):
        for make in waits[part]:
            make().wait_recv()
        waits[part].clear()

    def rows(start, size):
        return pl.ds(pl.multiple_of(start, 16), size)

    def copy_blocks(target, source, part):
        tall = source.shape[1]
        for block in range(source.shape[2] // width):
            target[part, block * tall:(block + 1) * tall, :] = source[
                part, :, block * width:(block + 1) * width
            ]

    def begin(part):
        send(
            part,
            lambda: remote(
                first_send.at[part], first_recv.at[part], first_s.at[part], first_r.at[part], (me, other)
            ),
        )

    def reduce_one(part):
        arrived(part)
        axis = plan[part][0]
        for hop in range(1, RADIX):
            away = rows((digits[axis] + hop) % RADIX * quarter, quarter)
            slot = pl.ds((hop - 1) * quarter, quarter)
            sent[part, slot, :] = (total[part, away, :] + first_recv[part, away, :].astype(F32)).astype(BF)
            send(
                part,
                lambda hop=hop, slot=slot: remote(
                    sent.at[part, slot], recv.at[part, slot],
                    step_s.at[part, hop - 1], step_r.at[part, hop - 1], (peers[axis](hop), core),
                ),
            )
        held = rows(digits[axis] * quarter, quarter)
        total[part, held, :] += first_recv[part, held, :].astype(F32)

    def reduce_two(part):
        arrived(part)
        first, second = plan[part]
        start = digits[first] * quarter

        def summed(at, size):
            sums = total[part, rows(start + at, size), :]
            for hop in range(1, RADIX):
                sums = sums + recv[part, rows((hop - 1) * quarter + at, size), :].astype(F32)
            return sums

        base = (RADIX - 1) * quarter
        for hop in range(1, RADIX):
            slot = pl.ds(base + (hop - 1) * shard, shard)
            sent[part, slot, :] = summed((digits[second] + hop) % RADIX * shard, shard).astype(BF)
            send(
                part,
                lambda hop=hop, slot=slot: remote(
                    sent.at[part, slot], recv.at[part, slot],
                    step_s.at[part, RADIX - 2 + hop], step_r.at[part, RADIX - 2 + hop], (peers[second](hop), core),
                ),
            )
        at = digits[second] * shard
        total[part, rows(start + at, shard), :] = summed(at, shard)

    def place(part):
        first, second = plan[part]
        return rows(digits[first] * quarter + digits[second] * shard, shard)

    def last_sum(part):
        arrived(part)
        sums = total[part, place(part), :]
        base = (RADIX - 1) * quarter
        for hop in range(1, RADIX):
            sums = sums + recv[part, pl.ds(base + (hop - 1) * shard, shard), :].astype(F32)
        base = base + (RADIX - 1) * shard
        for turn, bit in enumerate(extra):
            slot = pl.ds(base + turn * shard, shard)
            sent[part, slot, :] = sums.astype(BF)
            at = 2 * (RADIX - 1) + turn
            send(
                part,
                lambda bit=bit, slot=slot, at=at: remote(
                    sent.at[part, slot], recv.at[part, slot], step_s.at[part, at], step_r.at[part, at],
                    (mate(bit), core),
                ),
            )
            arrived(part)
            sums = sent[part, slot, :].astype(F32) + recv[part, slot, :].astype(F32)
        return sums.astype(BF)

    def spread_one(part):
        whole[part, place(part), :] = last_sum(part)
        for hop in range(1, RADIX):
            send(
                part,
                lambda hop=hop: remote(
                    whole.at[part, place(part)], whole.at[part, place(part)],
                    spread_s.at[part, hop - 1], spread_r.at[part, hop - 1], (peers[plan[part][1]](hop), core),
                ),
            )

    def direct(hop):
        return remote(
            attn_grad.at[place(2)], attn_grad.at[place(2)], direct_s.at[hop], direct_r.at[hop],
            (me - seat + (seat + hop) % RADIX**2, core),
        )

    def spread_direct():
        attn_grad[place(2), :] = last_sum(2)

        def start(hop, carry):
            direct(hop).start()
            return carry

        lax.fori_loop(1, RADIX**2, start, 0)

    def spread_two(part):
        arrived(part)
        axis = plan[part][0]
        for hop in range(1, RADIX):

            def make(hop=hop):
                held = rows(digits[axis] * quarter, quarter)
                return remote(
                    whole.at[part, held], whole.at[part, held],
                    spread_s.at[part, RADIX - 2 + hop], spread_r.at[part, RADIX - 2 + hop],
                    (peers[axis](hop), core),
                )

            send(part, make)

    def first_phase(
        far_f, far_key, far_value, tokens_f, normed, normal_one, scale_one, query, key, value, probs, mixed,
        middle, normal_two, scale_two, normed_two, cot_low, made, mlp_mine, mlp_away, square,
    ):
        grad_two = tokens_f
        grad_query, grad_key, grad_value, grad_mid_low = query, key, value, normed_two

        def spread(source, target):
            for which in range(count // (images * P_SIZE)):

                @pl.when(core == which)
                def _(which=which):
                    for image in range(images):
                        start = (which * images + image) * P_SIZE
                        target[image * ROWS:(image + 1) * ROWS, :] = source[start:start + ROWS, :]

        places = lax.broadcasted_iota(jnp.int32, (depth, LANES), 0) + me * depth
        lane_group = lax.broadcasted_iota(jnp.int32, (1, LANES), 1) // picks

        def answer(turn, carry):
            wish = jnp.zeros((1, LANES), jnp.int32)
            for step in range(group):
                hop = turn * group + step

                @pl.when(hop > 0)
                def _(hop=hop):
                    ask(hop).wait_recv()

                wish = jnp.where(lane_group == step, asked[hop][:1, :], wish)
            chooser = jnp.where(wish == places, 1.0, 0.0).astype(BF)
            picked = dot_tn(chooser, queue_ref[...]).astype(BF)
            parts_out[pl.ds(turn * group, group)] = picked.reshape(group, picks, width)
            for step in range(group):
                hop = turn * group + step

                @pl.when(hop > 0)
                def _(hop=hop):
                    give(hop).start()

            return carry

        wide[:count, :] = tokens_ref[...].astype(F32)
        wide[count:, :] = jnp.zeros((wide.shape[0] - count, width), F32)
        spread(wide, tokens_f)
        lax.fori_loop(0, chips // group, answer, 0)
        wide[:count, :] = cotangent_ref[...].astype(F32)
        spread(wide, made)
        own_row = lax.broadcasted_iota(jnp.int32, (ROWS, 1), 0) < P_SIZE
        lane = lax.broadcasted_iota(jnp.int32, (1, 2 * HEAD), 1)
        first_head = lane < HEAD
        key_lane = lax.broadcasted_iota(jnp.int32, (1, ROWS), 1)

        def halves(pair):
            zero = jnp.zeros_like(pair)
            return jnp.where(first_head, pair, zero), jnp.where(first_head, zero, pair)

        def place_of(image):
            return pl.ds(pl.multiple_of(image * ROWS, ROWS), ROWS)

        def weight(slot):
            return attn_ref[slot].reshape(width, width)

        def step_norm(image, carry):
            here = place_of(image)
            cot_low[here, :] = jnp.where(own_row, made[here, :], 0.0).astype(BF)
            normed_f, normal, scale = layer_norm(tokens_f[here, :], norms_ref[0:1, :], norms_ref[1:2, :])
            normal_one[here, :] = normal
            scale_one[here, :] = scale
            made[here, :] = jnp.where(own_row, normed_f, 0.0)
            return carry

        lax.fori_loop(0, images, step_norm, 0)
        swap(0).wait_recv()

        def step_own(image, carry):
            here = place_of(image)
            low = made[here, :].astype(BF)
            query[here, :] = dot_nt(low, weight(0)).astype(BF)
            middle[here, :] = dot_nt(low, weight(1))
            normal_two[here, :] = dot_nt(low, weight(2))
            return carry

        lax.fori_loop(0, images, step_own, 0)

        def collect(hop, sums):
            give(hop).wait_recv()
            return sums + given[hop].astype(F32)

        far_f[...] = lax.fori_loop(1, chips, collect, parts_out[0].astype(F32))
        far_low = far_f[...].astype(BF)
        far_key[...] = dot_nt(far_low, weight(1))
        far_value[...] = dot_nt(far_low, weight(2))

        def step_forward(image, carry):
            here = place_of(image)
            x = tokens_f[here, :]
            near = pl.ds(pl.multiple_of(image * NBR, NBR), NBR)

            def with_far(own, far):
                return jnp.concatenate([own[here, :][:FAR, :], far[near, :]], axis=0).astype(BF)

            normed[here, :] = with_far(made, far_f)
            q = query[here, :]
            k = with_far(middle, far_key)
            v = with_far(normal_two, far_value)
            key[here, :] = k
            value[here, :] = v
            bias = jnp.where(key_lane < P_SIZE, 0.0, -1e30)
            for slot in range(NBR):
                okay = valid_ref[core * images + image, slot] > 0
                bias = jnp.where(key_lane == FAR + slot, jnp.where(okay, 0.0, -1e30), bias)
            parts = []
            for pair in range(pairs):
                cols = slice(pair * 2 * HEAD, (pair + 1) * 2 * HEAD)
                k_pair = k[:, cols]
                sums = 0.0
                for head, (q_one, v_one) in enumerate(zip(halves(q[:, cols]), halves(v[:, cols]))):
                    scores = dot_nt(q_one, k_pair) * 0.125 + bias
                    top = jnp.max(scores, axis=-1, keepdims=True)
                    powers = jnp.exp(scores - top)
                    prob = powers / jnp.sum(powers, axis=-1, keepdims=True)
                    probs[image * 2 * pairs + 2 * pair + head] = prob
                    sums = sums + dot_nn(prob.astype(BF), v_one)
                parts.append(sums.astype(BF))
            mix = jnp.concatenate(parts, axis=1)
            mixed[here, :] = mix
            mid = x + dot_nn(mix, weight(3))
            middle[here, :] = mid
            two_f, normal, scale = layer_norm(mid, norms_ref[2:3, :], norms_ref[3:4, :])
            normal_two[here, :] = normal
            scale_two[here, :] = scale
            normed_two[here, :] = two_f.astype(BF)
            return carry

        lax.fori_loop(0, images, step_forward, 0)

        made[...] = jnp.zeros_like(made)
        grad_two[...] = jnp.zeros_like(grad_two)
        chunks = mlp_ref.shape[3] // CHUNK

        def step_mlp(half, target):
            def step(turn, carry):
                cols = pl.ds(pl.multiple_of(turn * CHUNK, CHUNK), CHUNK)
                w_one = mlp_ref[0, half, :, cols]
                w_two = mlp_ref[1, half, :, cols]
                two = normed_two[...]
                cot = cot_low[...]
                hidden, slope = gelu_pair(dot_nn(two, w_one))
                hidden = hidden.astype(BF)
                grad_inner = (dot_nn(cot, w_two) * slope).astype(BF)
                made[...] += dot_nt(hidden, w_two)
                grad_two[...] += dot_nt(grad_inner, w_one)
                target[0, :, cols] = dot_tn(two, grad_inner).astype(target.dtype)
                target[1, :, cols] = dot_tn(cot, hidden).astype(target.dtype)
                return carry

            lax.fori_loop(0, chunks, step, 0)

        swap(1).wait_recv()
        step_mlp(other, mlp_away)
        for part in range(2):
            copy_blocks(first_send, mlp_away, part)
            begin(part)
        step_mlp(core, mlp_mine)
        for part in range(2):
            copy_blocks(total, mlp_mine, part)
            reduce_one(part)

        norm_sum[...] = jnp.zeros_like(norm_sum)

        def step_backward(image, carry):
            here = place_of(image)
            made[here, :] += middle[here, :]
            both_out[core, here, :] = made[here, :].astype(BF)
            grad_n = grad_two[here, :]
            normal = normal_two[here, :]
            norm_sum[2:3, :] += jnp.sum(grad_n * normal, axis=0, keepdims=True)
            norm_sum[3:4, :] += jnp.sum(grad_n, axis=0, keepdims=True)
            grad_mid = cot_low[here, :].astype(F32) + norm_back(
                grad_n, normal, scale_two[here, :], norms_ref[2:3, :]
            )
            low = grad_mid.astype(BF)
            grad_mid_low[here, :] = low
            grad_mix = dot_nt(low, weight(3)).astype(BF)
            q = query[here, :]
            k = key[here, :]
            v = value[here, :]
            parts_q, parts_k, parts_v = [], [], []
            for pair in range(pairs):
                cols = slice(pair * 2 * HEAD, (pair + 1) * 2 * HEAD)
                gm_pair = grad_mix[:, cols]
                sum_q = sum_k = sum_v = 0.0
                for head, (q_one, k_one, v_one, gm_one) in enumerate(
                    zip(halves(q[:, cols]), halves(k[:, cols]), halves(v[:, cols]), halves(gm_pair))
                ):
                    prob = probs[image * 2 * pairs + 2 * pair + head]
                    grad_prob = dot_nt(gm_pair, v_one)
                    sum_v = sum_v + dot_tn(prob.astype(BF), gm_one)
                    weighed = prob * grad_prob
                    grad_score = (
                        weighed - prob * jnp.sum(weighed, axis=-1, keepdims=True)
                    ).astype(BF)
                    sum_q = sum_q + dot_nn(grad_score, k_one)
                    sum_k = sum_k + dot_tn(grad_score, q_one)
                parts_q.append((sum_q * 0.125).astype(BF))
                parts_k.append((sum_k * 0.125).astype(BF))
                parts_v.append(sum_v.astype(BF))
            gq = jnp.concatenate(parts_q, axis=1)
            gk = jnp.concatenate(parts_k, axis=1)
            gv = jnp.concatenate(parts_v, axis=1)
            grad_query[here, :] = gq
            grad_key[here, :] = gk
            grad_value[here, :] = gv
            grad_n = dot_nn(gq, weight(0)) + dot_nn(gk, weight(1)) + dot_nn(gv, weight(2))
            grad_n = jnp.where(own_row, grad_n, 0.0)
            normal = normal_one[here, :]
            norm_sum[0:1, :] += jnp.sum(grad_n * normal, axis=0, keepdims=True)
            norm_sum[1:2, :] += jnp.sum(grad_n, axis=0, keepdims=True)
            both_grad[core, here, :] = grad_mid + norm_back(
                grad_n, normal, scale_one[here, :], norms_ref[0:1, :]
            )
            return carry

        lax.fori_loop(0, images, step_backward, 0)
        reduce_two(0)
        tall = attn_own.shape[1]
        for slot, (left, right) in enumerate(
            ((grad_query, normed), (grad_key, normed), (grad_value, normed), (mixed, grad_mid_low))
        ):
            square[...] = dot_tn(left[...], right[...])
            span = pl.ds(slot * tall, tall)
            first_send[2, span, :] = square[rows(other * tall, tall), :].astype(BF)
            total[2, span, :] = square[rows(core * tall, tall), :]
        begin(2)


    tall_rows = images * ROWS
    flat_f = pltpu.VMEM((tall_rows, width), F32)
    flat_low = pltpu.VMEM((tall_rows, width), BF)
    column = pltpu.VMEM((tall_rows, 1), F32)
    near = pltpu.VMEM((picks, width), F32)
    pl.run_scoped(
        first_phase,
        near, near, near, flat_f, flat_low, flat_f, column, flat_low, flat_low, flat_low,
        pltpu.VMEM((images * width // HEAD, ROWS, ROWS), F32),
        flat_low, flat_f, flat_f, column, flat_low, flat_low, flat_f,
        pltpu.VMEM(mlp_own.shape, F32),
        pltpu.VMEM(mlp_own.shape, BF),
        pltpu.VMEM((width, width), F32),
    )

    def norm_send(make):
        make().start()
        pending.append(make)
        return make

    def join(which):
        ref = (both_out, both_grad)[which]
        return remote(ref.at[core], ref.at[core], join_s.at[which], join_r.at[which], (me, other))

    def norm_first():
        norm_pair[core] = norm_sum[...]
        return [norm_send(lambda: remote(norm_pair.at[core], norm_pair.at[core], norm_s.at[0], norm_r.at[0], (me, other)))]

    def norm_group(stage, digit, waited):
        for make in waited:
            make().wait_recv()
        if stage == 0:
            norm_sum[...] = norm_pair[0] + norm_pair[1]
        else:
            norm_sum[...] = (norm_slots[0, 0] + norm_slots[0, 1]) + (norm_slots[0, 2] + norm_slots[0, 3])
        norm_slots[stage, digit] = norm_sum[...]
        return [
            norm_send(
                lambda hop=hop, at=stage * (RADIX - 1) + hop: remote(
                    norm_slots.at[stage, digit], norm_slots.at[stage, digit], norm_s.at[at], norm_r.at[at],
                    (peers[stage](hop), core),
                )
            )
            for hop in range(1, RADIX)
        ]

    def norm_last(waited):
        for make in waited:
            make().wait_recv()
        norm_sum[...] = (norm_slots[1, 0] + norm_slots[1, 1]) + (norm_slots[1, 2] + norm_slots[1, 3])
        for turn, bit in enumerate(extra):
            norm_slots[2 + turn, 0] = norm_sum[...]
            make = norm_send(
                lambda bit=bit, turn=turn: remote(
                    norm_slots.at[2 + turn, 0], norm_slots.at[2 + turn, 1],
                    norm_s.at[2 * RADIX - 1 + turn], norm_r.at[2 * RADIX - 1 + turn], (mate(bit), core),
                )
            )
            make().wait_recv()
            norm_sum[...] = norm_slots[2 + turn, 0] + norm_slots[2 + turn, 1]
        norm_out[...] = norm_sum[...]

    def second_phase(left_in, right_in, left_base, right_base, left_made, right_made):
        def loads(slot):
            return [
                pltpu.make_async_copy(src.at[slot], dst.at[slot], load_s.at[side, slot])
                for side, (src, dst) in enumerate(((mlp_left, left_in), (mlp_right, right_in)))
            ]

        def stores(slot):
            return [
                pltpu.make_async_copy(src.at[slot], dst.at[slot], store_s.at[side, slot])
                for side, (src, dst) in enumerate(((left_made, mlp_left_new), (right_made, mlp_right_new)))
            ]

        slots = left_in.shape[0]
        for slot in range(slots):
            for copy in loads(slot):
                copy.start()
        for which in range(2):
            join(which).start()
        norm_wait = norm_first()
        reduce_two(1)
        spread_one(0)
        reduce_one(2)
        norm_wait = norm_group(0, lo, norm_wait)
        spread_one(1)
        spread_two(0)
        norm_wait = norm_group(1, hi, norm_wait)
        spread_two(1)

        for which in range(2):
            join(which).wait_recv()
        wide[...] = jnp.zeros_like(wide)
        for image in range(count // P_SIZE):
            which, at = image // images, image % images * ROWS
            span = slice(image * P_SIZE, (image + 1) * P_SIZE)
            wide[span, :] = both_out[which, at:at + ROWS, :].astype(F32)[:P_SIZE, :]
            input_grad_ref[span, :] = both_grad[which, at:at + P_SIZE, :]
        out_ref[...] = wide[:count, :].astype(BF)
        drains = [
            pltpu.make_async_copy(src, dst, drain_s.at[turn])
            for turn, (src, dst) in enumerate(((out_ref, out_any), (input_grad_ref, input_grad_any)))
        ]
        for copy in drains:
            copy.start()
        norm_last(norm_wait)
        reduce_two(2)

        misses = [([], []) for unused in range(slots)]

        def begin_slot(slot):
            for copy in loads(slot):
                copy.wait()
            arrived(slot)
            drains.append(pltpu.make_async_copy(whole.at[slot], whole_any.at[slot], drain_s.at[2 + slot]))
            drains[-1].start()
            grad = side_by_side(whole[slot], left_in.shape[1])
            left = left_in[slot]
            right = right_in[slot]
            set_bases(
                grad, left, right, left.astype(BF), right.astype(BF), left_base.at[slot], right_base.at[slot]
            )
            return [
                renew_chain(right_base.at[slot], right_made.at[slot], misses[slot][1]),
                renew_chain(left_base.at[slot], left_made.at[slot], misses[slot][0]),
            ]

        def attn_chain():
            for unused in range(DELAY):
                yield
            spread_direct()

        chains = begin_slot(0)
        for unused in range(AHEAD):
            for chain in chains:
                next(chain)
        for slot in range(1, slots):
            chains = chains + begin_slot(slot)
        in_step(chains + [attn_chain()])
        for slot in range(slots):
            for side in range(2):
                miss_ref[slot, side] = functools.reduce(jnp.maximum, misses[slot][side])
            for copy in stores(slot):
                copy.start()

        def finish_direct(hop, carry):
            direct(hop).wait()
            return carry

        lax.fori_loop(1, RADIX**2, finish_direct, 0)
        for slot in range(slots):
            for copy in stores(slot):
                copy.wait()
        for copy in drains:
            copy.wait()

    both_left = pltpu.VMEM(mlp_left.shape, F32)
    both_right = pltpu.VMEM(mlp_right.shape, F32)
    pl.run_scoped(
        second_phase, *([both_left, both_right] * 3)
    )
    for make in pending:
        make().wait_send()
    for which in range(2):
        join(which).wait_send()
        swap(which).wait_send()

    def finish(hop, carry):
        ask(hop).wait_send()
        give(hop).wait_send()
        return carry

    lax.fori_loop(1, chips, finish, 0)


def block(chips, nbr_index, nbr_valid, tokens, cotangent, queue, norms, attn, mlp, mlp_left, mlp_right):
    count, width = tokens.shape
    cores = width // attn.shape[1]
    images = nbr_valid.shape[0] // cores
    tall = images * ROWS
    padded = count + 16 - count % 8
    picks = images * NBR
    bits = chips.bit_length() - 1
    extra = max(0, bits - 4)
    height = attn.shape[0] * attn.shape[1]
    quarter, shard = height // RADIX, height // RADIX**2
    moving = (RADIX - 1) * (quarter + shard) + extra * shard
    vmem = pl.BlockSpec(memory_space=pltpu.VMEM)
    smem = pl.BlockSpec(memory_space=pltpu.SMEM)
    anywhere = pl.BlockSpec(memory_space=pl.ANY)
    dma = pltpu.SemaphoreType.DMA
    like = jax.ShapeDtypeStruct
    steps = 2 * (RADIX - 1)
    slots = mlp.shape[0]
    return pl.pallas_call(
        functools.partial(block_kernel, chips, images),
        in_specs=[smem] * 2 + [anywhere] * 2 + [vmem] * 2 + [anywhere] * 4,
        out_specs=[anywhere] * 3 + [vmem] * 2 + [smem] + [anywhere] * 2,
        out_shape=[
            like((count, width), BF),
            like((count, width), F32),
            like((2, height, width), BF),
            like((height, width), BF),
            like(norms.shape, F32),
            like((slots, 2), F32),
            like(mlp_left.shape, F32),
            like(mlp_right.shape, F32),
        ],
        scratch_shapes=[
            pltpu.VMEM(tokens.shape, BF),
            pltpu.VMEM(cotangent.shape, BF),
            pltpu.VMEM(attn.shape, F32),
            pltpu.VMEM(mlp.shape, F32),
            pltpu.VMEM((count, width), BF),
            pltpu.VMEM((count, width), F32),
            pltpu.VMEM((2, height, width), BF),
            pltpu.VMEM((attn.shape[0], cores) + attn.shape[1:], BF),
            pltpu.VMEM((mlp.shape[0], cores) + mlp.shape[1:], BF),
            pltpu.VMEM((chips, 8, LANES), jnp.int32),
            pltpu.VMEM((chips, picks, width), BF),
            pltpu.VMEM((chips, picks, width), BF),
            pltpu.VMEM((padded, width), F32),
            pltpu.VMEM((cores, tall, width), BF),
            pltpu.VMEM((cores, tall, width), F32),
            pltpu.VMEM((PARTS, height, width), F32),
            pltpu.VMEM((PARTS, height, width), BF),
            pltpu.VMEM((PARTS, height, width), BF),
            pltpu.VMEM((PARTS, moving, width), BF),
            pltpu.VMEM((PARTS, moving, width), BF),
            pltpu.VMEM(norms.shape, F32),
            pltpu.VMEM((cores,) + norms.shape, F32),
            pltpu.VMEM((2 + extra, RADIX) + norms.shape, F32),
            dma((chips,)), dma((chips,)), dma((chips,)), dma((chips,)),
            dma((2,)), dma((2,)),
            dma((PARTS,)), dma((PARTS,)),
            dma((PARTS, steps + extra)), dma((PARTS, steps + extra)),
            dma((PARTS, steps)), dma((PARTS, steps)),
            dma((steps + 1 + extra,)), dma((steps + 1 + extra,)),
            dma((2,)), dma((2,)),
            dma((RADIX**2,)), dma((RADIX**2,)),
            dma((2, slots)), dma((2, slots)),
            dma((4,)), dma((2 + slots,)),
        ],
        compiler_params=pltpu.CompilerParams(
            collective_id=0, has_side_effects=True, vmem_limit_bytes=62 * 1024 * 1024
        ),
        name="block_both_ways",
    )(nbr_index, nbr_valid, tokens, cotangent, queue, norms, attn, mlp, mlp_left, mlp_right)


def body(
    chips,
    tokens,
    cotangent,
    queue,
    nbr_index,
    nbr_valid,
    norm_params,
    norm_first,
    norm_second,
    attn_weight,
    mlp_weight,
    attn_first,
    attn_second,
    mlp_first,
    mlp_second,
    attn_left,
    attn_right,
    mlp_left,
    mlp_right,
):
    def flip(value):
        return value.transpose(0, 2, 1)

    attn_own = flip(attn_weight)
    block_out, input_grad, summed, attn_summed, norm_grad, miss, left_made, right_made = block(
        chips,
        nbr_index,
        nbr_valid,
        tokens,
        cotangent,
        queue,
        norm_params,
        attn_own,
        mlp_weight,
        mlp_left,
        mlp_right,
    )
    (
        mlp_grad,
        mlp_new,
        mlp_copy,
        mlp_first_new,
        mlp_second_new,
        attn_grad,
        attn_new,
        attn_copy,
        attn_first_new,
        attn_second_new,
        attn_right_new,
        attn_left_new,
        norm_grad,
        norm_new,
        norm_first_new,
        norm_second_new,
        mlp_left_new,
        mlp_right_new,
        block_out,
        input_grad,
    ) = update(
        miss,
        (summed, mlp_weight, mlp_first, mlp_second, mlp_left, mlp_right),
        (
            attn_summed.reshape(attn_own.shape),
            attn_own,
            flip(attn_first),
            flip(attn_second),
            attn_right,
            attn_left,
        ),
        (norm_grad, norm_params, norm_first, norm_second),
        (left_made, right_made, block_out, input_grad),
    )
    return (
        block_out,
        input_grad,
        norm_grad,
        flip(attn_grad),
        mlp_grad,
        norm_first_new,
        norm_second_new,
        norm_new,
        flip(attn_first_new),
        flip(attn_second_new),
        mlp_first_new,
        mlp_second_new,
        attn_left_new,
        attn_right_new,
        mlp_left_new,
        mlp_right_new,
        flip(attn_new),
        flip(attn_copy),
        mlp_new,
        mlp_copy,
    )


def solution(mesh):
    return jax.shard_map(
        functools.partial(body, mesh.shape["dp"]),
        mesh=mesh,
        in_specs=(
            P("dp", None),
            P("dp", None),
            P("dp", None),
            P("dp", None),
            P("dp", None),
            P(),
            P(),
            P(),
            P(None, None, "mp"),
            P(None, None, "mp"),
            P(None, None, "mp"),
            P(None, None, "mp"),
            P(None, None, "mp"),
            P(None, None, "mp"),
            P(None, "mp", None),
            P(None, "mp", None),
            P(None, "mp", None),
            P(None, "mp", None),
        ),
        out_specs=(
            P("dp", None),
            P("dp", None),
            P(),
            P(None, None, "mp"),
            P(None, None, "mp"),
            P(),
            P(),
            P(),
            P(None, None, "mp"),
            P(None, None, "mp"),
            P(None, None, "mp"),
            P(None, None, "mp"),
            P(None, "mp", None),
            P(None, "mp", None),
            P(None, "mp", None),
            P(None, "mp", None),
            P(None, None, "mp"),
            P(None, None, "mp"),
            P(None, None, "mp"),
            P(None, None, "mp"),
        ),
        check_vma=False,
    )
```
